32 devices in a mesh: sample: 4 (over x, core), chan: 8 (over z, y).
Axes of the slice: x: 2, y: 2, z: 4, core: 2. Of those that a mesh axis runs over, the one named last changes fastest.
Arguments:
- act_64: bfloat16 [4, 64, 8, 8, 256], P('sample'), may hold values from -6 to 6
- cot_32: bfloat16 [4, 32, 4, 4, 512], P('sample', None, None, None, 'chan'), may hold values from -2.5 to 2.5
- filters_32: bfloat16 [3, 3, 3, 256, 512], P(None, None, None, None, 'chan'), may hold values from -0.078125 to 0.078125
- act_128: bfloat16 [4, 128, 16, 16, 128], P('sample', 'chan'), may hold values from -6 to 6
Outputs:
- grad_filters_32: float32 [3, 3, 3, 256, 512], P(None, None, None, None, 'chan')
- grad_filters_64: float32 [3, 3, 3, 128, 256], P(None, None, None, 'chan')
- cot_64: float32 [4, 64, 8, 8, 256], P('sample', 'chan')
The draws below stay inside these ranges and needn't reach their ends.
All inputs are finite; a program needn't handle non-finite values.
Results may differ from the reference program's by a relative error of at most 0.0029.
Values may be sent and summed in bfloat16 or wider, within the bound.
No kernel may reach another device: no remote copies, remote signals or barrier semaphores. Data moves between devices by JAX's collectives and lax.ppermute only.
A program may use at most 64 MiB of HBM per device.

```python
import jax
import jax.numpy as jnp
from jax import lax

C1IN = 128
C2IN = 256
C2OUT = 512
DEPTH = 32
SIDE = 4
SAMPLES = 4
N_CHAN = 8


def raised(drawn, rng, source, target, shards_of, factor):
    def block_of(position):
        return (jnp.arange(drawn.shape[position]) // (drawn.shape[position] // shards_of)).reshape((-1,) + (1,) * (drawn.ndim - 1 - position))

    one_side = jax.random.permutation(rng, shards_of)[block_of(target)]
    far = (block_of(target) + shards_of // 2) % shards_of
    return jnp.where((block_of(source) == one_side) | (block_of(source) == far), factor * drawn, drawn)


def block_scale(rng, shape, cuts, smallest, high):
    def one(dim, blocks):
        heights = jax.random.uniform(jax.random.fold_in(jax.random.fold_in(rng, 6), dim), (blocks,), jnp.float32, smallest / len(cuts), high / len(cuts))
        return jnp.repeat(jnp.exp(heights), shape[dim] // blocks).reshape((-1,) + (1,) * (len(shape) - dim - 1))

    level = one(*cuts[0])
    for cut in cuts[1:]:
        level = level * one(*cut)
    return level


def normal_values(key, dims, width, limit, split=(), held_as=jnp.bfloat16):
    drawn = jax.random.normal(key, dims, jnp.float32) * width
    if len(split) > 0:
        drawn = block_scale(key, dims, split, -0.22, 0.18) * drawn
    return jnp.clip(drawn, min=-limit, max=limit).astype(held_as)


def heavy_noise(rng, dims, deviation, limit, cuts, heavy, held_as=jnp.bfloat16):
    result = deviation * jax.random.normal(rng, dims, jnp.float32)
    if cuts:
        result = result * block_scale(rng, dims, cuts, -0.22, 0.18)
    return jnp.clip(raised(result, jax.random.fold_in(rng, 3), *heavy), -limit, limit).astype(held_as)


def setup_inputs(seed: int = 0) -> dict:
    splits = jax.random.split(jax.random.key(seed), 5)
    return {
        "act_64": normal_values(splits[0], (SAMPLES, 2 * DEPTH, 2 * SIDE, 2 * SIDE, C2IN), 1.0, 6.0, ((0, 4),)),
        "cot_32": heavy_noise(splits[1], (SAMPLES, DEPTH, SIDE, SIDE, C2OUT), 0.2, 2.5, ((0, 4), (4, 8)), (4, 1, 8, 2.0)),
        "filters_32": normal_values(splits[2], (3, 3, 3, C2IN, C2OUT), (27 * C2IN) ** -0.5, 0.078125, ((4, 8),)),
        "act_128": normal_values(splits[3], (SAMPLES, 4 * DEPTH, 4 * SIDE, 4 * SIDE, C1IN), 1.0, 6.0, ((0, 4), (1, 8))),
    }


leak_slope = 0.3

def strided_conv(volume, filters):
    return lax.conv_general_dilated(volume[None], filters, (2, 2, 2), ((1, 1), (1, 1), (1, 1)), dimension_numbers=('NDHWC', 'DHWIO', 'NDHWC'), precision=lax.Precision.HIGHEST)[0]

def valid_conv(volume, filters):
    return lax.conv_general_dilated(volume[None], filters, (2, 2, 2), ((0, 0), (0, 0), (0, 0)), dimension_numbers=('NDHWC', 'DHWIO', 'NDHWC'), precision=lax.Precision.HIGHEST)[0]

def reference(act_64, cot_32, filters_32, act_128):
    filters_full = filters_32.astype(jnp.float32)
    slab_planes = 2 * DEPTH // N_CHAN
    lower_in = act_128.shape[4]
    lower_out = act_64.shape[4]

    def one_volume(carry, inputs):
        volume_64, cot_single, volume_128 = inputs
        volume_upper = volume_64.astype(jnp.float32)
        unused_out, pull_back = jax.vjp(strided_conv, volume_upper, filters_full)
        grad_volume, grad_filters = pull_back(cot_single.astype(jnp.float32))
        cot_lower = (grad_volume * jnp.where(volume_upper > 0, 1.0, leak_slope)).astype(jnp.float32)
        cot_float = cot_lower.astype(jnp.bfloat16).astype(jnp.float32)
        padded_lower = jnp.pad(volume_128.astype(jnp.float32), ((1, 1), (1, 1), (1, 1), (0, 0)))

        def one_slab(total, block):
            window = lax.dynamic_slice_in_dim(padded_lower, block * (2 * slab_planes), 2 * slab_planes + 1, 0)
            cot_slab = lax.dynamic_slice_in_dim(cot_float, block * slab_planes, slab_planes, 0)
            zero_filters = jnp.zeros((3, 3, 3, lower_in, lower_out), jnp.float32)
            unused_slab, pull_slab = jax.vjp(lambda weights: valid_conv(window, weights), zero_filters)
            term = pull_slab(cot_slab)[0]
            return (total + term, None)
        blocks = jnp.arange(N_CHAN, dtype=jnp.int32)
        grad_lower, unused_blocks = lax.scan(one_slab, jnp.zeros((3, 3, 3, lower_in, lower_out), jnp.float32), blocks)
        return ((carry[0] + grad_filters, carry[1] + grad_lower), cot_lower)
    start_carry = (jnp.zeros(filters_32.shape, jnp.float32), jnp.zeros((3, 3, 3, lower_in, lower_out), jnp.float32))
    totals, cot_all = lax.scan(one_volume, start_carry, (act_64, cot_32, act_128))
    return (totals[0] / SAMPLES, totals[1] / SAMPLES, cot_all)
```

```python
import jax
import jax.numpy as jnp
from jax import lax
from jax.sharding import PartitionSpec as P

leak_slope = 0.3
low = jnp.bfloat16


def partner(array, axis, by):
    size = lax.axis_size(axis)
    return lax.ppermute(array, axis, [(i, i ^ by) for i in range(size)])


def exchange(blocks, axis):
    return lax.all_to_all(blocks, axis, split_axis=0, concat_axis=0, tiled=True)


def filter_gradient(volume, cotangent, padding):
    return lax.conv_general_dilated(
        volume[None],
        cotangent[None],
        (1, 1, 1),
        padding,
        rhs_dilation=(2, 2, 2),
        dimension_numbers=("CDHWN", "IDHWO", "DHWNC"),
        preferred_element_type=jnp.float32,
    )


def input_gradient(cotangent, filters):
    return lax.conv_general_dilated(
        cotangent[None],
        filters[::-1, ::-1, ::-1],
        (1, 1, 1),
        ((1, 2), (1, 2), (1, 2)),
        lhs_dilation=(2, 2, 2),
        dimension_numbers=("NDHWC", "DHWOI", "NDHWC"),
        preferred_element_type=jnp.float32,
    )[0]


def body(act_64, cot_32, filters_32, act_128):
    shards = lax.axis_size("chan")
    samples = lax.axis_size("sample")
    position = lax.axis_index("chan")
    core = lax.axis_index("sample") % 2
    volume_64 = act_64[0]
    cot_local = cot_32[0]
    depth, height, width, shard_out = cot_local.shape
    planes, rows, columns, middle = volume_64.shape
    below = act_128.shape[4]
    slab = planes // shards
    part = middle // shards

    rim = lax.ppermute(act_128[:, -1:], "chan", [(i, i + 1) for i in range(shards - 1)])

    taps = filters_32.reshape(27, shards, part, shard_out).transpose(1, 0, 3, 2)
    lanes = 128 if taps.size // shards % 256 == 0 else 64
    taps = taps.reshape(shards, 2, -1, lanes)
    own_half = lax.dynamic_index_in_dim(taps, core, 1, keepdims=False)
    cot_rows = jnp.broadcast_to(cot_local.reshape(1, -1, lanes), (shards, cot_local.size // lanes, lanes))
    sent = jnp.concatenate([own_half, cot_rows], axis=1)
    got = exchange(sent, "chan")
    cut = own_half.shape[1]
    got_half = got[:, :cut]
    other_half = partner(got_half, "sample", 1)
    first = jnp.where(core == 0, got_half, other_half)
    second = jnp.where(core == 0, other_half, got_half)
    part_filters = jnp.concatenate([first, second], axis=1)
    part_filters = part_filters.reshape(shards, 3, 3, 3, shard_out, part)
    part_filters = part_filters.transpose(1, 2, 3, 5, 0, 4).reshape(3, 3, 3, part, -1)
    cot_all = got[:, cut:].reshape(shards, depth, height, width, shard_out)
    cot_all = cot_all.transpose(1, 2, 3, 0, 4).reshape(depth, height, width, -1)

    grad_upper = filter_gradient(volume_64, cot_local, ((1, 0),) * 3)
    total_upper = lax.psum(grad_upper, "sample")

    grad_part = input_gradient(cot_all, part_filters)
    own_part = lax.dynamic_slice_in_dim(volume_64, position * part, part, 3)
    cot_part = (grad_part * jnp.where(own_part > 0, 1.0, leak_slope)).astype(low)
    cot_got = exchange(cot_part.reshape(shards, -1, 128), "chan")
    cot_low = cot_got.reshape(shards, slab, rows, columns, part)
    cot_low = cot_low.transpose(1, 2, 3, 0, 4).reshape(slab, rows, columns, middle)

    window = jnp.concatenate([rim, act_128], axis=1)[0]
    grad_lower = filter_gradient(window, cot_low, ((0, 0), (1, 0), (1, 0)))
    blocks = grad_lower.reshape(27, shards, 2, -1, middle).transpose(2, 1, 0, 3, 4)
    mine = lax.dynamic_index_in_dim(blocks, core, 0, keepdims=False)
    theirs = lax.dynamic_index_in_dim(blocks, 1 - core, 0, keepdims=False)
    mine = mine + partner(theirs.astype(low), "sample", 1).astype(jnp.float32)
    got_terms = exchange(mine.astype(low), "chan")
    share = jnp.sum(got_terms.astype(jnp.float32), axis=0)
    if samples > 2:
        pairs = [[2 * i + k for i in range(samples // 2)] for k in range(2)]
        share = lax.psum(share, "sample", axis_index_groups=pairs)
    share = lax.all_gather(
        share, "sample", axis=1, tiled=True, axis_index_groups=[[i, i + 1] for i in range(0, samples, 2)]
    )
    total_lower = share.reshape(3, 3, 3, below // shards, middle)
    return (
        total_upper / samples,
        total_lower / samples,
        cot_low.astype(jnp.float32)[None],
    )


def solution(mesh):
    placed = (
        P("sample", None, None, None, None),
        P("sample", None, None, None, "chan"),
        P(None, None, None, None, "chan"),
        P("sample", "chan", None, None, None),
    )
    return jax.shard_map(
        body,
        mesh=mesh,
        in_specs=placed,
        out_specs=(
            P(None, None, None, None, "chan"),
            P(None, None, None, "chan", None),
            P("sample", "chan", None, None, None),
        ),
        check_vma=False,
    )
```

```python
import functools

import jax
import jax.numpy as jnp
from jax import lax
from jax.experimental import pallas as pl
from jax.experimental.pallas import tpu as pltpu
from jax.sharding import PartitionSpec as P

leak_slope = 0.3
low = jnp.bfloat16
wide = jnp.float32
params = pltpu.CompilerParams(vmem_limit_bytes=40 * 2**20)
whole = pl.BlockSpec(memory_space=pltpu.VMEM)
scalar = pl.BlockSpec(memory_space=pltpu.SMEM)


def slot_plan():
    groups = []
    for col in range(3):
        groups.append([(1, 1, col), (1, 2, col), (2, 1, col), (2, 2, col)])
    for col in range(3):
        groups.append([(2, 0, col), (1, 0, col), (0, 1, col), (0, 2, col)])
    groups.append([None, (0, 0, 2), (0, 0, 1), (0, 0, 0)])
    return groups


def tap_index(tap):
    return (tap[0] * 3 + tap[1]) * 3 + tap[2]


def lane_slot(shape):
    return lax.broadcasted_iota(jnp.int32, shape, len(shape) - 1) // 32


def pack_kernel(core_ref, filters_ref, cot_ref, sent_ref):
    half = filters_ref.shape[1] // 2
    groups = slot_plan()
    rows = len(groups) * half
    start = pl.multiple_of(core_ref[0] * half, half)
    slots = lane_slot((half, 128))
    shards = sent_ref.shape[0]
    for g, group in enumerate(groups):
        for tile in range(shards // 4):
            turned = []
            for tap in group:
                if tap is None:
                    turned.append([jnp.zeros((half, 128), wide)] * 4)
                    continue
                block = filters_ref[tap_index(tap), pl.ds(start, half), pl.ds(tile * 128, 128)].astype(wide)
                turned.append([block] + [pltpu.roll(block, 32 * r, 1) for r in range(1, 4)])
            for m in range(4):
                joined = turned[0][(0 - m) % 4]
                for k in range(1, 4):
                    joined = jnp.where(slots == k, turned[k][(k - m) % 4], joined)
                sent_ref[tile * 4 + m, pl.ds(g * half, half), :] = joined.astype(low)
    turned_cot = cot_ref[...].astype(wide).T.astype(low)
    outs, cells = turned_cot.shape
    for d in range(shards):
        for b in range(cells // 128):
            sent_ref[d, pl.ds(rows + b * outs, outs), :] = turned_cot[:, b * 128 : (b + 1) * 128]


def pack(core, filters, cot, shards):
    outs = filters.shape[1]
    rows = len(slot_plan()) * (outs // 2) + cot.shape[0] // 128 * outs
    return pl.pallas_call(
        pack_kernel,
        out_shape=jax.ShapeDtypeStruct((shards, rows, 128), low),
        in_specs=[scalar, whole, whole],
        out_specs=whole,
        compiler_params=params,
        cost_estimate=pl.CostEstimate(flops=10**6, bytes_accessed=3 * 10**6, transcendentals=0),
    )(core, filters, cot)


def sign_kernel(position_ref, volume_ref, own_ref):
    part = position_ref[0] % 4
    rows = own_ref.shape[0]
    slots = lane_slot((rows, 128))
    joined = None
    for depth_par in range(2):
        for row_par in range(2):
            slot = depth_par * 2 + row_par
            block = volume_ref[:, depth_par, :, row_par].astype(wide).reshape(rows, 128)
            block = pltpu.roll(block, (slot - part + 4) % 4 * 32, 1)
            joined = block if joined is None else jnp.where(slots == slot, block, joined)
    own_ref[...] = joined.astype(low)


def own_signs(position, volume):
    planes, rows, columns, channels = volume.shape
    split = volume.reshape(planes // 2, 2, rows // 2, 2, columns, channels)
    count = planes * rows * columns // 4
    return pl.pallas_call(
        sign_kernel,
        out_shape=jax.ShapeDtypeStruct((count, 128), low),
        grid_spec=pltpu.PrefetchScalarGridSpec(
            num_scalar_prefetch=1,
            grid=(1,),
            in_specs=[
                pl.BlockSpec(
                    (planes // 2, 2, rows // 2, 2, columns, 128),
                    lambda i, at: (0, 0, 0, 0, 0, at[0] // 4),
                )
            ],
            out_specs=pl.BlockSpec((count, 128), lambda i, at: (0, 0)),
        ),
        compiler_params=params,
        cost_estimate=pl.CostEstimate(flops=10**6, bytes_accessed=4 * 10**6, transcendentals=0),
    )(position, split)


def spread_kernel(grid, core_ref, got_ref, other_ref, own_ref, sent_ref, weight, turned, products, joined):
    depth, height, width = grid
    cells = depth * height * width
    shards = got_ref.shape[0]
    groups = len(slot_plan())
    half = other_ref.shape[1] // groups
    outs = 2 * half
    core = core_ref[0]
    for c in range(shards):
        first = pl.multiple_of(c * outs + core * half, half)
        second = pl.multiple_of(c * outs + (1 - core) * half, half)
        for g in range(groups):
            weight[pl.ds(first, half), pl.ds(g * 128, 128)] = got_ref[c, pl.ds(g * half, half), :]
            weight[pl.ds(second, half), pl.ds(g * 128, 128)] = other_ref[c, pl.ds(g * half, half), :]
        for b in range(cells // 128):
            turned[pl.ds(c * outs, outs), pl.ds(b * 128, 128)] = got_ref[
                c, pl.ds(groups * half + b * outs, outs), :
            ]
    products[pl.ds(0, cells), :] = lax.dot_general(
        turned[...], weight[...], (((0,), (0,)), ((), ())), preferred_element_type=wide
    )
    products[pl.ds(cells, products.shape[0] - cells), :] = jnp.zeros(
        (products.shape[0] - cells, products.shape[1]), wide
    )
    chunk = cells // shards
    place = lax.broadcasted_iota(jnp.int32, (chunk, 128), 0)
    slots = lane_slot((chunk, 128))
    last_col = place % width == width - 1
    last_row = place // width % height == height - 1
    row_step, plane_step = width, width * height
    for n in range(shards):
        sums = [None, None]
        for col in range(3):
            shift = 1 if col == 0 else 0
            base = n * chunk + shift

            def piece(group, offset):
                return products[pl.ds(base + offset, chunk), pl.ds(group * 128, 128)]

            part = piece(col, 0)
            part = part + jnp.where(slots >= 2, piece(3 + col, plane_step), 0.0)
            by_row = piece(3 + col, row_step)
            moved = pltpu.roll(by_row, 96, 1)
            corner = piece(6, plane_step + row_step)
            if col > 0:
                corner = pltpu.roll(corner, 32 * col, 1)
            rows = jnp.where(slots == 1, by_row, jnp.where(slots == 3, moved + corner, 0.0))
            part = part + jnp.where(last_row, 0.0, rows)
            if shift:
                part = jnp.where(last_col, 0.0, part)
            to = 0 if col == 1 else 1
            sums[to] = part if sums[to] is None else sums[to] + part
        joined[pl.ds(0, chunk, stride=2), :] = sums[0]
        joined[pl.ds(1, chunk, stride=2), :] = sums[1]
        span = pl.ds(n * 2 * chunk, 2 * chunk)
        slope = jnp.where(own_ref[span, :].astype(wide) > 0, 1.0, leak_slope)
        sent_ref[n] = (joined[...] * slope).astype(low)


def spread(core, got, other, own, grid):
    cells = grid[0] * grid[1] * grid[2]
    shards = got.shape[0]
    groups = len(slot_plan())
    outs = 2 * other.shape[1] // groups
    return pl.pallas_call(
        functools.partial(spread_kernel, grid),
        out_shape=jax.ShapeDtypeStruct((shards, 2 * cells // shards, 128), low),
        in_specs=[scalar, whole, whole, whole],
        out_specs=whole,
        scratch_shapes=[
            pltpu.VMEM((shards * outs, groups * 128), low),
            pltpu.VMEM((shards * outs, cells), low),
            pltpu.VMEM((cells + 32, groups * 128), wide),
            pltpu.VMEM((2 * cells // shards, 128), wide),
        ],
        compiler_params=params,
        cost_estimate=pl.CostEstimate(flops=5 * 10**8, bytes_accessed=3 * 10**6, transcendentals=0),
    )(core, got, other, own)


def unpack_kernel(got_ref, wide_ref, low_ref):
    shards, rows, _ = got_ref.shape
    planes, height, columns, _ = wide_ref.shape
    slots = lane_slot((rows, 128))
    for tile in range(shards // 4):
        turned = []
        for m in range(4):
            block = got_ref[tile * 4 + m].astype(wide)
            turned.append([block] + [pltpu.roll(block, 32 * r, 1) for r in range(1, 4)])
        for slot in range(4):
            joined = turned[0][(0 - slot) % 4]
            for m in range(1, 4):
                joined = jnp.where(slots == m, turned[m][(m - slot) % 4], joined)
            joined = joined.reshape(planes // 2, height // 2, columns, 128)
            lanes = pl.ds(tile * 128, 128)
            for z in range(planes // 2):
                for y in range(height // 2):
                    at = (2 * z + slot // 2, 2 * y + slot % 2)
                    wide_ref[at[0], at[1], :, lanes] = joined[z, y]
    low_ref[...] = wide_ref[...].astype(low)


def unpack(got, grid):
    shape = (*grid, got.shape[0] * 32)
    return pl.pallas_call(
        unpack_kernel,
        out_shape=(jax.ShapeDtypeStruct(shape, wide), jax.ShapeDtypeStruct(shape, low)),
        in_specs=[whole],
        out_specs=(whole, whole),
        compiler_params=params,
        cost_estimate=pl.CostEstimate(flops=10**6, bytes_accessed=2 * 10**6, transcendentals=0),
    )(got)


def partner(array, axis, by):
    size = lax.axis_size(axis)
    return lax.ppermute(array, axis, [(i, i ^ by) for i in range(size)])


def exchange(blocks, axis):
    return lax.all_to_all(blocks, axis, split_axis=0, concat_axis=0, tiled=True)


def filter_gradient(volume, cotangent, padding):
    return lax.conv_general_dilated(
        volume[None],
        cotangent[None],
        (1, 1, 1),
        padding,
        rhs_dilation=(2, 2, 2),
        dimension_numbers=("CDHWN", "IDHWO", "DHWNC"),
        preferred_element_type=jnp.float32,
    )


def input_gradient(cotangent, filters):
    return lax.conv_general_dilated(
        cotangent[None],
        filters[::-1, ::-1, ::-1],
        (1, 1, 1),
        ((1, 2), (1, 2), (1, 2)),
        lhs_dilation=(2, 2, 2),
        dimension_numbers=("NDHWC", "DHWOI", "NDHWC"),
        preferred_element_type=jnp.float32,
    )[0]


def plain_body(act_64, cot_32, filters_32, act_128):
    shards = lax.axis_size("chan")
    samples = lax.axis_size("sample")
    position = lax.axis_index("chan")
    core = lax.axis_index("sample") % 2
    volume_64 = act_64[0]
    cot_local = cot_32[0]
    depth, height, width, shard_out = cot_local.shape
    planes, rows, columns, middle = volume_64.shape
    below = act_128.shape[4]
    slab = planes // shards
    part = middle // shards

    rim = lax.ppermute(act_128[:, -1:], "chan", [(i, i + 1) for i in range(shards - 1)])

    taps = filters_32.reshape(27, shards, part, shard_out).transpose(1, 0, 3, 2)
    lanes = 128 if taps.size // shards % 256 == 0 else 64
    taps = taps.reshape(shards, 2, -1, lanes)
    own_half = lax.dynamic_index_in_dim(taps, core, 1, keepdims=False)
    cot_rows = jnp.broadcast_to(cot_local.reshape(1, -1, lanes), (shards, cot_local.size // lanes, lanes))
    sent = jnp.concatenate([own_half, cot_rows], axis=1)
    got = exchange(sent, "chan")
    cut = own_half.shape[1]
    got_half = got[:, :cut]
    other_half = partner(got_half, "sample", 1)
    first = jnp.where(core == 0, got_half, other_half)
    second = jnp.where(core == 0, other_half, got_half)
    part_filters = jnp.concatenate([first, second], axis=1)
    part_filters = part_filters.reshape(shards, 3, 3, 3, shard_out, part)
    part_filters = part_filters.transpose(1, 2, 3, 5, 0, 4).reshape(3, 3, 3, part, -1)
    cot_all = got[:, cut:].reshape(shards, depth, height, width, shard_out)
    cot_all = cot_all.transpose(1, 2, 3, 0, 4).reshape(depth, height, width, -1)

    grad_upper = filter_gradient(volume_64, cot_local, ((1, 0),) * 3)
    total_upper = lax.psum(grad_upper, "sample")

    grad_part = input_gradient(cot_all, part_filters)
    own_part = lax.dynamic_slice_in_dim(volume_64, position * part, part, 3)
    cot_part = (grad_part * jnp.where(own_part > 0, 1.0, leak_slope)).astype(low)
    cot_got = exchange(cot_part.reshape(shards, -1, 128), "chan")
    cot_low = cot_got.reshape(shards, slab, rows, columns, part)
    cot_low = cot_low.transpose(1, 2, 3, 0, 4).reshape(slab, rows, columns, middle)

    window = jnp.concatenate([rim, act_128], axis=1)[0]
    grad_lower = filter_gradient(window, cot_low, ((0, 0), (1, 0), (1, 0)))
    blocks = grad_lower.reshape(27, shards, 2, -1, middle).transpose(2, 1, 0, 3, 4)
    mine = lax.dynamic_index_in_dim(blocks, core, 0, keepdims=False)
    theirs = lax.dynamic_index_in_dim(blocks, 1 - core, 0, keepdims=False)
    mine = mine + partner(theirs.astype(low), "sample", 1).astype(jnp.float32)
    got_terms = exchange(mine.astype(low), "chan")
    share = jnp.sum(got_terms.astype(jnp.float32), axis=0)
    if samples > 2:
        pairs = [[2 * i + k for i in range(samples // 2)] for k in range(2)]
        share = lax.psum(share, "sample", axis_index_groups=pairs)
    share = lax.all_gather(
        share, "sample", axis=1, tiled=True, axis_index_groups=[[i, i + 1] for i in range(0, samples, 2)]
    )
    total_lower = share.reshape(3, 3, 3, below // shards, middle)
    return (
        total_upper / samples,
        total_lower / samples,
        cot_low.astype(jnp.float32)[None],
    )


def chip_sum(terms, samples):
    core = lax.axis_index("sample") % 2
    blocks = terms.reshape(27, 2, -1, terms.shape[2])
    mine = lax.dynamic_index_in_dim(blocks, core, 1, keepdims=False)
    theirs = lax.dynamic_index_in_dim(blocks, 1 - core, 1, keepdims=False)
    mine = (mine + partner(theirs.astype(low), "sample", 1).astype(wide)).astype(low)
    total = mine.astype(wide)
    for by in range(2, samples, 2):
        pairs = [(i, (i + by) % samples) for i in range(samples)]
        total = total + lax.ppermute(mine, "sample", pairs).astype(wide)
    total = total * (1.0 / samples)
    other = partner(total, "sample", 1)
    first = jnp.where(core == 0, total, other)
    second = jnp.where(core == 0, other, total)
    return jnp.concatenate([first, second], axis=1)


def body(act_64, cot_32, filters_32, act_128):
    shards = lax.axis_size("chan")
    samples = lax.axis_size("sample")
    middle = act_64.shape[4]
    grid = cot_32.shape[1:4]
    shard_out = cot_32.shape[4]
    below = act_128.shape[4]
    if middle != 32 * shards or shards % 4 or samples != 4 or shard_out != 64 or (2 * grid[2]) != 8:
        return plain_body(act_64, cot_32, filters_32, act_128)
    core = lax.axis_index("sample") % 2
    cores = core[None].astype(jnp.int32)
    position = lax.axis_index("chan")[None].astype(jnp.int32)
    volume_64 = act_64[0]
    cot_local = cot_32[0]
    slab = volume_64.shape[0] // shards

    rim = lax.ppermute(act_128[:, -1:], "chan", [(i, i + 1) for i in range(shards - 1)])
    turned = filters_32.transpose(0, 1, 2, 4, 3).reshape(27, shard_out, middle)
    sent = pack(cores, turned, cot_local.reshape(-1, shard_out), shards)
    got = exchange(sent, "chan")
    other = partner(got[:, : len(slot_plan()) * shard_out // 2], "sample", 1)
    own = own_signs(position, volume_64)

    grad_upper = filter_gradient(volume_64, cot_local, ((1, 0),) * 3)
    grad_upper = grad_upper.transpose(0, 1, 2, 4, 3).reshape(27, shard_out, middle)
    total_upper = chip_sum(grad_upper, samples).reshape(3, 3, 3, shard_out, middle)
    total_upper = total_upper.transpose(0, 1, 2, 4, 3)

    cot_got = exchange(spread(cores, got, other, own, grid), "chan")
    cot_full, cot_low = unpack(cot_got, (slab, *volume_64.shape[1:3]))

    window = jnp.concatenate([rim, act_128], axis=1)[0]
    grad_lower = filter_gradient(window, cot_low, ((0, 0), (1, 0), (1, 0)))
    blocks = grad_lower.reshape(27, shards, 2, -1, middle).transpose(2, 1, 0, 3, 4)
    mine = lax.dynamic_index_in_dim(blocks, core, 0, keepdims=False)
    theirs = lax.dynamic_index_in_dim(blocks, 1 - core, 0, keepdims=False)
    mine = mine + partner(theirs.astype(low), "sample", 1).astype(wide)
    got_terms = exchange(mine.astype(low), "chan")
    share = jnp.sum(got_terms.astype(wide), axis=0)
    shares = lax.all_gather(share, "sample", axis=0)
    shares = shares.reshape(samples // 2, 2, *share.shape).sum(axis=0) * (1.0 / samples)
    total_lower = shares.transpose(1, 0, 2, 3).reshape(3, 3, 3, below // shards, middle)
    return (total_upper, total_lower, cot_full[None])


def solution(mesh):
    placed = (
        P("sample", None, None, None, None),
        P("sample", None, None, None, "chan"),
        P(None, None, None, None, "chan"),
        P("sample", "chan", None, None, None),
    )
    return jax.shard_map(
        body,
        mesh=mesh,
        in_specs=placed,
        out_specs=(
            P(None, None, None, None, "chan"),
            P(None, None, None, "chan", None),
            P("sample", "chan", None, None, None),
        ),
        check_vma=False,
    )
```

```python
import functools
import math

import jax
import jax.numpy as jnp
from jax import lax
from jax.experimental import pallas as pl
from jax.experimental.pallas import tpu as pltpu
from jax.sharding import PartitionSpec as P

leak_slope = 0.3
low = jnp.bfloat16
wide = jnp.float32
params = pltpu.CompilerParams(vmem_limit_bytes=40 * 2**20)
whole = pl.BlockSpec(memory_space=pltpu.VMEM)
scalar = pl.BlockSpec(memory_space=pltpu.SMEM)
anywhere = pl.BlockSpec(memory_space=pltpu.HBM)


def slot_plan():
    groups = []
    for col in range(3):
        groups.append([(1, 1, col), (1, 2, col), (2, 1, col), (2, 2, col)])
    for col in range(3):
        groups.append([(2, 0, col), (1, 0, col), (0, 1, col), (0, 2, col)])
    groups.append([None, (0, 0, 2), (0, 0, 1), (0, 0, 0)])
    return groups


def tap_index(tap):
    return (tap[0] * 3 + tap[1]) * 3 + tap[2]


def lane_slot(shape):
    return lax.broadcasted_iota(jnp.int32, shape, len(shape) - 1) // 32


def pack_kernel(core_ref, filters_ref, cot_ref, sent_ref, held, cot_held, staged, arrived, left):
    taps, half, _ = held.shape
    groups = slot_plan()
    start = pl.multiple_of(core_ref[0] * half, half)
    fetch_filters = pltpu.make_async_copy(filters_ref.at[:, pl.ds(start, half), :], held, arrived.at[0])
    fetch_cot = pltpu.make_async_copy(cot_ref, cot_held, arrived.at[1])
    fetch_cot.start()
    fetch_filters.start()
    slots = lane_slot((half, 128))
    shards = staged.shape[0]
    rows = len(groups) * half
    outs = cot_held.shape[1]
    cells = cot_held.shape[0]

    def send(index, first, count):
        part = pl.ds(first, count)
        return pltpu.make_async_copy(staged.at[:, part, :], sent_ref.at[:, part, :], left.at[index])

    fetch_cot.wait()
    turned_cot = cot_held[...].astype(wide).T.astype(low)
    for d in range(shards):
        for b in range(cells // 128):
            staged[d, pl.ds(rows + b * outs, outs), :] = turned_cot[:, b * 128 : (b + 1) * 128]
    copies = [send(0, rows, cells // 128 * outs)]
    copies[0].start()
    fetch_filters.wait()
    for g, group in enumerate(groups):
        for tile in range(shards // 4):
            turned = []
            for tap in group:
                if tap is None:
                    turned.append([jnp.zeros((half, 128), wide)] * 4)
                    continue
                block = held[tap_index(tap), :, pl.ds(tile * 128, 128)].astype(wide)
                turned.append([block] + [pltpu.roll(block, 32 * r, 1) for r in range(1, 4)])
            for m in range(4):
                joined = turned[0][(0 - m) % 4]
                for k in range(1, 4):
                    joined = jnp.where(slots == k, turned[k][(k - m) % 4], joined)
                staged[tile * 4 + m, pl.ds(g * half, half), :] = joined.astype(low)
        copies.append(send(g + 1, g * half, half))
        copies[-1].start()
    for copy in copies:
        copy.wait()


def pack(core, filters, cot, shards):
    taps, outs, middle = filters.shape
    groups = len(slot_plan())
    shape = (shards, groups * (outs // 2) + cot.shape[0] // 128 * outs, 128)
    return pl.pallas_call(
        pack_kernel,
        out_shape=pltpu.HBM(shape, low),
        in_specs=[scalar, anywhere, anywhere],
        out_specs=anywhere,
        scratch_shapes=[
            pltpu.VMEM((taps, outs // 2, middle), low),
            pltpu.VMEM(cot.shape, low),
            pltpu.VMEM(shape, low),
            pltpu.SemaphoreType.DMA((2,)),
            pltpu.SemaphoreType.DMA((groups + 1,)),
        ],
        compiler_params=params,
        cost_estimate=pl.CostEstimate(flops=10**6, bytes_accessed=3 * 10**6, transcendentals=0),
    )(core, pltpu.with_memory_space_constraint(filters, pltpu.HBM), pltpu.with_memory_space_constraint(cot, pltpu.HBM))


def sign_kernel(position_ref, volume_ref, own_ref):
    part = position_ref[0] % 4
    rows = own_ref.shape[0]
    slots = lane_slot((rows, 128))
    joined = None
    for depth_par in range(2):
        for row_par in range(2):
            slot = depth_par * 2 + row_par
            block = volume_ref[:, depth_par, :, row_par].astype(wide).reshape(rows, 128)
            block = pltpu.roll(block, (slot - part + 4) % 4 * 32, 1)
            joined = block if joined is None else jnp.where(slots == slot, block, joined)
    own_ref[...] = joined.astype(low)


def own_signs(position, volume):
    planes, rows, columns, channels = volume.shape
    split = volume.reshape(planes // 2, 2, rows // 2, 2, columns, channels)
    count = planes * rows * columns // 4
    return pl.pallas_call(
        sign_kernel,
        out_shape=jax.ShapeDtypeStruct((count, 128), low),
        grid_spec=pltpu.PrefetchScalarGridSpec(
            num_scalar_prefetch=1,
            grid=(1,),
            in_specs=[
                pl.BlockSpec(
                    (planes // 2, 2, rows // 2, 2, columns, 128),
                    lambda i, at: (0, 0, 0, 0, 0, at[0] // 4),
                )
            ],
            out_specs=pl.BlockSpec((count, 128), lambda i, at: (0, 0)),
        ),
        compiler_params=params,
        cost_estimate=pl.CostEstimate(flops=10**6, bytes_accessed=4 * 10**6, transcendentals=0),
    )(position, split)


def first_kernel(core_ref, got_ref, products_ref, later_ref, weight, turned):
    shards = got_ref.shape[0]
    half = later_ref.shape[0] // shards
    groups = len(slot_plan())
    core = core_ref[0]
    for c in range(shards):
        span = pl.ds(c * half, half)
        for g in range(groups):
            weight[span, pl.ds(g * 128, 128)] = got_ref[c, pl.ds(g * half, half), :]
        for b in range(later_ref.shape[1] // 128):
            lanes = pl.ds(b * 128, 128)
            first = groups * half + b * 2 * half
            turned[span, lanes] = got_ref[c, pl.ds(pl.multiple_of(first + core * half, half), half), :]
            later_ref[span, lanes] = got_ref[c, pl.ds(pl.multiple_of(first + (1 - core) * half, half), half), :]
    products_ref[...] = lax.dot_general(
        turned[...], weight[...], (((0,), (0,)), ((), ())), preferred_element_type=wide
    )


def spread_kernel(grid, first_ref, later_ref, other_ref, own_ref, sent_ref, weight, products, joined):
    depth, height, width = grid
    cells = depth * height * width
    shards = other_ref.shape[0]
    groups = len(slot_plan())
    half = later_ref.shape[0] // shards
    for c in range(shards):
        for g in range(groups):
            weight[pl.ds(c * half, half), pl.ds(g * 128, 128)] = other_ref[c, pl.ds(g * half, half), :]
    products[pl.ds(0, cells), :] = first_ref[...] + lax.dot_general(
        later_ref[...], weight[...], (((0,), (0,)), ((), ())), preferred_element_type=wide
    )
    products[pl.ds(cells, products.shape[0] - cells), :] = jnp.zeros(
        (products.shape[0] - cells, products.shape[1]), wide
    )
    chunk = cells // shards
    place = lax.broadcasted_iota(jnp.int32, (chunk, 128), 0)
    slots = lane_slot((chunk, 128))
    last_col = place % width == width - 1
    last_row = place // width % height == height - 1
    row_step, plane_step = width, width * height
    for n in range(shards):
        sums = [None, None]
        for col in range(3):
            shift = 1 if col == 0 else 0
            base = n * chunk + shift

            def piece(group, offset):
                return products[pl.ds(base + offset, chunk), pl.ds(group * 128, 128)]

            part = piece(col, 0)
            part = part + jnp.where(slots >= 2, piece(3 + col, plane_step), 0.0)
            by_row = piece(3 + col, row_step)
            moved = pltpu.roll(by_row, 96, 1)
            corner = piece(6, plane_step + row_step)
            if col > 0:
                corner = pltpu.roll(corner, 32 * col, 1)
            rows = jnp.where(slots == 1, by_row, jnp.where(slots == 3, moved + corner, 0.0))
            part = part + jnp.where(last_row, 0.0, rows)
            if shift:
                part = jnp.where(last_col, 0.0, part)
            to = 0 if col == 1 else 1
            sums[to] = part if sums[to] is None else sums[to] + part
        joined[pl.ds(0, chunk, stride=2), :] = sums[0]
        joined[pl.ds(1, chunk, stride=2), :] = sums[1]
        span = pl.ds(n * 2 * chunk, 2 * chunk)
        slope = jnp.where(own_ref[span, :].astype(wide) > 0, 1.0, leak_slope)
        sent_ref[n] = (joined[...] * slope).astype(low)


def first_terms(core, got, cells):
    shards = got.shape[0]
    groups = len(slot_plan())
    half = got.shape[1] // (groups + 2 * (cells // 128))
    lanes = groups * 128
    return pl.pallas_call(
        first_kernel,
        out_shape=(
            jax.ShapeDtypeStruct((cells, lanes), wide),
            jax.ShapeDtypeStruct((shards * half, cells), low),
        ),
        in_specs=[scalar, whole],
        out_specs=(whole, whole),
        scratch_shapes=[pltpu.VMEM((shards * half, lanes), low), pltpu.VMEM((shards * half, cells), low)],
        compiler_params=params,
        cost_estimate=pl.CostEstimate(flops=10**8, bytes_accessed=3 * 10**6, transcendentals=0),
    )(core, got)


def spread(first, later, other, own, grid):
    cells, lanes = first.shape
    shards = other.shape[0]
    half = later.shape[0] // shards
    rows = lanes // 128 * half
    return pl.pallas_call(
        functools.partial(spread_kernel, grid),
        out_shape=jax.ShapeDtypeStruct((shards, 2 * cells // shards, 128), low),
        grid=(1,),
        in_specs=[whole, whole, pl.BlockSpec((shards, rows, 128), lambda i: (0, 0, 0)), whole],
        out_specs=whole,
        scratch_shapes=[
            pltpu.VMEM((shards * half, lanes), low),
            pltpu.VMEM((cells + 32, lanes), wide),
            pltpu.VMEM((2 * cells // shards, 128), wide),
        ],
        compiler_params=params,
        cost_estimate=pl.CostEstimate(flops=5 * 10**8, bytes_accessed=3 * 10**6, transcendentals=0),
    )(first, later, other, own)


def unpack_kernel(got_ref, wide_ref):
    shards, rows, _ = got_ref.shape
    planes, height, columns, _ = wide_ref.shape
    slots = lane_slot((rows, 128))
    for tile in range(shards // 4):
        turned = []
        for m in range(4):
            block = got_ref[tile * 4 + m].astype(wide)
            turned.append([block] + [pltpu.roll(block, 32 * r, 1) for r in range(1, 4)])
        for slot in range(4):
            joined = turned[0][(0 - slot) % 4]
            for m in range(1, 4):
                joined = jnp.where(slots == m, turned[m][(m - slot) % 4], joined)
            joined = joined.reshape(planes // 2, height // 2, columns, 128)
            lanes = pl.ds(tile * 128, 128)
            for z in range(planes // 2):
                for y in range(height // 2):
                    at = (2 * z + slot // 2, 2 * y + slot % 2)
                    wide_ref[at[0], at[1], :, lanes] = joined[z, y]


def unpack(got, grid):
    shape = (*grid, got.shape[0] * 32)
    return pl.pallas_call(
        unpack_kernel,
        out_shape=jax.ShapeDtypeStruct(shape, wide),
        in_specs=[whole],
        out_specs=whole,
        compiler_params=params,
        cost_estimate=pl.CostEstimate(flops=10**6, bytes_accessed=2 * 10**6, transcendentals=0),
    )(got)


def window_kernel(rim_ref, volume_ref, window_ref, grid):
    planes, rows, columns, channels = grid.shape
    grid[0] = rim_ref[0].astype(wide)
    grid[pl.ds(1, planes - 1)] = volume_ref[...].astype(wide)
    flat = grid.reshape(planes * rows * columns, channels)
    half = columns // 2
    count = planes * rows * half
    first = lax.broadcasted_iota(jnp.int32, (count, channels), 0) % half == 0
    even = flat[pl.ds(0, count, stride=2), :]
    odd = flat[pl.ds(1, count, stride=2), :]
    before = jnp.where(first, 0.0, pltpu.roll(odd, 1, 0))
    for col, part in enumerate((before, even, odd)):
        part = part.reshape(planes, rows // 2, 2, half, channels)
        on_even, on_odd = part[:, :, 0], part[:, :, 1]
        ahead = jnp.concatenate([jnp.zeros_like(on_odd[:, :1]), on_odd[:, :-1]], axis=1)
        for row, taken in enumerate((ahead, on_even, on_odd)):
            taken = taken.reshape(planes, rows // 2 * half, channels).astype(low)
            for plane in range(planes):
                window_ref[col * 3 + row, plane % 2, plane // 2] = taken[plane]


def windows(rim, volume):
    planes, rows, columns, channels = volume.shape
    shape = (9, 2, planes // 2 + 1, rows * columns // 4, channels)
    return pl.pallas_call(
        window_kernel,
        out_shape=jax.ShapeDtypeStruct(shape, low),
        in_specs=[whole, whole],
        out_specs=whole,
        scratch_shapes=[pltpu.VMEM((planes + 1, rows, columns, channels), wide)],
        compiler_params=params,
        cost_estimate=pl.CostEstimate(flops=10**6, bytes_accessed=4 * 10**6, transcendentals=0),
    )(rim, volume)


def lanes_joined(blocks, slot, slots):
    joined = blocks[0][(0 - slot) % 4]
    for m in range(1, 4):
        joined = jnp.where(slots == m, blocks[m][(m - slot) % 4], joined)
    return joined


def lower_kernel(core_ref, got_ref, other_ref, own_window, other_window, sent_ref, cells, staged, left):
    shards, rows, _ = got_ref.shape
    planes, height, columns, middle = cells.shape
    count = staged.shape[1] // (own_window.shape[4] // shards)
    slots = lane_slot((rows, 128))
    sides = []
    for source in (got_ref, other_ref):
        for tile in range(shards // 4):
            turned = []
            for m in range(4):
                block = source[tile * 4 + m].astype(wide)
                turned.append([block] + [pltpu.roll(block, 32 * r, 1) for r in range(1, 4)])
            for slot in range(4):
                joined = lanes_joined(turned, slot, slots).reshape(planes // 2, height // 2, columns, 128)
                for z in range(planes // 2):
                    for y in range(height // 2):
                        cells[2 * z + slot // 2, 2 * y + slot % 2, :, pl.ds(tile * 128, 128)] = joined[z, y]
        sides.append(cells[...].reshape(planes * height * columns, middle).T.astype(low))
    below = own_window.shape[4]
    share = below // shards
    copies = []
    for pair in range(count // 2):
        total = None
        for side, window in zip(sides, (own_window, other_window), strict=True):
            both = []
            for n in range(2):
                tap = jnp.minimum(core_ref[0] * count + 2 * pair + n, 26)
                depth, row, col = tap // 9, tap // 3 % 3, tap % 3
                taken = window[col * 3 + row, depth % 2, pl.ds(depth // 2, planes)]
                both.append(taken.reshape(planes * height * columns, below))
            term = jnp.dot(side, jnp.concatenate(both, axis=1), preferred_element_type=wide)
            total = term if total is None else total + term
        total = total.T.astype(low)
        for n in range(2):
            for d in range(shards):
                start = n * below + d * share
                staged[d, pl.ds((2 * pair + n) * share, share), :] = total[start : start + share]
        part = pl.ds(2 * pair * share, 2 * share)
        copies.append(pltpu.make_async_copy(staged.at[:, part, :], sent_ref.at[:, part, :], left.at[pair]))
        copies[-1].start()
    for copy in copies:
        copy.wait()


def lower_terms(core, got, other, own_window, other_window, grid):
    shards = got.shape[0]
    below = own_window.shape[4]
    middle = 32 * shards
    return pl.pallas_call(
        lower_kernel,
        out_shape=pltpu.HBM((shards, 14 * below // shards, middle), low),
        in_specs=[scalar, whole, whole, whole, whole],
        out_specs=anywhere,
        scratch_shapes=[
            pltpu.VMEM((*grid, middle), wide),
            pltpu.VMEM((shards, 14 * below // shards, middle), low),
            pltpu.SemaphoreType.DMA((7,)),
        ],
        compiler_params=params,
        cost_estimate=pl.CostEstimate(flops=10**9, bytes_accessed=6 * 10**6, transcendentals=0),
    )(core, got, other, own_window, other_window)


def partner(array, axis, by):
    size = lax.axis_size(axis)
    return lax.ppermute(array, axis, [(i, i ^ by) for i in range(size)])


def exchange(blocks, axis):
    return lax.all_to_all(blocks, axis, split_axis=0, concat_axis=0, tiled=True)


def filter_gradient(volume, cotangent, padding):
    return lax.conv_general_dilated(
        volume[None],
        cotangent[None],
        (1, 1, 1),
        padding,
        rhs_dilation=(2, 2, 2),
        dimension_numbers=("CDHWN", "IDHWO", "DHWNC"),
        preferred_element_type=jnp.float32,
    )


def input_gradient(cotangent, filters):
    return lax.conv_general_dilated(
        cotangent[None],
        filters[::-1, ::-1, ::-1],
        (1, 1, 1),
        ((1, 2), (1, 2), (1, 2)),
        lhs_dilation=(2, 2, 2),
        dimension_numbers=("NDHWC", "DHWOI", "NDHWC"),
        preferred_element_type=jnp.float32,
    )[0]


def plain_body(act_64, cot_32, filters_32, act_128):
    shards = lax.axis_size("chan")
    samples = lax.axis_size("sample")
    position = lax.axis_index("chan")
    core = lax.axis_index("sample") % 2
    volume_64 = act_64[0]
    cot_local = cot_32[0]
    depth, height, width, shard_out = cot_local.shape
    planes, rows, columns, middle = volume_64.shape
    below = act_128.shape[4]
    slab = planes // shards
    part = middle // shards

    rim = lax.ppermute(act_128[:, -1:], "chan", [(i, i + 1) for i in range(shards - 1)])

    taps = filters_32.reshape(27, shards, part, shard_out).transpose(1, 0, 3, 2)
    lanes = 128 if taps.size // shards % 256 == 0 else 64
    taps = taps.reshape(shards, 2, -1, lanes)
    own_half = lax.dynamic_index_in_dim(taps, core, 1, keepdims=False)
    cot_rows = jnp.broadcast_to(cot_local.reshape(1, -1, lanes), (shards, cot_local.size // lanes, lanes))
    sent = jnp.concatenate([own_half, cot_rows], axis=1)
    got = exchange(sent, "chan")
    cut = own_half.shape[1]
    got_half = got[:, :cut]
    other_half = partner(got_half, "sample", 1)
    first = jnp.where(core == 0, got_half, other_half)
    second = jnp.where(core == 0, other_half, got_half)
    part_filters = jnp.concatenate([first, second], axis=1)
    part_filters = part_filters.reshape(shards, 3, 3, 3, shard_out, part)
    part_filters = part_filters.transpose(1, 2, 3, 5, 0, 4).reshape(3, 3, 3, part, -1)
    cot_all = got[:, cut:].reshape(shards, depth, height, width, shard_out)
    cot_all = cot_all.transpose(1, 2, 3, 0, 4).reshape(depth, height, width, -1)

    grad_upper = filter_gradient(volume_64, cot_local, ((1, 0),) * 3)
    total_upper = lax.psum(grad_upper, "sample")

    grad_part = input_gradient(cot_all, part_filters)
    own_part = lax.dynamic_slice_in_dim(volume_64, position * part, part, 3)
    cot_part = (grad_part * jnp.where(own_part > 0, 1.0, leak_slope)).astype(low)
    cot_got = exchange(cot_part.reshape(shards, -1, 128), "chan")
    cot_low = cot_got.reshape(shards, slab, rows, columns, part)
    cot_low = cot_low.transpose(1, 2, 3, 0, 4).reshape(slab, rows, columns, middle)

    window = jnp.concatenate([rim, act_128], axis=1)[0]
    grad_lower = filter_gradient(window, cot_low, ((0, 0), (1, 0), (1, 0)))
    blocks = grad_lower.reshape(27, shards, 2, -1, middle).transpose(2, 1, 0, 3, 4)
    mine = lax.dynamic_index_in_dim(blocks, core, 0, keepdims=False)
    theirs = lax.dynamic_index_in_dim(blocks, 1 - core, 0, keepdims=False)
    mine = mine + partner(theirs.astype(low), "sample", 1).astype(jnp.float32)
    got_terms = exchange(mine.astype(low), "chan")
    share = jnp.sum(got_terms.astype(jnp.float32), axis=0)
    if samples > 2:
        pairs = [[2 * i + k for i in range(samples // 2)] for k in range(2)]
        share = lax.psum(share, "sample", axis_index_groups=pairs)
    share = lax.all_gather(
        share, "sample", axis=1, tiled=True, axis_index_groups=[[i, i + 1] for i in range(0, samples, 2)]
    )
    total_lower = share.reshape(3, 3, 3, below // shards, middle)
    return (
        total_upper / samples,
        total_lower / samples,
        cot_low.astype(jnp.float32)[None],
    )


def core_halves(terms):
    core = lax.axis_index("sample") % 2
    blocks = terms.reshape(27, 2, -1, terms.shape[2])
    mine = lax.dynamic_index_in_dim(blocks, core, 1, keepdims=False)
    theirs = lax.dynamic_index_in_dim(blocks, 1 - core, 1, keepdims=False)
    return mine, theirs.astype(low)


def sample_sum(mine, theirs, samples):
    core = lax.axis_index("sample") % 2
    mine = (mine + partner(theirs, "sample", 1).astype(wide)).astype(low)
    total = mine.astype(wide)
    for by in range(2, samples, 2):
        pairs = [(i, (i + by) % samples) for i in range(samples)]
        total = total + lax.ppermute(mine, "sample", pairs).astype(wide)
    total = total * (1.0 / samples)
    other = partner(total, "sample", 1)
    first = jnp.where(core == 0, total, other)
    second = jnp.where(core == 0, other, total)
    return jnp.concatenate([first, second], axis=1)


def body(act_64, cot_32, filters_32, act_128):
    shards = lax.axis_size("chan")
    samples = lax.axis_size("sample")
    middle = act_64.shape[4]
    grid = cot_32.shape[1:4]
    shard_out = cot_32.shape[4]
    below = act_128.shape[4]
    if middle != 32 * shards or shards % 4 or samples != 4 or shard_out != 64 or (2 * grid[2]) != 8:
        return plain_body(act_64, cot_32, filters_32, act_128)
    core = lax.axis_index("sample") % 2
    cores = core[None].astype(jnp.int32)
    position = lax.axis_index("chan")[None].astype(jnp.int32)
    volume_64 = act_64[0]
    cot_local = cot_32[0]
    slab = volume_64.shape[0] // shards

    rim = lax.ppermute(act_128[:, -1:], "chan", [(i, i + 1) for i in range(shards - 1)])
    turned = filters_32.transpose(0, 1, 2, 4, 3).reshape(27, shard_out, middle)
    sent = pack(cores, turned, cot_local.reshape(-1, shard_out), shards)
    got = exchange(sent, "chan")

    own = own_signs(position, volume_64)
    window = windows(rim[0], act_128[0])
    grad_upper = filter_gradient(volume_64, cot_local, ((1, 0),) * 3)
    grad_upper = grad_upper.transpose(0, 1, 2, 4, 3).reshape(27, shard_out, middle)
    halves = core_halves(grad_upper)
    got, own, window, halves = lax.optimization_barrier((got, own, window, halves))
    other = partner(got, "sample", 1)
    first, later = first_terms(cores, got, math.prod(grid))
    cot_sent = spread(first, later, other, own, grid)

    cot_sent, window, halves = lax.optimization_barrier((cot_sent, window, halves))
    cot_got = exchange(cot_sent, "chan")
    other_window = partner(window, "sample", 1)
    total_upper = sample_sum(*halves, samples).reshape(3, 3, 3, shard_out, middle)
    total_upper = total_upper.transpose(0, 1, 2, 4, 3)

    other_cot = partner(cot_got, "sample", 1)
    slab_grid = (slab, *volume_64.shape[1:3])
    terms = lower_terms(cores, cot_got, other_cot, window, other_window, slab_grid)
    share = jnp.sum(exchange(terms, "chan").astype(wide), axis=0)
    cot_full = unpack(cot_got, slab_grid)
    shares = lax.all_gather(share.astype(low), "sample", axis=0).astype(wide)
    shares = shares.reshape(samples // 2, -1, middle).sum(axis=0) * (1.0 / samples)
    total_lower = shares[: 27 * below // shards].reshape(3, 3, 3, below // shards, middle)
    return (total_upper, total_lower, cot_full[None])


def solution(mesh):
    placed = (
        P("sample", None, None, None, None),
        P("sample", None, None, None, "chan"),
        P(None, None, None, None, "chan"),
        P("sample", "chan", None, None, None),
    )
    return jax.shard_map(
        body,
        mesh=mesh,
        in_specs=placed,
        out_specs=(
            P(None, None, None, None, "chan"),
            P(None, None, None, "chan", None),
            P("sample", "chan", None, None, None),
        ),
        check_vma=False,
    )
```

```python
import functools
import math

import jax
import jax.numpy as jnp
from jax import lax
from jax.experimental import pallas as pl
from jax.experimental.pallas import tpu as pltpu
from jax.sharding import PartitionSpec as P

leak_slope = 0.3
low = jnp.bfloat16
wide = jnp.float32
params = pltpu.CompilerParams(vmem_limit_bytes=20 * 2**20)
whole = pl.BlockSpec(memory_space=pltpu.VMEM)
scalar = pl.BlockSpec(memory_space=pltpu.SMEM)
anywhere = pl.BlockSpec(memory_space=pltpu.HBM)


def slot_plan():
    groups = []
    for col in range(3):
        groups.append([(1, 1, col), (1, 2, col), (2, 1, col), (2, 2, col)])
    for col in range(3):
        groups.append([(2, 0, col), (1, 0, col), (0, 1, col), (0, 2, col)])
    groups.append([None, (0, 0, 2), (0, 0, 1), (0, 0, 0)])
    return groups


def tap_index(tap):
    return (tap[0] * 3 + tap[1]) * 3 + tap[2]


def lane_slot(shape):
    return lax.broadcasted_iota(jnp.int32, shape, len(shape) - 1) // 32


def pack_kernel(core_ref, filters_ref, cot_ref, sent_ref, held, cot_held, staged, arrived, left):
    taps, half, _ = held.shape
    groups = slot_plan()
    start = pl.multiple_of(core_ref[0] * half, half)
    fetch_filters = pltpu.make_async_copy(filters_ref.at[:, pl.ds(start, half), :], held, arrived.at[0])
    fetch_cot = pltpu.make_async_copy(cot_ref, cot_held, arrived.at[1])
    fetch_cot.start()
    fetch_filters.start()
    slots = lane_slot((half, 128))
    shards = staged.shape[0]
    rows = len(groups) * half
    outs = cot_held.shape[1]
    cells = cot_held.shape[0]

    def send(index, first, count):
        part = pl.ds(first, count)
        return pltpu.make_async_copy(staged.at[:, part, :], sent_ref.at[:, part, :], left.at[index])

    fetch_cot.wait()
    turned_cot = cot_held[...].astype(wide).T.astype(low)
    for d in range(shards):
        for b in range(cells // 128):
            staged[d, pl.ds(rows + b * outs, outs), :] = turned_cot[:, b * 128 : (b + 1) * 128]
    copies = [send(0, rows, cells // 128 * outs)]
    copies[0].start()
    fetch_filters.wait()
    for g, group in enumerate(groups):
        for tile in range(shards // 4):
            turned = []
            for tap in group:
                if tap is None:
                    turned.append([jnp.zeros((half, 128), wide)] * 4)
                    continue
                block = held[tap_index(tap), :, pl.ds(tile * 128, 128)].astype(wide)
                turned.append([block] + [pltpu.roll(block, 32 * r, 1) for r in range(1, 4)])
            for m in range(4):
                joined = turned[0][(0 - m) % 4]
                for k in range(1, 4):
                    joined = jnp.where(slots == k, turned[k][(k - m) % 4], joined)
                staged[tile * 4 + m, pl.ds(g * half, half), :] = joined.astype(low)
        copies.append(send(g + 1, g * half, half))
        copies[-1].start()
    for copy in copies:
        copy.wait()


def pack(core, filters, cot, shards):
    taps, outs, middle = filters.shape
    groups = len(slot_plan())
    shape = (shards, groups * (outs // 2) + cot.shape[0] // 128 * outs, 128)
    return pl.pallas_call(
        pack_kernel,
        out_shape=pltpu.HBM(shape, low),
        in_specs=[scalar, anywhere, anywhere],
        out_specs=anywhere,
        scratch_shapes=[
            pltpu.VMEM((taps, outs // 2, middle), low),
            pltpu.VMEM(cot.shape, low),
            pltpu.VMEM(shape, low),
            pltpu.SemaphoreType.DMA((2,)),
            pltpu.SemaphoreType.DMA((groups + 1,)),
        ],
        compiler_params=params,
        cost_estimate=pl.CostEstimate(flops=10**6, bytes_accessed=3 * 10**6, transcendentals=0),
    )(core, pltpu.with_memory_space_constraint(filters, pltpu.HBM), pltpu.with_memory_space_constraint(cot, pltpu.HBM))


def sign_kernel(position_ref, volume_ref, own_ref):
    part = position_ref[0] % 4
    rows = own_ref.shape[0]
    slots = lane_slot((rows, 128))
    joined = None
    for depth_par in range(2):
        for row_par in range(2):
            slot = depth_par * 2 + row_par
            block = volume_ref[:, depth_par, :, row_par].astype(wide).reshape(rows, 128)
            block = pltpu.roll(block, (slot - part + 4) % 4 * 32, 1)
            joined = block if joined is None else jnp.where(slots == slot, block, joined)
    own_ref[...] = joined.astype(low)


def own_signs(position, volume):
    planes, rows, columns, channels = volume.shape
    split = volume.reshape(planes // 2, 2, rows // 2, 2, columns, channels)
    count = planes * rows * columns // 4
    return pl.pallas_call(
        sign_kernel,
        out_shape=jax.ShapeDtypeStruct((count, 128), low),
        grid_spec=pltpu.PrefetchScalarGridSpec(
            num_scalar_prefetch=1,
            grid=(1,),
            in_specs=[
                pl.BlockSpec(
                    (planes // 2, 2, rows // 2, 2, columns, 128),
                    lambda i, at: (0, 0, 0, 0, 0, at[0] // 4),
                )
            ],
            out_specs=pl.BlockSpec((count, 128), lambda i, at: (0, 0)),
        ),
        compiler_params=params,
        cost_estimate=pl.CostEstimate(flops=10**6, bytes_accessed=4 * 10**6, transcendentals=0),
    )(position, split)


def first_kernel(core_ref, got_ref, products_ref, later_ref, weight, turned):
    shards = got_ref.shape[0]
    half = later_ref.shape[0] // shards
    groups = len(slot_plan())
    core = core_ref[0]
    for c in range(shards):
        span = pl.ds(c * half, half)
        for g in range(groups):
            weight[span, pl.ds(g * 128, 128)] = got_ref[c, pl.ds(g * half, half), :]
        for b in range(later_ref.shape[1] // 128):
            lanes = pl.ds(b * 128, 128)
            first = groups * half + b * 2 * half
            turned[span, lanes] = got_ref[c, pl.ds(pl.multiple_of(first + core * half, half), half), :]
            later_ref[span, lanes] = got_ref[c, pl.ds(pl.multiple_of(first + (1 - core) * half, half), half), :]
    products_ref[...] = lax.dot_general(
        turned[...], weight[...], (((0,), (0,)), ((), ())), preferred_element_type=wide
    )


def spread_kernel(grid, first_ref, later_ref, other_ref, own_ref, sent_ref, weight, products, joined):
    depth, height, width = grid
    cells = depth * height * width
    shards = other_ref.shape[0]
    groups = len(slot_plan())
    half = later_ref.shape[0] // shards
    for c in range(shards):
        for g in range(groups):
            weight[pl.ds(c * half, half), pl.ds(g * 128, 128)] = other_ref[c, pl.ds(g * half, half), :]
    products[pl.ds(0, cells), :] = first_ref[...] + lax.dot_general(
        later_ref[...], weight[...], (((0,), (0,)), ((), ())), preferred_element_type=wide
    )
    products[pl.ds(cells, products.shape[0] - cells), :] = jnp.zeros(
        (products.shape[0] - cells, products.shape[1]), wide
    )
    chunk = cells // shards
    place = lax.broadcasted_iota(jnp.int32, (chunk, 128), 0)
    slots = lane_slot((chunk, 128))
    last_col = place % width == width - 1
    last_row = place // width % height == height - 1
    row_step, plane_step = width, width * height
    for n in range(shards):
        sums = [None, None]
        for col in range(3):
            shift = 1 if col == 0 else 0
            base = n * chunk + shift

            def piece(group, offset):
                return products[pl.ds(base + offset, chunk), pl.ds(group * 128, 128)]

            part = piece(col, 0)
            part = part + jnp.where(slots >= 2, piece(3 + col, plane_step), 0.0)
            by_row = piece(3 + col, row_step)
            moved = pltpu.roll(by_row, 96, 1)
            corner = piece(6, plane_step + row_step)
            if col > 0:
                corner = pltpu.roll(corner, 32 * col, 1)
            rows = jnp.where(slots == 1, by_row, jnp.where(slots == 3, moved + corner, 0.0))
            part = part + jnp.where(last_row, 0.0, rows)
            if shift:
                part = jnp.where(last_col, 0.0, part)
            to = 0 if col == 1 else 1
            sums[to] = part if sums[to] is None else sums[to] + part
        joined[pl.ds(0, chunk, stride=2), :] = sums[0]
        joined[pl.ds(1, chunk, stride=2), :] = sums[1]
        span = pl.ds(n * 2 * chunk, 2 * chunk)
        slope = jnp.where(own_ref[span, :].astype(wide) > 0, 1.0, leak_slope)
        sent_ref[n] = (joined[...] * slope).astype(low)


def first_terms(core, got, cells):
    shards = got.shape[0]
    groups = len(slot_plan())
    half = got.shape[1] // (groups + 2 * (cells // 128))
    lanes = groups * 128
    return pl.pallas_call(
        first_kernel,
        out_shape=(
            jax.ShapeDtypeStruct((cells, lanes), wide),
            jax.ShapeDtypeStruct((shards * half, cells), low),
        ),
        in_specs=[scalar, whole],
        out_specs=(whole, whole),
        scratch_shapes=[pltpu.VMEM((shards * half, lanes), low), pltpu.VMEM((shards * half, cells), low)],
        compiler_params=params,
        cost_estimate=pl.CostEstimate(flops=10**8, bytes_accessed=3 * 10**6, transcendentals=0),
    )(core, got)


def spread(first, later, other, own, grid):
    cells, lanes = first.shape
    shards = other.shape[0]
    half = later.shape[0] // shards
    rows = lanes // 128 * half
    return pl.pallas_call(
        functools.partial(spread_kernel, grid),
        out_shape=jax.ShapeDtypeStruct((shards, 2 * cells // shards, 128), low),
        grid=(1,),
        in_specs=[whole, whole, pl.BlockSpec((shards, rows, 128), lambda i: (0, 0, 0)), whole],
        out_specs=whole,
        scratch_shapes=[
            pltpu.VMEM((shards * half, lanes), low),
            pltpu.VMEM((cells + 32, lanes), wide),
            pltpu.VMEM((2 * cells // shards, 128), wide),
        ],
        compiler_params=params,
        cost_estimate=pl.CostEstimate(flops=5 * 10**8, bytes_accessed=3 * 10**6, transcendentals=0),
    )(first, later, other, own)


def unpack_kernel(got_ref, wide_ref):
    shards, rows, _ = got_ref.shape
    planes, height, columns, _ = wide_ref.shape
    slots = lane_slot((rows, 128))
    for tile in range(shards // 4):
        turned = []
        for m in range(4):
            block = got_ref[tile * 4 + m].astype(wide)
            turned.append([block] + [pltpu.roll(block, 32 * r, 1) for r in range(1, 4)])
        for slot in range(4):
            joined = turned[0][(0 - slot) % 4]
            for m in range(1, 4):
                joined = jnp.where(slots == m, turned[m][(m - slot) % 4], joined)
            joined = joined.reshape(planes // 2, height // 2, columns, 128)
            lanes = pl.ds(tile * 128, 128)
            for z in range(planes // 2):
                for y in range(height // 2):
                    at = (2 * z + slot // 2, 2 * y + slot % 2)
                    wide_ref[at[0], at[1], :, lanes] = joined[z, y]


def unpack(got, grid):
    shape = (*grid, got.shape[0] * 32)
    return pl.pallas_call(
        unpack_kernel,
        out_shape=jax.ShapeDtypeStruct(shape, wide),
        in_specs=[whole],
        out_specs=whole,
        compiler_params=params,
        cost_estimate=pl.CostEstimate(flops=10**6, bytes_accessed=2 * 10**6, transcendentals=0),
    )(got)


def tap_cells(flat, planes, rows, columns):
    channels = flat.shape[1]
    half = columns // 2
    count = planes * rows * half
    first = lax.broadcasted_iota(jnp.int32, (count, channels), 0) % half == 0
    even = flat[pl.ds(0, count, stride=2), :]
    odd = flat[pl.ds(1, count, stride=2), :]
    before = jnp.where(first, 0.0, pltpu.roll(odd, 1, 0))
    cells = []
    for part in (before, even, odd):
        part = part.reshape(planes, rows // 2, 2, half, channels)
        on_even, on_odd = part[:, :, 0], part[:, :, 1]
        ahead = jnp.concatenate([jnp.zeros_like(on_odd[:, :1]), on_odd[:, :-1]], axis=1)
        for taken in (ahead, on_even, on_odd):
            cells.append(taken.reshape(planes, rows // 2 * half, channels).astype(low))
    return cells


def window_kernel(volume_ref, window_ref, done_ref, flat):
    done_ref[...] = jnp.zeros_like(done_ref)
    planes, rows, columns, _ = volume_ref.shape
    flat[...] = volume_ref[...].astype(wide).reshape(flat.shape)
    for n, taken in enumerate(tap_cells(flat, planes, rows, columns)):
        for plane in range(planes):
            window_ref[n, plane % 2, plane // 2] = taken[plane]


def windows(volume):
    planes, rows, columns, channels = volume.shape
    shape = (9, 2, planes // 2, rows * columns // 4, channels)
    return pl.pallas_call(
        window_kernel,
        out_shape=(jax.ShapeDtypeStruct(shape, low), jax.ShapeDtypeStruct((8, 128), wide)),
        in_specs=[whole],
        out_specs=(whole, whole),
        scratch_shapes=[pltpu.VMEM((planes * rows * columns, channels), wide)],
        compiler_params=params,
        cost_estimate=pl.CostEstimate(flops=10**6, bytes_accessed=4 * 10**6, transcendentals=0),
    )(volume)


def lanes_joined(blocks, slot, slots):
    joined = blocks[0][(0 - slot) % 4]
    for m in range(1, 4):
        joined = jnp.where(slots == m, blocks[m][(m - slot) % 4], joined)
    return joined


def cotangent_side(source_ref, cells):
    shards, rows, _ = source_ref.shape
    planes, height, columns, middle = cells.shape
    slots = lane_slot((rows, 128))
    for tile in range(shards // 4):
        turned = []
        for m in range(4):
            block = source_ref[tile * 4 + m].astype(wide)
            turned.append([block] + [pltpu.roll(block, 32 * r, 1) for r in range(1, 4)])
        for slot in range(4):
            joined = lanes_joined(turned, slot, slots).reshape(planes // 2, height // 2, columns, 128)
            for z in range(planes // 2):
                for y in range(height // 2):
                    cells[2 * z + slot // 2, 2 * y + slot % 2, :, pl.ds(tile * 128, 128)] = joined[z, y]
    return cells[...].reshape(planes * height * columns, middle).T.astype(low)


def rim_cells(rim_ref, flat, first_cells):
    _, rows, columns, _ = rim_ref.shape
    flat[...] = rim_ref[...].astype(wide).reshape(flat.shape)
    for n, taken in enumerate(tap_cells(flat, 1, rows, columns)):
        first_cells[n] = taken[0]


def tap_pair(window, first_cells, start):
    planes = window.shape[2]
    both = []
    for n in range(2):
        tap = jnp.minimum(start + n, 26)
        depth, row, col = tap // 9, tap // 3 % 3, tap % 3
        which, parity = col * 3 + row, (depth + 1) % 2
        lowest = jnp.where(depth == 0, first_cells[which], window[which, parity, 0])
        below = jnp.where(depth == 0, 0, 1)
        rest = window[which, parity, pl.ds(below, planes - 1)]
        both.append(jnp.concatenate([lowest, rest.reshape(-1, window.shape[4])], axis=0))
    return jnp.concatenate(both, axis=1)


def lower_first_kernel(core_ref, got_ref, window, rim_ref, done_ref, total_ref, cells, flat, first_cells):
    del done_ref
    rim_cells(rim_ref, flat, first_cells)
    side = cotangent_side(got_ref, cells)
    count = total_ref.shape[0]
    for pair in range(count):
        taps = tap_pair(window, first_cells, (core_ref[0] * count + pair) * 2)
        total_ref[pair] = jnp.dot(side, taps, preferred_element_type=wide)


def lower_scratch(grid, middle, window, rim):
    return [
        pltpu.VMEM((*grid, middle), wide),
        pltpu.VMEM((math.prod(rim.shape[:3]), rim.shape[3]), wide),
        pltpu.VMEM((9, *window.shape[3:]), low),
    ]


def lower_first(core, got, window, rim, done, grid):
    middle = 32 * got.shape[0]
    return pl.pallas_call(
        lower_first_kernel,
        out_shape=jax.ShapeDtypeStruct((7, middle, 2 * window.shape[4]), wide),
        in_specs=[scalar, whole, whole, whole, whole],
        out_specs=whole,
        scratch_shapes=lower_scratch(grid, middle, window, rim),
        compiler_params=params,
        cost_estimate=pl.CostEstimate(flops=5 * 10**8, bytes_accessed=5 * 10**6, transcendentals=0),
    )(core, got, window, rim, done)


def lower_kernel(core_ref, total_ref, other_ref, window, rim_ref, sent_ref, cells, flat, first_cells, staged, left):
    rim_cells(rim_ref, flat, first_cells)
    side = cotangent_side(other_ref, cells)
    shards = staged.shape[0]
    below = window.shape[4]
    share = below // shards
    copies = []
    for pair in range(total_ref.shape[0]):
        taps = tap_pair(window, first_cells, (core_ref[0] * total_ref.shape[0] + pair) * 2)
        total = total_ref[pair] + jnp.dot(side, taps, preferred_element_type=wide)
        total = total.T.astype(low)
        for n in range(2):
            for d in range(shards):
                start = n * below + d * share
                staged[d, pl.ds((2 * pair + n) * share, share), :] = total[start : start + share]
        part = pl.ds(2 * pair * share, 2 * share)
        copies.append(pltpu.make_async_copy(staged.at[:, part, :], sent_ref.at[:, part, :], left.at[pair]))
        copies[-1].start()
    for copy in copies:
        copy.wait()


def lower_terms(core, total, other, window, rim, grid):
    shards = other.shape[0]
    pairs, middle, lanes = total.shape
    shape = (shards, pairs * lanes // shards, middle)
    return pl.pallas_call(
        lower_kernel,
        out_shape=pltpu.HBM(shape, low),
        in_specs=[scalar, whole, whole, whole, whole],
        out_specs=anywhere,
        scratch_shapes=lower_scratch(grid, middle, window, rim)
        + [pltpu.VMEM(shape, low), pltpu.SemaphoreType.DMA((pairs,))],
        compiler_params=params,
        cost_estimate=pl.CostEstimate(flops=5 * 10**8, bytes_accessed=5 * 10**6, transcendentals=0),
    )(core, total, other, window, rim)


def upper_kernel(core_ref, volume_ref, cot_ref, mine_ref, theirs_ref, flat, cot_flat, lined, left):
    planes, rows, columns, channels = volume_ref.shape
    depth, height, width, outs = cot_ref.shape
    half = outs // 2
    tiles = channels // 128
    for tile in range(tiles):
        lanes = pl.ds(tile * 128, 128)
        flat[tile] = volume_ref[:, :, :, lanes].astype(wide).reshape(flat.shape[1:])
    cot_wide = cot_ref[...].astype(wide).reshape(cot_flat.shape[0], outs)
    cot_flat[...] = jnp.concatenate([cot_wide, jnp.zeros((cot_flat.shape[0], 128 - outs), wide)], axis=1)
    pieces = [cot_flat[pl.ds(n, depth, stride=height * width), :] for n in range(height * width)]
    left[...] = jnp.concatenate(pieces, axis=0).T[:outs].astype(low)
    core = core_ref[0]
    split = [left[pl.ds(pl.multiple_of(at * half, half), half), :] for at in (core, 1 - core)]
    side = jnp.concatenate(split, axis=0)
    first = lax.broadcasted_iota(jnp.int32, (depth, 128), 0) == 0
    stride = 2 * rows * columns
    for row in range(rows):
        for col in range(columns):
            for tile in range(tiles):
                even = flat[tile, pl.ds(row * columns + col, depth, stride=stride), :]
                odd = flat[tile, pl.ds(stride // 2 + row * columns + col, depth, stride=stride), :]
                before = jnp.where(first, 0.0, pltpu.roll(odd, 1, 0))
                for depth_tap, part in enumerate((before, even, odd)):
                    lined[depth_tap, row, col, :, pl.ds(tile * 128, 128)] = part.astype(low)
    nothing = jnp.zeros((depth, channels), low)
    for tap in range(27):
        depth_tap, row_tap, col_tap = tap // 9, tap // 3 % 3, tap % 3
        taken = []
        for y in range(height):
            for x in range(width):
                row, col = 2 * y + row_tap - 1, 2 * x + col_tap - 1
                taken.append(nothing if row < 0 or col < 0 else lined[depth_tap, row, col])
        term = jnp.dot(side, jnp.concatenate(taken, axis=0), preferred_element_type=wide)
        mine_ref[tap] = term[:half]
        theirs_ref[tap] = term[half:].astype(low)


def upper_terms(core, volume, cot):
    planes, rows, columns, channels = volume.shape
    depth, height, width, outs = cot.shape
    shape = (27, outs // 2, channels)
    return pl.pallas_call(
        upper_kernel,
        out_shape=(jax.ShapeDtypeStruct(shape, wide), jax.ShapeDtypeStruct(shape, low)),
        in_specs=[scalar, whole, whole],
        out_specs=(whole, whole),
        scratch_shapes=[
            pltpu.VMEM((channels // 128, planes * rows * columns, 128), wide),
            pltpu.VMEM((depth * height * width, 128), wide),
            pltpu.VMEM((3, rows, columns, depth, channels), low),
            pltpu.VMEM((outs, depth * height * width), low),
        ],
        compiler_params=params,
        cost_estimate=pl.CostEstimate(flops=5 * 10**8, bytes_accessed=6 * 10**6, transcendentals=0),
    )(core, volume, cot)


def partner(array, axis, by):
    size = lax.axis_size(axis)
    return lax.ppermute(array, axis, [(i, i ^ by) for i in range(size)])


def exchange(blocks, axis):
    return lax.all_to_all(blocks, axis, split_axis=0, concat_axis=0, tiled=True)


def filter_gradient(volume, cotangent, padding):
    return lax.conv_general_dilated(
        volume[None],
        cotangent[None],
        (1, 1, 1),
        padding,
        rhs_dilation=(2, 2, 2),
        dimension_numbers=("CDHWN", "IDHWO", "DHWNC"),
        preferred_element_type=jnp.float32,
    )


def input_gradient(cotangent, filters):
    return lax.conv_general_dilated(
        cotangent[None],
        filters[::-1, ::-1, ::-1],
        (1, 1, 1),
        ((1, 2), (1, 2), (1, 2)),
        lhs_dilation=(2, 2, 2),
        dimension_numbers=("NDHWC", "DHWOI", "NDHWC"),
        preferred_element_type=jnp.float32,
    )[0]


def plain_body(act_64, cot_32, filters_32, act_128):
    shards = lax.axis_size("chan")
    samples = lax.axis_size("sample")
    position = lax.axis_index("chan")
    core = lax.axis_index("sample") % 2
    volume_64 = act_64[0]
    cot_local = cot_32[0]
    depth, height, width, shard_out = cot_local.shape
    planes, rows, columns, middle = volume_64.shape
    below = act_128.shape[4]
    slab = planes // shards
    part = middle // shards

    rim = lax.ppermute(act_128[:, -1:], "chan", [(i, i + 1) for i in range(shards - 1)])

    taps = filters_32.reshape(27, shards, part, shard_out).transpose(1, 0, 3, 2)
    lanes = 128 if taps.size // shards % 256 == 0 else 64
    taps = taps.reshape(shards, 2, -1, lanes)
    own_half = lax.dynamic_index_in_dim(taps, core, 1, keepdims=False)
    cot_rows = jnp.broadcast_to(cot_local.reshape(1, -1, lanes), (shards, cot_local.size // lanes, lanes))
    sent = jnp.concatenate([own_half, cot_rows], axis=1)
    got = exchange(sent, "chan")
    cut = own_half.shape[1]
    got_half = got[:, :cut]
    other_half = partner(got_half, "sample", 1)
    first = jnp.where(core == 0, got_half, other_half)
    second = jnp.where(core == 0, other_half, got_half)
    part_filters = jnp.concatenate([first, second], axis=1)
    part_filters = part_filters.reshape(shards, 3, 3, 3, shard_out, part)
    part_filters = part_filters.transpose(1, 2, 3, 5, 0, 4).reshape(3, 3, 3, part, -1)
    cot_all = got[:, cut:].reshape(shards, depth, height, width, shard_out)
    cot_all = cot_all.transpose(1, 2, 3, 0, 4).reshape(depth, height, width, -1)

    grad_upper = filter_gradient(volume_64, cot_local, ((1, 0),) * 3)
    total_upper = lax.psum(grad_upper, "sample")

    grad_part = input_gradient(cot_all, part_filters)
    own_part = lax.dynamic_slice_in_dim(volume_64, position * part, part, 3)
    cot_part = (grad_part * jnp.where(own_part > 0, 1.0, leak_slope)).astype(low)
    cot_got = exchange(cot_part.reshape(shards, -1, 128), "chan")
    cot_low = cot_got.reshape(shards, slab, rows, columns, part)
    cot_low = cot_low.transpose(1, 2, 3, 0, 4).reshape(slab, rows, columns, middle)

    window = jnp.concatenate([rim, act_128], axis=1)[0]
    grad_lower = filter_gradient(window, cot_low, ((0, 0), (1, 0), (1, 0)))
    blocks = grad_lower.reshape(27, shards, 2, -1, middle).transpose(2, 1, 0, 3, 4)
    mine = lax.dynamic_index_in_dim(blocks, core, 0, keepdims=False)
    theirs = lax.dynamic_index_in_dim(blocks, 1 - core, 0, keepdims=False)
    mine = mine + partner(theirs.astype(low), "sample", 1).astype(jnp.float32)
    got_terms = exchange(mine.astype(low), "chan")
    share = jnp.sum(got_terms.astype(jnp.float32), axis=0)
    if samples > 2:
        pairs = [[2 * i + k for i in range(samples // 2)] for k in range(2)]
        share = lax.psum(share, "sample", axis_index_groups=pairs)
    share = lax.all_gather(
        share, "sample", axis=1, tiled=True, axis_index_groups=[[i, i + 1] for i in range(0, samples, 2)]
    )
    total_lower = share.reshape(3, 3, 3, below // shards, middle)
    return (
        total_upper / samples,
        total_lower / samples,
        cot_low.astype(jnp.float32)[None],
    )


def core_sum(mine, theirs):
    return (mine + partner(theirs, "sample", 1).astype(wide)).astype(low)


def sample_sum(mine, samples):
    core = lax.axis_index("sample") % 2
    total = mine.astype(wide)
    for by in range(2, samples, 2):
        pairs = [(i, (i + by) % samples) for i in range(samples)]
        total = total + lax.ppermute(mine, "sample", pairs).astype(wide)
    total = total * (1.0 / samples)
    other = partner(total, "sample", 1)
    first = jnp.where(core == 0, total, other)
    second = jnp.where(core == 0, other, total)
    return jnp.concatenate([first, second], axis=1)


def body(act_64, cot_32, filters_32, act_128):
    shards = lax.axis_size("chan")
    samples = lax.axis_size("sample")
    middle = act_64.shape[4]
    grid = cot_32.shape[1:4]
    shard_out = cot_32.shape[4]
    below = act_128.shape[4]
    if middle != 32 * shards or shards % 4 or samples != 4 or shard_out != 64 or (2 * grid[2]) != 8:
        return plain_body(act_64, cot_32, filters_32, act_128)
    core = lax.axis_index("sample") % 2
    cores = core[None].astype(jnp.int32)
    position = lax.axis_index("chan")[None].astype(jnp.int32)
    volume_64 = act_64[0]
    cot_local = cot_32[0]
    slab = volume_64.shape[0] // shards

    rim = lax.ppermute(act_128[:, -1:], "chan", [(i, i + 1) for i in range(shards - 1)])
    turned = filters_32.transpose(0, 1, 2, 4, 3).reshape(27, shard_out, middle)
    sent = pack(cores, turned, cot_local.reshape(-1, shard_out), shards)
    got = exchange(sent, "chan")

    own = own_signs(position, volume_64)
    other_act = partner(act_128, "sample", 1)
    halves = upper_terms(cores, volume_64, cot_local)
    window, done = windows(act_128[0])
    other_window, other_done = windows(other_act[0])
    done = done + other_done
    got, own, rim, done, halves = lax.optimization_barrier((got, own, rim, done, halves))
    other = partner(got, "sample", 1)
    first, later = first_terms(cores, got, math.prod(grid))
    cot_sent = spread(first, later, other, own, grid)

    cot_sent, rim, halves = lax.optimization_barrier((cot_sent, rim, halves))
    cot_got = exchange(cot_sent, "chan")
    chip_upper = core_sum(*halves)
    chip_upper, rim = lax.optimization_barrier((chip_upper, rim))
    other_rim = partner(rim, "sample", 1)
    total_upper = sample_sum(chip_upper, samples).reshape(3, 3, 3, shard_out, middle)
    total_upper = total_upper.transpose(0, 1, 2, 4, 3)

    other_cot = partner(cot_got, "sample", 1)
    slab_grid = (slab, *volume_64.shape[1:3])
    own_terms = lower_first(cores, cot_got, window, rim[0], done, slab_grid)
    terms = lower_terms(cores, own_terms, other_cot, other_window, other_rim[0], slab_grid)
    share = jnp.sum(exchange(terms, "chan").astype(wide), axis=0)
    cot_full = unpack(cot_got, slab_grid)
    shares = lax.all_gather(share.astype(low), "sample", axis=0).astype(wide)
    shares = shares.reshape(samples // 2, -1, middle).sum(axis=0) * (1.0 / samples)
    total_lower = shares[: 27 * below // shards].reshape(3, 3, 3, below // shards, middle)
    return (total_upper, total_lower, cot_full[None])


def solution(mesh):
    placed = (
        P("sample", None, None, None, None),
        P("sample", None, None, None, "chan"),
        P(None, None, None, None, "chan"),
        P("sample", "chan", None, None, None),
    )
    return jax.shard_map(
        body,
        mesh=mesh,
        in_specs=placed,
        out_specs=(
            P(None, None, None, None, "chan"),
            P(None, None, None, "chan", None),
            P("sample", "chan", None, None, None),
        ),
        check_vma=False,
    )
```

```python
import functools
import math

import jax
import jax.numpy as jnp
from jax import lax
from jax.experimental import pallas as pl
from jax.experimental.pallas import tpu as pltpu
from jax.sharding import PartitionSpec as P

leak_slope = 0.3
low = jnp.bfloat16
wide = jnp.float32
params = pltpu.CompilerParams(vmem_limit_bytes=20 * 2**20)
whole = pl.BlockSpec(memory_space=pltpu.VMEM)
scalar = pl.BlockSpec(memory_space=pltpu.SMEM)
anywhere = pl.BlockSpec(memory_space=pltpu.HBM)


def slot_plan():
    groups = []
    for col in range(3):
        groups.append([(1, 1, col), (1, 2, col), (2, 1, col), (2, 2, col)])
    for col in range(3):
        groups.append([(2, 0, col), (1, 0, col), (0, 1, col), (0, 2, col)])
    groups.append([None, (0, 0, 2), (0, 0, 1), (0, 0, 0)])
    return groups


def tap_index(tap):
    return (tap[0] * 3 + tap[1]) * 3 + tap[2]


def lane_slot(shape):
    return lax.broadcasted_iota(jnp.int32, shape, len(shape) - 1) // 32


def pack_kernel(core_ref, filters_ref, cot_ref, sent_ref, held, cot_held, staged, arrived, left):
    taps, half, _ = held.shape
    groups = slot_plan()
    start = pl.multiple_of(core_ref[0] * half, half)
    fetch_filters = pltpu.make_async_copy(filters_ref.at[:, pl.ds(start, half), :], held, arrived.at[0])
    fetch_cot = pltpu.make_async_copy(cot_ref, cot_held, arrived.at[1])
    fetch_cot.start()
    fetch_filters.start()
    slots = lane_slot((half, 128))
    shards = staged.shape[0]
    rows = len(groups) * half
    outs = cot_held.shape[1]
    cells = cot_held.shape[0]

    def send(index, first, count):
        part = pl.ds(first, count)
        return pltpu.make_async_copy(staged.at[:, part, :], sent_ref.at[:, part, :], left.at[index])

    fetch_cot.wait()
    turned_cot = cot_held[...].astype(wide).T.astype(low)
    for d in range(shards):
        for b in range(cells // 128):
            staged[d, pl.ds(rows + b * outs, outs), :] = turned_cot[:, b * 128 : (b + 1) * 128]
    copies = [send(0, rows, cells // 128 * outs)]
    copies[0].start()
    fetch_filters.wait()
    for g, group in enumerate(groups):
        for tile in range(shards // 4):
            turned = []
            for tap in group:
                if tap is None:
                    turned.append([jnp.zeros((half, 128), wide)] * 4)
                    continue
                block = held[tap_index(tap), :, pl.ds(tile * 128, 128)].astype(wide)
                turned.append([block] + [pltpu.roll(block, 32 * r, 1) for r in range(1, 4)])
            for m in range(4):
                joined = turned[0][(0 - m) % 4]
                for k in range(1, 4):
                    joined = jnp.where(slots == k, turned[k][(k - m) % 4], joined)
                staged[tile * 4 + m, pl.ds(g * half, half), :] = joined.astype(low)
        copies.append(send(g + 1, g * half, half))
        copies[-1].start()
    for copy in copies:
        copy.wait()


def pack(core, filters, cot, shards):
    taps, outs, middle = filters.shape
    groups = len(slot_plan())
    shape = (shards, groups * (outs // 2) + cot.shape[0] // 128 * outs, 128)
    return pl.pallas_call(
        pack_kernel,
        out_shape=pltpu.HBM(shape, low),
        in_specs=[scalar, anywhere, anywhere],
        out_specs=anywhere,
        scratch_shapes=[
            pltpu.VMEM((taps, outs // 2, middle), low),
            pltpu.VMEM(cot.shape, low),
            pltpu.VMEM(shape, low),
            pltpu.SemaphoreType.DMA((2,)),
            pltpu.SemaphoreType.DMA((groups + 1,)),
        ],
        compiler_params=params,
        cost_estimate=pl.CostEstimate(flops=10**6, bytes_accessed=3 * 10**6, transcendentals=0),
    )(core, pltpu.with_memory_space_constraint(filters, pltpu.HBM), pltpu.with_memory_space_constraint(cot, pltpu.HBM))


def sign_kernel(position_ref, volume_ref, own_ref):
    part = position_ref[0] % 4
    rows = own_ref.shape[0]
    slots = lane_slot((rows, 128))
    joined = None
    for depth_par in range(2):
        for row_par in range(2):
            slot = depth_par * 2 + row_par
            block = volume_ref[:, depth_par, :, row_par].astype(wide).reshape(rows, 128)
            block = pltpu.roll(block, (slot - part + 4) % 4 * 32, 1)
            joined = block if joined is None else jnp.where(slots == slot, block, joined)
    own_ref[...] = joined.astype(low)


def own_signs(position, volume):
    planes, rows, columns, channels = volume.shape
    split = volume.reshape(planes // 2, 2, rows // 2, 2, columns, channels)
    count = planes * rows * columns // 4
    return pl.pallas_call(
        sign_kernel,
        out_shape=jax.ShapeDtypeStruct((count, 128), low),
        grid_spec=pltpu.PrefetchScalarGridSpec(
            num_scalar_prefetch=1,
            grid=(1,),
            in_specs=[
                pl.BlockSpec(
                    (planes // 2, 2, rows // 2, 2, columns, 128),
                    lambda i, at: (0, 0, 0, 0, 0, at[0] // 4),
                )
            ],
            out_specs=pl.BlockSpec((count, 128), lambda i, at: (0, 0)),
        ),
        compiler_params=params,
        cost_estimate=pl.CostEstimate(flops=10**6, bytes_accessed=4 * 10**6, transcendentals=0),
    )(position, split)


def weight_kernel(got_ref, weight_ref):
    shards = got_ref.shape[0]
    groups = len(slot_plan())
    half = weight_ref.shape[0] // shards
    for c in range(shards):
        for g in range(groups):
            weight_ref[pl.ds(c * half, half), pl.ds(g * 128, 128)] = got_ref[c, pl.ds(g * half, half), :]


def weights(got, half):
    shards = got.shape[0]
    groups = len(slot_plan())
    return pl.pallas_call(
        weight_kernel,
        out_shape=jax.ShapeDtypeStruct((shards * half, groups * 128), low),
        grid=(1,),
        in_specs=[pl.BlockSpec((shards, groups * half, 128), lambda i: (0, 0, 0))],
        out_specs=whole,
        compiler_params=params,
        cost_estimate=pl.CostEstimate(flops=10**5, bytes_accessed=10**6, transcendentals=0),
    )(got)


def first_kernel(core_ref, got_ref, weight_ref, products_ref, later_ref, turned):
    shards = got_ref.shape[0]
    half = later_ref.shape[0] // shards
    groups = len(slot_plan())
    core = core_ref[0]
    for c in range(shards):
        span = pl.ds(c * half, half)
        for b in range(later_ref.shape[1] // 128):
            lanes = pl.ds(b * 128, 128)
            first = groups * half + b * 2 * half
            turned[span, lanes] = got_ref[c, pl.ds(pl.multiple_of(first + core * half, half), half), :]
            later_ref[span, lanes] = got_ref[c, pl.ds(pl.multiple_of(first + (1 - core) * half, half), half), :]
    products_ref[...] = lax.dot_general(
        turned[...], weight_ref[...], (((0,), (0,)), ((), ())), preferred_element_type=wide
    )


def spread_kernel(grid, first_ref, later_ref, other_ref, own_ref, sent_ref, products, joined):
    depth, height, width = grid
    cells = depth * height * width
    shards = sent_ref.shape[0]
    products[pl.ds(0, cells), :] = first_ref[...] + lax.dot_general(
        later_ref[...], other_ref[...], (((0,), (0,)), ((), ())), preferred_element_type=wide
    )
    products[pl.ds(cells, products.shape[0] - cells), :] = jnp.zeros(
        (products.shape[0] - cells, products.shape[1]), wide
    )
    chunk = cells // shards
    place = lax.broadcasted_iota(jnp.int32, (chunk, 128), 0)
    slots = lane_slot((chunk, 128))
    last_col = place % width == width - 1
    last_row = place // width % height == height - 1
    row_step, plane_step = width, width * height
    for n in range(shards):
        sums = [None, None]
        for col in range(3):
            shift = 1 if col == 0 else 0
            base = n * chunk + shift

            def piece(group, offset):
                return products[pl.ds(base + offset, chunk), pl.ds(group * 128, 128)]

            part = piece(col, 0)
            part = part + jnp.where(slots >= 2, piece(3 + col, plane_step), 0.0)
            by_row = piece(3 + col, row_step)
            moved = pltpu.roll(by_row, 96, 1)
            corner = piece(6, plane_step + row_step)
            if col > 0:
                corner = pltpu.roll(corner, 32 * col, 1)
            rows = jnp.where(slots == 1, by_row, jnp.where(slots == 3, moved + corner, 0.0))
            part = part + jnp.where(last_row, 0.0, rows)
            if shift:
                part = jnp.where(last_col, 0.0, part)
            to = 0 if col == 1 else 1
            sums[to] = part if sums[to] is None else sums[to] + part
        joined[pl.ds(0, chunk, stride=2), :] = sums[0]
        joined[pl.ds(1, chunk, stride=2), :] = sums[1]
        span = pl.ds(n * 2 * chunk, 2 * chunk)
        slope = jnp.where(own_ref[span, :].astype(wide) > 0, 1.0, leak_slope)
        sent_ref[n] = (joined[...] * slope).astype(low)


def first_terms(core, got, weight, cells):
    rows, lanes = weight.shape
    return pl.pallas_call(
        first_kernel,
        out_shape=(jax.ShapeDtypeStruct((cells, lanes), wide), jax.ShapeDtypeStruct((rows, cells), low)),
        in_specs=[scalar, whole, whole],
        out_specs=(whole, whole),
        scratch_shapes=[pltpu.VMEM((rows, cells), low)],
        compiler_params=params,
        cost_estimate=pl.CostEstimate(flops=10**8, bytes_accessed=3 * 10**6, transcendentals=0),
    )(core, got, weight)


def spread(first, later, other, own, grid, shards):
    cells, lanes = first.shape
    return pl.pallas_call(
        functools.partial(spread_kernel, grid),
        out_shape=jax.ShapeDtypeStruct((shards, 2 * cells // shards, 128), low),
        in_specs=[whole, whole, whole, whole],
        out_specs=whole,
        scratch_shapes=[
            pltpu.VMEM((cells + 32, lanes), wide),
            pltpu.VMEM((2 * cells // shards, 128), wide),
        ],
        compiler_params=params,
        cost_estimate=pl.CostEstimate(flops=5 * 10**8, bytes_accessed=3 * 10**6, transcendentals=0),
    )(first, later, other, own)


def unpack_kernel(got_ref, wide_ref):
    shards, rows, _ = got_ref.shape
    planes, height, columns, _ = wide_ref.shape
    slots = lane_slot((rows, 128))
    for tile in range(shards // 4):
        turned = []
        for m in range(4):
            block = got_ref[tile * 4 + m].astype(wide)
            turned.append([block] + [pltpu.roll(block, 32 * r, 1) for r in range(1, 4)])
        for slot in range(4):
            joined = turned[0][(0 - slot) % 4]
            for m in range(1, 4):
                joined = jnp.where(slots == m, turned[m][(m - slot) % 4], joined)
            joined = joined.reshape(planes // 2, height // 2, columns, 128)
            lanes = pl.ds(tile * 128, 128)
            for z in range(planes // 2):
                for y in range(height // 2):
                    at = (2 * z + slot // 2, 2 * y + slot % 2)
                    wide_ref[at[0], at[1], :, lanes] = joined[z, y]


def unpack(got, grid):
    shape = (*grid, got.shape[0] * 32)
    return pl.pallas_call(
        unpack_kernel,
        out_shape=jax.ShapeDtypeStruct(shape, wide),
        in_specs=[whole],
        out_specs=whole,
        compiler_params=params,
        cost_estimate=pl.CostEstimate(flops=10**6, bytes_accessed=2 * 10**6, transcendentals=0),
    )(got)


def tap_cells(flat, planes, rows, columns):
    channels = flat.shape[1]
    half = columns // 2
    count = planes * rows * half
    first = lax.broadcasted_iota(jnp.int32, (count, channels), 0) % half == 0
    even = flat[pl.ds(0, count, stride=2), :]
    odd = flat[pl.ds(1, count, stride=2), :]
    before = jnp.where(first, 0.0, pltpu.roll(odd, 1, 0))
    cells = []
    for part in (before, even, odd):
        part = part.reshape(planes, rows // 2, 2, half, channels)
        on_even, on_odd = part[:, :, 0], part[:, :, 1]
        ahead = jnp.concatenate([jnp.zeros_like(on_odd[:, :1]), on_odd[:, :-1]], axis=1)
        for taken in (ahead, on_even, on_odd):
            cells.append(taken.reshape(planes, rows // 2 * half, channels).astype(low))
    return cells


def window_kernel(volume_ref, window_ref, done_ref, flat):
    done_ref[...] = jnp.zeros_like(done_ref)
    planes, rows, columns, _ = volume_ref.shape
    flat[...] = volume_ref[...].astype(wide).reshape(flat.shape)
    for n, taken in enumerate(tap_cells(flat, planes, rows, columns)):
        for plane in range(planes):
            window_ref[n, plane % 2, plane // 2] = taken[plane]


def windows(volume):
    planes, rows, columns, channels = volume.shape
    shape = (9, 2, planes // 2, rows * columns // 4, channels)
    return pl.pallas_call(
        window_kernel,
        out_shape=(jax.ShapeDtypeStruct(shape, low), jax.ShapeDtypeStruct((8, 128), wide)),
        in_specs=[whole],
        out_specs=(whole, whole),
        scratch_shapes=[pltpu.VMEM((planes * rows * columns, channels), wide)],
        compiler_params=params,
        cost_estimate=pl.CostEstimate(flops=10**6, bytes_accessed=4 * 10**6, transcendentals=0),
    )(volume)


def lanes_joined(blocks, slot, slots):
    joined = blocks[0][(0 - slot) % 4]
    for m in range(1, 4):
        joined = jnp.where(slots == m, blocks[m][(m - slot) % 4], joined)
    return joined


def cotangent_side(source_ref, cells):
    shards, rows, _ = source_ref.shape
    planes, height, columns, middle = cells.shape
    slots = lane_slot((rows, 128))
    for tile in range(shards // 4):
        turned = []
        for m in range(4):
            block = source_ref[tile * 4 + m].astype(wide)
            turned.append([block] + [pltpu.roll(block, 32 * r, 1) for r in range(1, 4)])
        for slot in range(4):
            joined = lanes_joined(turned, slot, slots).reshape(planes // 2, height // 2, columns, 128)
            for z in range(planes // 2):
                for y in range(height // 2):
                    cells[2 * z + slot // 2, 2 * y + slot % 2, :, pl.ds(tile * 128, 128)] = joined[z, y]
    return cells[...].reshape(planes * height * columns, middle).T.astype(low)


def rim_cells(rim_ref, flat, first_cells):
    _, rows, columns, _ = rim_ref.shape
    flat[...] = rim_ref[...].astype(wide).reshape(flat.shape)
    for n, taken in enumerate(tap_cells(flat, 1, rows, columns)):
        first_cells[n] = taken[0]


def tap_pair(window, first_cells, start):
    planes = window.shape[2]
    both = []
    for n in range(2):
        tap = jnp.minimum(start + n, 26)
        depth, row, col = tap // 9, tap // 3 % 3, tap % 3
        which, parity = col * 3 + row, (depth + 1) % 2
        lowest = jnp.where(depth == 0, first_cells[which], window[which, parity, 0])
        below = jnp.where(depth == 0, 0, 1)
        rest = window[which, parity, pl.ds(below, planes - 1)]
        both.append(jnp.concatenate([lowest, rest.reshape(-1, window.shape[4])], axis=0))
    return jnp.concatenate(both, axis=1)


def lower_first_kernel(core_ref, got_ref, window, rim_ref, done_ref, total_ref, cells, flat, first_cells):
    del done_ref
    rim_cells(rim_ref, flat, first_cells)
    side = cotangent_side(got_ref, cells)
    count = total_ref.shape[0]
    for pair in range(count):
        taps = tap_pair(window, first_cells, (core_ref[0] * count + pair) * 2)
        total_ref[pair] = jnp.dot(side, taps, preferred_element_type=wide)


def lower_scratch(grid, middle, window, rim):
    return [
        pltpu.VMEM((*grid, middle), wide),
        pltpu.VMEM((math.prod(rim.shape[:3]), rim.shape[3]), wide),
        pltpu.VMEM((9, *window.shape[3:]), low),
    ]


def lower_first(core, got, window, rim, done, grid):
    middle = 32 * got.shape[0]
    return pl.pallas_call(
        lower_first_kernel,
        out_shape=jax.ShapeDtypeStruct((7, middle, 2 * window.shape[4]), wide),
        in_specs=[scalar, whole, whole, whole, whole],
        out_specs=whole,
        scratch_shapes=lower_scratch(grid, middle, window, rim),
        compiler_params=params,
        cost_estimate=pl.CostEstimate(flops=5 * 10**8, bytes_accessed=5 * 10**6, transcendentals=0),
    )(core, got, window, rim, done)


def lower_kernel(core_ref, total_ref, other_ref, window, rim_ref, sent_ref, cells, flat, first_cells, staged, left):
    rim_cells(rim_ref, flat, first_cells)
    side = cotangent_side(other_ref, cells)
    shards = staged.shape[0]
    below = window.shape[4]
    share = below // shards
    copies = []
    for pair in range(total_ref.shape[0]):
        taps = tap_pair(window, first_cells, (core_ref[0] * total_ref.shape[0] + pair) * 2)
        total = total_ref[pair] + jnp.dot(side, taps, preferred_element_type=wide)
        total = total.T.astype(low)
        for n in range(2):
            for d in range(shards):
                start = n * below + d * share
                staged[d, pl.ds((2 * pair + n) * share, share), :] = total[start : start + share]
        part = pl.ds(2 * pair * share, 2 * share)
        copies.append(pltpu.make_async_copy(staged.at[:, part, :], sent_ref.at[:, part, :], left.at[pair]))
        copies[-1].start()
    for copy in copies:
        copy.wait()


def lower_terms(core, total, other, window, rim, grid):
    shards = other.shape[0]
    pairs, middle, lanes = total.shape
    shape = (shards, pairs * lanes // shards, middle)
    return pl.pallas_call(
        lower_kernel,
        out_shape=pltpu.HBM(shape, low),
        in_specs=[scalar, whole, whole, whole, whole],
        out_specs=anywhere,
        scratch_shapes=lower_scratch(grid, middle, window, rim)
        + [pltpu.VMEM(shape, low), pltpu.SemaphoreType.DMA((pairs,))],
        compiler_params=params,
        cost_estimate=pl.CostEstimate(flops=5 * 10**8, bytes_accessed=5 * 10**6, transcendentals=0),
    )(core, total, other, window, rim)


def upper_kernel(core_ref, volume_ref, cot_ref, mine_ref, theirs_ref, flat, cot_flat, lined, left):
    planes, rows, columns, channels = volume_ref.shape
    depth, height, width, outs = cot_ref.shape
    half = outs // 2
    tiles = channels // 128
    for tile in range(tiles):
        lanes = pl.ds(tile * 128, 128)
        flat[tile] = volume_ref[:, :, :, lanes].astype(wide).reshape(flat.shape[1:])
    cot_wide = cot_ref[...].astype(wide).reshape(cot_flat.shape[0], outs)
    cot_flat[...] = jnp.concatenate([cot_wide, jnp.zeros((cot_flat.shape[0], 128 - outs), wide)], axis=1)
    pieces = [cot_flat[pl.ds(n, depth, stride=height * width), :] for n in range(height * width)]
    left[...] = jnp.concatenate(pieces, axis=0).T[:outs].astype(low)
    core = core_ref[0]
    split = [left[pl.ds(pl.multiple_of(at * half, half), half), :] for at in (core, 1 - core)]
    side = jnp.concatenate(split, axis=0)
    first = lax.broadcasted_iota(jnp.int32, (depth, 128), 0) == 0
    stride = 2 * rows * columns
    for row in range(rows):
        for col in range(columns):
            for tile in range(tiles):
                even = flat[tile, pl.ds(row * columns + col, depth, stride=stride), :]
                odd = flat[tile, pl.ds(stride // 2 + row * columns + col, depth, stride=stride), :]
                before = jnp.where(first, 0.0, pltpu.roll(odd, 1, 0))
                for depth_tap, part in enumerate((before, even, odd)):
                    lined[depth_tap, row, col, :, pl.ds(tile * 128, 128)] = part.astype(low)
    nothing = jnp.zeros((depth, channels), low)
    for tap in range(27):
        depth_tap, row_tap, col_tap = tap // 9, tap // 3 % 3, tap % 3
        taken = []
        for y in range(height):
            for x in range(width):
                row, col = 2 * y + row_tap - 1, 2 * x + col_tap - 1
                taken.append(nothing if row < 0 or col < 0 else lined[depth_tap, row, col])
        term = jnp.dot(side, jnp.concatenate(taken, axis=0), preferred_element_type=wide)
        mine_ref[tap] = term[:half]
        theirs_ref[tap] = term[half:].astype(low)


def upper_terms(core, volume, cot):
    planes, rows, columns, channels = volume.shape
    depth, height, width, outs = cot.shape
    shape = (27, outs // 2, channels)
    return pl.pallas_call(
        upper_kernel,
        out_shape=(jax.ShapeDtypeStruct(shape, wide), jax.ShapeDtypeStruct(shape, low)),
        in_specs=[scalar, whole, whole],
        out_specs=(whole, whole),
        scratch_shapes=[
            pltpu.VMEM((channels // 128, planes * rows * columns, 128), wide),
            pltpu.VMEM((depth * height * width, 128), wide),
            pltpu.VMEM((3, rows, columns, depth, channels), low),
            pltpu.VMEM((outs, depth * height * width), low),
        ],
        compiler_params=params,
        cost_estimate=pl.CostEstimate(flops=5 * 10**8, bytes_accessed=6 * 10**6, transcendentals=0),
    )(core, volume, cot)


def partner(array, axis, by):
    size = lax.axis_size(axis)
    return lax.ppermute(array, axis, [(i, i ^ by) for i in range(size)])


def exchange(blocks, axis):
    return lax.all_to_all(blocks, axis, split_axis=0, concat_axis=0, tiled=True)


def filter_gradient(volume, cotangent, padding):
    return lax.conv_general_dilated(
        volume[None],
        cotangent[None],
        (1, 1, 1),
        padding,
        rhs_dilation=(2, 2, 2),
        dimension_numbers=("CDHWN", "IDHWO", "DHWNC"),
        preferred_element_type=jnp.float32,
    )


def input_gradient(cotangent, filters):
    return lax.conv_general_dilated(
        cotangent[None],
        filters[::-1, ::-1, ::-1],
        (1, 1, 1),
        ((1, 2), (1, 2), (1, 2)),
        lhs_dilation=(2, 2, 2),
        dimension_numbers=("NDHWC", "DHWOI", "NDHWC"),
        preferred_element_type=jnp.float32,
    )[0]


def plain_body(act_64, cot_32, filters_32, act_128):
    shards = lax.axis_size("chan")
    samples = lax.axis_size("sample")
    position = lax.axis_index("chan")
    core = lax.axis_index("sample") % 2
    volume_64 = act_64[0]
    cot_local = cot_32[0]
    depth, height, width, shard_out = cot_local.shape
    planes, rows, columns, middle = volume_64.shape
    below = act_128.shape[4]
    slab = planes // shards
    part = middle // shards

    rim = lax.ppermute(act_128[:, -1:], "chan", [(i, i + 1) for i in range(shards - 1)])

    taps = filters_32.reshape(27, shards, part, shard_out).transpose(1, 0, 3, 2)
    lanes = 128 if taps.size // shards % 256 == 0 else 64
    taps = taps.reshape(shards, 2, -1, lanes)
    own_half = lax.dynamic_index_in_dim(taps, core, 1, keepdims=False)
    cot_rows = jnp.broadcast_to(cot_local.reshape(1, -1, lanes), (shards, cot_local.size // lanes, lanes))
    sent = jnp.concatenate([own_half, cot_rows], axis=1)
    got = exchange(sent, "chan")
    cut = own_half.shape[1]
    got_half = got[:, :cut]
    other_half = partner(got_half, "sample", 1)
    first = jnp.where(core == 0, got_half, other_half)
    second = jnp.where(core == 0, other_half, got_half)
    part_filters = jnp.concatenate([first, second], axis=1)
    part_filters = part_filters.reshape(shards, 3, 3, 3, shard_out, part)
    part_filters = part_filters.transpose(1, 2, 3, 5, 0, 4).reshape(3, 3, 3, part, -1)
    cot_all = got[:, cut:].reshape(shards, depth, height, width, shard_out)
    cot_all = cot_all.transpose(1, 2, 3, 0, 4).reshape(depth, height, width, -1)

    grad_upper = filter_gradient(volume_64, cot_local, ((1, 0),) * 3)
    total_upper = lax.psum(grad_upper, "sample")

    grad_part = input_gradient(cot_all, part_filters)
    own_part = lax.dynamic_slice_in_dim(volume_64, position * part, part, 3)
    cot_part = (grad_part * jnp.where(own_part > 0, 1.0, leak_slope)).astype(low)
    cot_got = exchange(cot_part.reshape(shards, -1, 128), "chan")
    cot_low = cot_got.reshape(shards, slab, rows, columns, part)
    cot_low = cot_low.transpose(1, 2, 3, 0, 4).reshape(slab, rows, columns, middle)

    window = jnp.concatenate([rim, act_128], axis=1)[0]
    grad_lower = filter_gradient(window, cot_low, ((0, 0), (1, 0), (1, 0)))
    blocks = grad_lower.reshape(27, shards, 2, -1, middle).transpose(2, 1, 0, 3, 4)
    mine = lax.dynamic_index_in_dim(blocks, core, 0, keepdims=False)
    theirs = lax.dynamic_index_in_dim(blocks, 1 - core, 0, keepdims=False)
    mine = mine + partner(theirs.astype(low), "sample", 1).astype(jnp.float32)
    got_terms = exchange(mine.astype(low), "chan")
    share = jnp.sum(got_terms.astype(jnp.float32), axis=0)
    if samples > 2:
        pairs = [[2 * i + k for i in range(samples // 2)] for k in range(2)]
        share = lax.psum(share, "sample", axis_index_groups=pairs)
    share = lax.all_gather(
        share, "sample", axis=1, tiled=True, axis_index_groups=[[i, i + 1] for i in range(0, samples, 2)]
    )
    total_lower = share.reshape(3, 3, 3, below // shards, middle)
    return (
        total_upper / samples,
        total_lower / samples,
        cot_low.astype(jnp.float32)[None],
    )


def core_sum(mine, theirs):
    return (mine + partner(theirs, "sample", 1).astype(wide)).astype(low)


def sample_sum(mine, samples):
    core = lax.axis_index("sample") % 2
    total = mine.astype(wide)
    for by in range(2, samples, 2):
        pairs = [(i, (i + by) % samples) for i in range(samples)]
        total = total + lax.ppermute(mine, "sample", pairs).astype(wide)
    total = total * (1.0 / samples)
    other = partner(total, "sample", 1)
    first = jnp.where(core == 0, total, other)
    second = jnp.where(core == 0, other, total)
    return jnp.concatenate([first, second], axis=1)


def body(act_64, cot_32, filters_32, act_128):
    shards = lax.axis_size("chan")
    samples = lax.axis_size("sample")
    middle = act_64.shape[4]
    grid = cot_32.shape[1:4]
    shard_out = cot_32.shape[4]
    below = act_128.shape[4]
    if middle != 32 * shards or shards % 4 or samples != 4 or shard_out != 64 or (2 * grid[2]) != 8:
        return plain_body(act_64, cot_32, filters_32, act_128)
    core = lax.axis_index("sample") % 2
    cores = core[None].astype(jnp.int32)
    position = lax.axis_index("chan")[None].astype(jnp.int32)
    volume_64 = act_64[0]
    cot_local = cot_32[0]
    slab = volume_64.shape[0] // shards

    rim = lax.ppermute(act_128[:, -1:], "chan", [(i, i + 1) for i in range(shards - 1)])
    turned = filters_32.transpose(0, 1, 2, 4, 3).reshape(27, shard_out, middle)
    sent = pack(cores, turned, cot_local.reshape(-1, shard_out), shards)
    got = exchange(sent, "chan")

    own = own_signs(position, volume_64)
    other_act = partner(act_128, "sample", 1)
    halves = upper_terms(cores, volume_64, cot_local)
    window, done = windows(act_128[0])
    other_window, other_done = windows(other_act[0])
    done = done + other_done
    chip_upper = core_sum(*halves)
    beside = (got, own, rim, done, chip_upper)
    got, own, rim, done, chip_upper = lax.optimization_barrier(beside)
    weight = weights(got, shard_out // 2)
    other_weight = partner(weight, "sample", 1)
    first, later = first_terms(cores, got, weight, math.prod(grid))
    cot_sent = spread(first, later, other_weight, own, grid, shards)

    cot_sent, rim, chip_upper = lax.optimization_barrier((cot_sent, rim, chip_upper))
    cot_got = exchange(cot_sent, "chan")
    other_rim = partner(rim, "sample", 1)
    cot_got, other_rim = lax.optimization_barrier((cot_got, other_rim))
    total_upper = sample_sum(chip_upper, samples).reshape(3, 3, 3, shard_out, middle)
    total_upper = total_upper.transpose(0, 1, 2, 4, 3)

    other_cot = partner(cot_got, "sample", 1)
    slab_grid = (slab, *volume_64.shape[1:3])
    own_terms = lower_first(cores, cot_got, window, rim[0], done, slab_grid)
    terms = lower_terms(cores, own_terms, other_cot, other_window, other_rim[0], slab_grid)
    share = jnp.sum(exchange(terms, "chan").astype(wide), axis=0)
    cot_full = unpack(cot_got, slab_grid)
    shares = lax.all_gather(share.astype(low), "sample", axis=0).astype(wide)
    shares = shares.reshape(samples // 2, -1, middle).sum(axis=0) * (1.0 / samples)
    total_lower = shares[: 27 * below // shards].reshape(3, 3, 3, below // shards, middle)
    return (total_upper, total_lower, cot_full[None])


def solution(mesh):
    placed = (
        P("sample", None, None, None, None),
        P("sample", None, None, None, "chan"),
        P(None, None, None, None, "chan"),
        P("sample", "chan", None, None, None),
    )
    return jax.shard_map(
        body,
        mesh=mesh,
        in_specs=placed,
        out_specs=(
            P(None, None, None, None, "chan"),
            P(None, None, None, "chan", None),
            P("sample", "chan", None, None, None),
        ),
        check_vma=False,
    )
```

```python
import functools
import math

import jax
import jax.numpy as jnp
from jax import lax
from jax.experimental import pallas as pl
from jax.experimental.pallas import tpu as pltpu
from jax.sharding import PartitionSpec as P

leak_slope = 0.3
low = jnp.bfloat16
wide = jnp.float32
params = pltpu.CompilerParams(vmem_limit_bytes=20 * 2**20)
whole = pl.BlockSpec(memory_space=pltpu.VMEM)
scalar = pl.BlockSpec(memory_space=pltpu.SMEM)
anywhere = pl.BlockSpec(memory_space=pltpu.HBM)


def slot_plan():
    groups = []
    for col in range(3):
        groups.append([(1, 1, col), (1, 2, col), (2, 1, col), (2, 2, col)])
    for col in range(3):
        groups.append([(2, 0, col), (1, 0, col), (0, 1, col), (0, 2, col)])
    groups.append([None, (0, 0, 2), (0, 0, 1), (0, 0, 0)])
    return groups


def tap_index(tap):
    return (tap[0] * 3 + tap[1]) * 3 + tap[2]


def lane_slot(shape):
    return lax.broadcasted_iota(jnp.int32, shape, len(shape) - 1) // 32


def pack_kernel(core_ref, filters_ref, cot_ref, sent_ref, held, cot_held, staged, arrived, left):
    taps, half, _ = held.shape
    groups = slot_plan()
    start = pl.multiple_of(core_ref[0] * half, half)
    fetch_filters = pltpu.make_async_copy(filters_ref.at[:, pl.ds(start, half), :], held, arrived.at[0])
    fetch_cot = pltpu.make_async_copy(cot_ref, cot_held, arrived.at[1])
    fetch_cot.start()
    fetch_filters.start()
    slots = lane_slot((half, 128))
    shards = staged.shape[0]
    rows = len(groups) * half
    outs = cot_held.shape[1]
    cells = cot_held.shape[0]

    def send(index, first, count):
        part = pl.ds(first, count)
        return pltpu.make_async_copy(staged.at[:, part, :], sent_ref.at[:, part, :], left.at[index])

    fetch_cot.wait()
    turned_cot = cot_held[...].astype(wide).T.astype(low)
    for d in range(shards):
        for b in range(cells // 128):
            staged[d, pl.ds(rows + b * outs, outs), :] = turned_cot[:, b * 128 : (b + 1) * 128]
    copies = [send(0, rows, cells // 128 * outs)]
    copies[0].start()
    fetch_filters.wait()
    for g, group in enumerate(groups):
        for tile in range(shards // 4):
            turned = []
            for tap in group:
                if tap is None:
                    turned.append([jnp.zeros((half, 128), wide)] * 4)
                    continue
                block = held[tap_index(tap), :, pl.ds(tile * 128, 128)].astype(wide)
                turned.append([block] + [pltpu.roll(block, 32 * r, 1) for r in range(1, 4)])
            for m in range(4):
                joined = turned[0][(0 - m) % 4]
                for k in range(1, 4):
                    joined = jnp.where(slots == k, turned[k][(k - m) % 4], joined)
                staged[tile * 4 + m, pl.ds(g * half, half), :] = joined.astype(low)
        copies.append(send(g + 1, g * half, half))
        copies[-1].start()
    for copy in copies:
        copy.wait()


def pack(core, filters, cot, shards):
    taps, outs, middle = filters.shape
    groups = len(slot_plan())
    shape = (shards, groups * (outs // 2) + cot.shape[0] // 128 * outs, 128)
    return pl.pallas_call(
        pack_kernel,
        out_shape=pltpu.HBM(shape, low),
        in_specs=[scalar, anywhere, anywhere],
        out_specs=anywhere,
        scratch_shapes=[
            pltpu.VMEM((taps, outs // 2, middle), low),
            pltpu.VMEM(cot.shape, low),
            pltpu.VMEM(shape, low),
            pltpu.SemaphoreType.DMA((2,)),
            pltpu.SemaphoreType.DMA((groups + 1,)),
        ],
        compiler_params=params,
        cost_estimate=pl.CostEstimate(flops=10**6, bytes_accessed=3 * 10**6, transcendentals=0),
    )(core, pltpu.with_memory_space_constraint(filters, pltpu.HBM), pltpu.with_memory_space_constraint(cot, pltpu.HBM))


def sign_kernel(position_ref, volume_ref, own_ref):
    part = position_ref[0] % 4
    rows = own_ref.shape[0]
    slots = lane_slot((rows, 128))
    joined = None
    for depth_par in range(2):
        for row_par in range(2):
            slot = depth_par * 2 + row_par
            block = volume_ref[:, depth_par, :, row_par].astype(wide).reshape(rows, 128)
            block = pltpu.roll(block, (slot - part + 4) % 4 * 32, 1)
            joined = block if joined is None else jnp.where(slots == slot, block, joined)
    own_ref[...] = joined.astype(low)


def own_signs(position, volume):
    planes, rows, columns, channels = volume.shape
    split = volume.reshape(planes // 2, 2, rows // 2, 2, columns, channels)
    count = planes * rows * columns // 4
    return pl.pallas_call(
        sign_kernel,
        out_shape=jax.ShapeDtypeStruct((count, 128), low),
        grid_spec=pltpu.PrefetchScalarGridSpec(
            num_scalar_prefetch=1,
            grid=(1,),
            in_specs=[
                pl.BlockSpec(
                    (planes // 2, 2, rows // 2, 2, columns, 128),
                    lambda i, at: (0, 0, 0, 0, 0, at[0] // 4),
                )
            ],
            out_specs=pl.BlockSpec((count, 128), lambda i, at: (0, 0)),
        ),
        compiler_params=params,
        cost_estimate=pl.CostEstimate(flops=10**6, bytes_accessed=4 * 10**6, transcendentals=0),
    )(position, split)


def weight_kernel(got_ref, weight_ref):
    shards = got_ref.shape[0]
    groups = len(slot_plan())
    half = weight_ref.shape[0] // shards
    for c in range(shards):
        for g in range(groups):
            weight_ref[pl.ds(c * half, half), pl.ds(g * 128, 128)] = got_ref[c, pl.ds(g * half, half), :]


def weights(got, half):
    shards = got.shape[0]
    groups = len(slot_plan())
    return pl.pallas_call(
        weight_kernel,
        out_shape=jax.ShapeDtypeStruct((shards * half, groups * 128), low),
        grid=(1,),
        in_specs=[pl.BlockSpec((shards, groups * half, 128), lambda i: (0, 0, 0))],
        out_specs=whole,
        compiler_params=params,
        cost_estimate=pl.CostEstimate(flops=10**5, bytes_accessed=10**6, transcendentals=0),
    )(got)


def first_kernel(core_ref, got_ref, weight_ref, products_ref, later_ref, turned):
    shards = got_ref.shape[0]
    half = later_ref.shape[0] // shards
    groups = len(slot_plan())
    core = core_ref[0]
    for c in range(shards):
        span = pl.ds(c * half, half)
        for b in range(later_ref.shape[1] // 128):
            lanes = pl.ds(b * 128, 128)
            first = groups * half + b * 2 * half
            turned[span, lanes] = got_ref[c, pl.ds(pl.multiple_of(first + core * half, half), half), :]
            later_ref[span, lanes] = got_ref[c, pl.ds(pl.multiple_of(first + (1 - core) * half, half), half), :]
    products_ref[...] = lax.dot_general(
        turned[...], weight_ref[...], (((0,), (0,)), ((), ())), preferred_element_type=wide
    )


def spread_kernel(grid, first_ref, later_ref, other_ref, own_ref, sent_ref, products, joined):
    depth, height, width = grid
    cells = depth * height * width
    shards = sent_ref.shape[0]
    products[pl.ds(0, cells), :] = first_ref[...] + lax.dot_general(
        later_ref[...], other_ref[...], (((0,), (0,)), ((), ())), preferred_element_type=wide
    )
    products[pl.ds(cells, products.shape[0] - cells), :] = jnp.zeros(
        (products.shape[0] - cells, products.shape[1]), wide
    )
    chunk = cells // shards
    place = lax.broadcasted_iota(jnp.int32, (chunk, 128), 0)
    slots = lane_slot((chunk, 128))
    last_col = place % width == width - 1
    last_row = place // width % height == height - 1
    row_step, plane_step = width, width * height
    for n in range(shards):
        sums = [None, None]
        for col in range(3):
            shift = 1 if col == 0 else 0
            base = n * chunk + shift

            def piece(group, offset):
                return products[pl.ds(base + offset, chunk), pl.ds(group * 128, 128)]

            part = piece(col, 0)
            part = part + jnp.where(slots >= 2, piece(3 + col, plane_step), 0.0)
            by_row = piece(3 + col, row_step)
            moved = pltpu.roll(by_row, 96, 1)
            corner = piece(6, plane_step + row_step)
            if col > 0:
                corner = pltpu.roll(corner, 32 * col, 1)
            rows = jnp.where(slots == 1, by_row, jnp.where(slots == 3, moved + corner, 0.0))
            part = part + jnp.where(last_row, 0.0, rows)
            if shift:
                part = jnp.where(last_col, 0.0, part)
            to = 0 if col == 1 else 1
            sums[to] = part if sums[to] is None else sums[to] + part
        joined[pl.ds(0, chunk, stride=2), :] = sums[0]
        joined[pl.ds(1, chunk, stride=2), :] = sums[1]
        span = pl.ds(n * 2 * chunk, 2 * chunk)
        slope = jnp.where(own_ref[span, :].astype(wide) > 0, 1.0, leak_slope)
        sent_ref[n] = (joined[...] * slope).astype(low)


def first_terms(core, got, weight, cells):
    rows, lanes = weight.shape
    return pl.pallas_call(
        first_kernel,
        out_shape=(jax.ShapeDtypeStruct((cells, lanes), wide), jax.ShapeDtypeStruct((rows, cells), low)),
        in_specs=[scalar, whole, whole],
        out_specs=(whole, whole),
        scratch_shapes=[pltpu.VMEM((rows, cells), low)],
        compiler_params=params,
        cost_estimate=pl.CostEstimate(flops=10**8, bytes_accessed=3 * 10**6, transcendentals=0),
    )(core, got, weight)


def spread(first, later, other, own, grid, shards):
    cells, lanes = first.shape
    return pl.pallas_call(
        functools.partial(spread_kernel, grid),
        out_shape=jax.ShapeDtypeStruct((shards, 2 * cells // shards, 128), low),
        in_specs=[whole, whole, whole, whole],
        out_specs=whole,
        scratch_shapes=[
            pltpu.VMEM((cells + 32, lanes), wide),
            pltpu.VMEM((2 * cells // shards, 128), wide),
        ],
        compiler_params=params,
        cost_estimate=pl.CostEstimate(flops=5 * 10**8, bytes_accessed=3 * 10**6, transcendentals=0),
    )(first, later, other, own)


def unpack_kernel(got_ref, wide_ref):
    shards, rows, _ = got_ref.shape
    planes, height, columns, _ = wide_ref.shape
    slots = lane_slot((rows, 128))
    for tile in range(shards // 4):
        turned = []
        for m in range(4):
            block = got_ref[tile * 4 + m].astype(wide)
            turned.append([block] + [pltpu.roll(block, 32 * r, 1) for r in range(1, 4)])
        for slot in range(4):
            joined = turned[0][(0 - slot) % 4]
            for m in range(1, 4):
                joined = jnp.where(slots == m, turned[m][(m - slot) % 4], joined)
            joined = joined.reshape(planes // 2, height // 2, columns, 128)
            lanes = pl.ds(tile * 128, 128)
            for z in range(planes // 2):
                for y in range(height // 2):
                    at = (2 * z + slot // 2, 2 * y + slot % 2)
                    wide_ref[at[0], at[1], :, lanes] = joined[z, y]


def unpack(got, grid):
    shape = (*grid, got.shape[0] * 32)
    return pl.pallas_call(
        unpack_kernel,
        out_shape=jax.ShapeDtypeStruct(shape, wide),
        in_specs=[whole],
        out_specs=whole,
        compiler_params=params,
        cost_estimate=pl.CostEstimate(flops=10**6, bytes_accessed=2 * 10**6, transcendentals=0),
    )(got)


def tap_cells(flat, planes, rows, columns):
    channels = flat.shape[1]
    half = columns // 2
    count = planes * rows * half
    first = lax.broadcasted_iota(jnp.int32, (count, channels), 0) % half == 0
    even = flat[pl.ds(0, count, stride=2), :]
    odd = flat[pl.ds(1, count, stride=2), :]
    before = jnp.where(first, 0.0, pltpu.roll(odd, 1, 0))
    cells = []
    for part in (before, even, odd):
        part = part.reshape(planes, rows // 2, 2, half, channels)
        on_even, on_odd = part[:, :, 0], part[:, :, 1]
        ahead = jnp.concatenate([jnp.zeros_like(on_odd[:, :1]), on_odd[:, :-1]], axis=1)
        for taken in (ahead, on_even, on_odd):
            cells.append(taken.reshape(planes, rows // 2 * half, channels).astype(low))
    return cells


def window_kernel(volume_ref, window_ref, done_ref, flat):
    done_ref[...] = jnp.zeros_like(done_ref)
    planes, rows, columns, _ = volume_ref.shape
    flat[...] = volume_ref[...].astype(wide).reshape(flat.shape)
    for n, taken in enumerate(tap_cells(flat, planes, rows, columns)):
        for plane in range(planes):
            window_ref[n, plane % 2, plane // 2] = taken[plane]


def windows(volume):
    planes, rows, columns, channels = volume.shape
    shape = (9, 2, planes // 2, rows * columns // 4, channels)
    return pl.pallas_call(
        window_kernel,
        out_shape=(jax.ShapeDtypeStruct(shape, low), jax.ShapeDtypeStruct((8, 128), wide)),
        in_specs=[whole],
        out_specs=(whole, whole),
        scratch_shapes=[pltpu.VMEM((planes * rows * columns, channels), wide)],
        compiler_params=params,
        cost_estimate=pl.CostEstimate(flops=10**6, bytes_accessed=4 * 10**6, transcendentals=0),
    )(volume)


def lanes_joined(blocks, slot, slots):
    joined = blocks[0][(0 - slot) % 4]
    for m in range(1, 4):
        joined = jnp.where(slots == m, blocks[m][(m - slot) % 4], joined)
    return joined


def cotangent_side(source_ref, cells):
    shards, rows, _ = source_ref.shape
    planes, height, columns, middle = cells.shape
    slots = lane_slot((rows, 128))
    for tile in range(shards // 4):
        turned = []
        for m in range(4):
            block = source_ref[tile * 4 + m].astype(wide)
            turned.append([block] + [pltpu.roll(block, 32 * r, 1) for r in range(1, 4)])
        for slot in range(4):
            joined = lanes_joined(turned, slot, slots).reshape(planes // 2, height // 2, columns, 128)
            for z in range(planes // 2):
                for y in range(height // 2):
                    cells[2 * z + slot // 2, 2 * y + slot % 2, :, pl.ds(tile * 128, 128)] = joined[z, y]
    return cells[...].reshape(planes * height * columns, middle).T.astype(low)


def rim_cells(rim_ref, flat, first_cells):
    _, rows, columns, _ = rim_ref.shape
    flat[...] = rim_ref[...].astype(wide).reshape(flat.shape)
    for n, taken in enumerate(tap_cells(flat, 1, rows, columns)):
        first_cells[n] = taken[0]


def tap_pair(window, first_cells, core, pair):
    planes = window.shape[2]
    both = []
    for n in (2 * pair, 2 * pair + 1):
        tap = core * 14 + n if n < 13 else 13
        depth, row, col = tap // 9, tap // 3 % 3, tap % 3
        which, parity = col * 3 + row, (depth + 1) % 2
        lowest = jnp.where(depth == 0, first_cells[which], window[which, parity, 0])
        below = jnp.where(depth == 0, 0, 1)
        rest = window[which, parity, pl.ds(below, planes - 1)]
        both.append(jnp.concatenate([lowest, rest.reshape(-1, window.shape[4])], axis=0))
    return jnp.concatenate(both, axis=1)


def lower_first_kernel(core_ref, got_ref, window, rim_ref, done_ref, total_ref, cells, flat, first_cells):
    del done_ref
    rim_cells(rim_ref, flat, first_cells)
    side = cotangent_side(got_ref, cells)
    count = total_ref.shape[0]
    for pair in range(count):
        taps = tap_pair(window, first_cells, core_ref[0], pair)
        total_ref[pair] = jnp.dot(side, taps, preferred_element_type=wide)


def lower_scratch(grid, middle, window, rim):
    return [
        pltpu.VMEM((*grid, middle), wide),
        pltpu.VMEM((math.prod(rim.shape[:3]), rim.shape[3]), wide),
        pltpu.VMEM((9, *window.shape[3:]), low),
    ]


def lower_first(core, got, window, rim, done, grid):
    middle = 32 * got.shape[0]
    return pl.pallas_call(
        lower_first_kernel,
        out_shape=jax.ShapeDtypeStruct((7, middle, 2 * window.shape[4]), wide),
        in_specs=[scalar, whole, whole, whole, whole],
        out_specs=whole,
        scratch_shapes=lower_scratch(grid, middle, window, rim),
        compiler_params=params,
        cost_estimate=pl.CostEstimate(flops=5 * 10**8, bytes_accessed=5 * 10**6, transcendentals=0),
    )(core, got, window, rim, done)


def lower_kernel(core_ref, total_ref, other_ref, window, rim_ref, sent_ref, cells, flat, first_cells, staged, left):
    rim_cells(rim_ref, flat, first_cells)
    side = cotangent_side(other_ref, cells)
    shards = staged.shape[0]
    below = window.shape[4]
    share = below // shards
    copies = []
    for pair in range(total_ref.shape[0]):
        taps = tap_pair(window, first_cells, core_ref[0], pair)
        total = total_ref[pair] + jnp.dot(side, taps, preferred_element_type=wide)
        total = total.T.astype(low)
        count = 0
        for n in (2 * pair, 2 * pair + 1):
            rows = total[n % 2 * below : (n % 2 + 1) * below]
            halves = [rows[:, :128], rows[:, 128:]]
            if n == 13:
                halves = [jnp.where(core_ref[0] == 0, *halves)]
            for half in halves:
                start = 2 * pair * 2 * share + count * share
                for d in range(shards):
                    staged[d, pl.ds(start, share), :] = half[d * share : (d + 1) * share]
                count += 1
        part = pl.ds(4 * pair * share, count * share)
        copies.append(pltpu.make_async_copy(staged.at[:, part, :], sent_ref.at[:, part, :], left.at[pair]))
        copies[-1].start()
    for copy in copies:
        copy.wait()


def lower_terms(core, total, other, window, rim, grid):
    shards = other.shape[0]
    pairs, middle, _ = total.shape
    shape = (shards, 27 * window.shape[4] // shards, 128)
    return pl.pallas_call(
        lower_kernel,
        out_shape=pltpu.HBM(shape, low),
        in_specs=[scalar, whole, whole, whole, whole],
        out_specs=anywhere,
        scratch_shapes=lower_scratch(grid, middle, window, rim)
        + [pltpu.VMEM(shape, low), pltpu.SemaphoreType.DMA((pairs,))],
        compiler_params=params,
        cost_estimate=pl.CostEstimate(flops=5 * 10**8, bytes_accessed=5 * 10**6, transcendentals=0),
    )(core, total, other, window, rim)


def total_kernel(shares_ref, total_ref, *, scale):
    share = total_ref.shape[1]
    for core in range(2):
        total = shares_ref[core].astype(wide)
        for by in range(2, shares_ref.shape[0], 2):
            total = total + shares_ref[core + by].astype(wide)
        total = total * scale
        for n in range(13):
            for half in range(2):
                start = (2 * n + half) * share
                total_ref[core * 14 + n, :, pl.ds(half * 128, 128)] = total[start : start + share]
        total_ref[13, :, pl.ds(core * 128, 128)] = total[26 * share : 27 * share]


def total_terms(shares, scale):
    return pl.pallas_call(
        functools.partial(total_kernel, scale=scale),
        out_shape=jax.ShapeDtypeStruct((27, shares.shape[1] // 27, 2 * shares.shape[2]), wide),
        in_specs=[whole],
        out_specs=whole,
        compiler_params=params,
        cost_estimate=pl.CostEstimate(flops=10**6, bytes_accessed=10**6, transcendentals=0),
    )(shares)


def upper_kernel(core_ref, volume_ref, cot_ref, mine_ref, theirs_ref, flat, cot_flat, lined, left):
    planes, rows, columns, channels = volume_ref.shape
    depth, height, width, outs = cot_ref.shape
    half = outs // 2
    tiles = channels // 128
    for tile in range(tiles):
        lanes = pl.ds(tile * 128, 128)
        flat[tile] = volume_ref[:, :, :, lanes].astype(wide).reshape(flat.shape[1:])
    cot_wide = cot_ref[...].astype(wide).reshape(cot_flat.shape[0], outs)
    cot_flat[...] = jnp.concatenate([cot_wide, jnp.zeros((cot_flat.shape[0], 128 - outs), wide)], axis=1)
    pieces = [cot_flat[pl.ds(n, depth, stride=height * width), :] for n in range(height * width)]
    left[...] = jnp.concatenate(pieces, axis=0).T[:outs].astype(low)
    core = core_ref[0]
    split = [left[pl.ds(pl.multiple_of(at * half, half), half), :] for at in (core, 1 - core)]
    side = jnp.concatenate(split, axis=0)
    first = lax.broadcasted_iota(jnp.int32, (depth, 128), 0) == 0
    stride = 2 * rows * columns
    for row in range(rows):
        for col in range(columns):
            for tile in range(tiles):
                even = flat[tile, pl.ds(row * columns + col, depth, stride=stride), :]
                odd = flat[tile, pl.ds(stride // 2 + row * columns + col, depth, stride=stride), :]
                before = jnp.where(first, 0.0, pltpu.roll(odd, 1, 0))
                for depth_tap, part in enumerate((before, even, odd)):
                    lined[depth_tap, row, col, :, pl.ds(tile * 128, 128)] = part.astype(low)
    nothing = jnp.zeros((depth, channels), low)
    for tap in range(27):
        depth_tap, row_tap, col_tap = tap // 9, tap // 3 % 3, tap % 3
        taken = []
        for y in range(height):
            for x in range(width):
                row, col = 2 * y + row_tap - 1, 2 * x + col_tap - 1
                taken.append(nothing if row < 0 or col < 0 else lined[depth_tap, row, col])
        term = jnp.dot(side, jnp.concatenate(taken, axis=0), preferred_element_type=wide)
        mine_ref[tap] = term[:half]
        theirs_ref[tap] = term[half:].astype(low)


def upper_terms(core, volume, cot):
    planes, rows, columns, channels = volume.shape
    depth, height, width, outs = cot.shape
    shape = (27, outs // 2, channels)
    return pl.pallas_call(
        upper_kernel,
        out_shape=(jax.ShapeDtypeStruct(shape, wide), jax.ShapeDtypeStruct(shape, low)),
        in_specs=[scalar, whole, whole],
        out_specs=(whole, whole),
        scratch_shapes=[
            pltpu.VMEM((channels // 128, planes * rows * columns, 128), wide),
            pltpu.VMEM((depth * height * width, 128), wide),
            pltpu.VMEM((3, rows, columns, depth, channels), low),
            pltpu.VMEM((outs, depth * height * width), low),
        ],
        compiler_params=params,
        cost_estimate=pl.CostEstimate(flops=5 * 10**8, bytes_accessed=6 * 10**6, transcendentals=0),
    )(core, volume, cot)


def partner(array, axis, by):
    size = lax.axis_size(axis)
    return lax.ppermute(array, axis, [(i, i ^ by) for i in range(size)])


def exchange(blocks, axis):
    return lax.all_to_all(blocks, axis, split_axis=0, concat_axis=0, tiled=True)


def filter_gradient(volume, cotangent, padding):
    return lax.conv_general_dilated(
        volume[None],
        cotangent[None],
        (1, 1, 1),
        padding,
        rhs_dilation=(2, 2, 2),
        dimension_numbers=("CDHWN", "IDHWO", "DHWNC"),
        preferred_element_type=jnp.float32,
    )


def input_gradient(cotangent, filters):
    return lax.conv_general_dilated(
        cotangent[None],
        filters[::-1, ::-1, ::-1],
        (1, 1, 1),
        ((1, 2), (1, 2), (1, 2)),
        lhs_dilation=(2, 2, 2),
        dimension_numbers=("NDHWC", "DHWOI", "NDHWC"),
        preferred_element_type=jnp.float32,
    )[0]


def plain_body(act_64, cot_32, filters_32, act_128):
    shards = lax.axis_size("chan")
    samples = lax.axis_size("sample")
    position = lax.axis_index("chan")
    core = lax.axis_index("sample") % 2
    volume_64 = act_64[0]
    cot_local = cot_32[0]
    depth, height, width, shard_out = cot_local.shape
    planes, rows, columns, middle = volume_64.shape
    below = act_128.shape[4]
    slab = planes // shards
    part = middle // shards

    rim = lax.ppermute(act_128[:, -1:], "chan", [(i, i + 1) for i in range(shards - 1)])

    taps = filters_32.reshape(27, shards, part, shard_out).transpose(1, 0, 3, 2)
    lanes = 128 if taps.size // shards % 256 == 0 else 64
    taps = taps.reshape(shards, 2, -1, lanes)
    own_half = lax.dynamic_index_in_dim(taps, core, 1, keepdims=False)
    cot_rows = jnp.broadcast_to(cot_local.reshape(1, -1, lanes), (shards, cot_local.size // lanes, lanes))
    sent = jnp.concatenate([own_half, cot_rows], axis=1)
    got = exchange(sent, "chan")
    cut = own_half.shape[1]
    got_half = got[:, :cut]
    other_half = partner(got_half, "sample", 1)
    first = jnp.where(core == 0, got_half, other_half)
    second = jnp.where(core == 0, other_half, got_half)
    part_filters = jnp.concatenate([first, second], axis=1)
    part_filters = part_filters.reshape(shards, 3, 3, 3, shard_out, part)
    part_filters = part_filters.transpose(1, 2, 3, 5, 0, 4).reshape(3, 3, 3, part, -1)
    cot_all = got[:, cut:].reshape(shards, depth, height, width, shard_out)
    cot_all = cot_all.transpose(1, 2, 3, 0, 4).reshape(depth, height, width, -1)

    grad_upper = filter_gradient(volume_64, cot_local, ((1, 0),) * 3)
    total_upper = lax.psum(grad_upper, "sample")

    grad_part = input_gradient(cot_all, part_filters)
    own_part = lax.dynamic_slice_in_dim(volume_64, position * part, part, 3)
    cot_part = (grad_part * jnp.where(own_part > 0, 1.0, leak_slope)).astype(low)
    cot_got = exchange(cot_part.reshape(shards, -1, 128), "chan")
    cot_low = cot_got.reshape(shards, slab, rows, columns, part)
    cot_low = cot_low.transpose(1, 2, 3, 0, 4).reshape(slab, rows, columns, middle)

    window = jnp.concatenate([rim, act_128], axis=1)[0]
    grad_lower = filter_gradient(window, cot_low, ((0, 0), (1, 0), (1, 0)))
    blocks = grad_lower.reshape(27, shards, 2, -1, middle).transpose(2, 1, 0, 3, 4)
    mine = lax.dynamic_index_in_dim(blocks, core, 0, keepdims=False)
    theirs = lax.dynamic_index_in_dim(blocks, 1 - core, 0, keepdims=False)
    mine = mine + partner(theirs.astype(low), "sample", 1).astype(jnp.float32)
    got_terms = exchange(mine.astype(low), "chan")
    share = jnp.sum(got_terms.astype(jnp.float32), axis=0)
    if samples > 2:
        pairs = [[2 * i + k for i in range(samples // 2)] for k in range(2)]
        share = lax.psum(share, "sample", axis_index_groups=pairs)
    share = lax.all_gather(
        share, "sample", axis=1, tiled=True, axis_index_groups=[[i, i + 1] for i in range(0, samples, 2)]
    )
    total_lower = share.reshape(3, 3, 3, below // shards, middle)
    return (
        total_upper / samples,
        total_lower / samples,
        cot_low.astype(jnp.float32)[None],
    )


def core_sum(mine, theirs):
    return (mine + partner(theirs, "sample", 1).astype(wide)).astype(low)


def sample_sum(mine, samples):
    core = lax.axis_index("sample") % 2
    total = mine.astype(wide)
    for by in range(2, samples, 2):
        pairs = [(i, (i + by) % samples) for i in range(samples)]
        total = total + lax.ppermute(mine, "sample", pairs).astype(wide)
    total = total * (1.0 / samples)
    other = partner(total, "sample", 1)
    first = jnp.where(core == 0, total, other)
    second = jnp.where(core == 0, other, total)
    return jnp.concatenate([first, second], axis=1)


def body(act_64, cot_32, filters_32, act_128):
    shards = lax.axis_size("chan")
    samples = lax.axis_size("sample")
    middle = act_64.shape[4]
    grid = cot_32.shape[1:4]
    shard_out = cot_32.shape[4]
    below = act_128.shape[4]
    if middle != 32 * shards or shards % 4 or samples != 4 or shard_out != 64 or (2 * grid[2]) != 8:
        return plain_body(act_64, cot_32, filters_32, act_128)
    core = lax.axis_index("sample") % 2
    cores = core[None].astype(jnp.int32)
    position = lax.axis_index("chan")[None].astype(jnp.int32)
    volume_64 = act_64[0]
    cot_local = cot_32[0]
    slab = volume_64.shape[0] // shards

    rim = lax.ppermute(act_128[:, -1:], "chan", [(i, i + 1) for i in range(shards - 1)])
    turned = filters_32.transpose(0, 1, 2, 4, 3).reshape(27, shard_out, middle)
    sent = pack(cores, turned, cot_local.reshape(-1, shard_out), shards)
    got = exchange(sent, "chan")

    own = own_signs(position, volume_64)
    other_act = partner(act_128, "sample", 1)
    halves = upper_terms(cores, volume_64, cot_local)
    window, done = windows(act_128[0])
    other_window, other_done = windows(other_act[0])
    done = done + other_done
    chip_upper = core_sum(*halves)
    beside = (got, own, rim, done, chip_upper)
    got, own, rim, done, chip_upper = lax.optimization_barrier(beside)
    weight = weights(got, shard_out // 2)
    other_weight = partner(weight, "sample", 1)
    first, later = first_terms(cores, got, weight, math.prod(grid))
    cot_sent = spread(first, later, other_weight, own, grid, shards)

    cot_sent, rim, chip_upper = lax.optimization_barrier((cot_sent, rim, chip_upper))
    cot_got = exchange(cot_sent, "chan")
    other_rim = partner(rim, "sample", 1)
    cot_got, other_rim = lax.optimization_barrier((cot_got, other_rim))
    total_upper = sample_sum(chip_upper, samples).reshape(3, 3, 3, shard_out, middle)
    total_upper = total_upper.transpose(0, 1, 2, 4, 3)

    other_cot = partner(cot_got, "sample", 1)
    slab_grid = (slab, *volume_64.shape[1:3])
    own_terms = lower_first(cores, cot_got, window, rim[0], done, slab_grid)
    terms = lower_terms(cores, own_terms, other_cot, other_window, other_rim[0], slab_grid)
    share = jnp.sum(exchange(terms, "chan").astype(wide), axis=0)
    cot_full = unpack(cot_got, slab_grid)
    shares = lax.all_gather(share.astype(low), "sample", axis=0)
    total_lower = total_terms(shares, 1.0 / samples).reshape(3, 3, 3, below // shards, middle)
    return (total_upper, total_lower, cot_full[None])


def solution(mesh):
    placed = (
        P("sample", None, None, None, None),
        P("sample", None, None, None, "chan"),
        P(None, None, None, None, "chan"),
        P("sample", "chan", None, None, None),
    )
    return jax.shard_map(
        body,
        mesh=mesh,
        in_specs=placed,
        out_specs=(
            P(None, None, None, None, "chan"),
            P(None, None, None, "chan", None),
            P("sample", "chan", None, None, None),
        ),
        check_vma=False,
    )
```

```python
import functools
import math

import jax
import jax.numpy as jnp
from jax import lax
from jax.experimental import pallas as pl
from jax.experimental.pallas import tpu as pltpu
from jax.sharding import PartitionSpec as P

leak_slope = 0.3
low = jnp.bfloat16
wide = jnp.float32
params = pltpu.CompilerParams(vmem_limit_bytes=20 * 2**20)
whole = pl.BlockSpec(memory_space=pltpu.VMEM)
scalar = pl.BlockSpec(memory_space=pltpu.SMEM)
anywhere = pl.BlockSpec(memory_space=pltpu.HBM)


def slot_plan():
    groups = []
    for col in range(3):
        groups.append([(1, 1, col), (1, 2, col), (2, 1, col), (2, 2, col)])
    for col in range(3):
        groups.append([(2, 0, col), (1, 0, col), (0, 1, col), (0, 2, col)])
    groups.append([None, (0, 0, 2), (0, 0, 1), (0, 0, 0)])
    return groups


def tap_index(tap):
    return (tap[0] * 3 + tap[1]) * 3 + tap[2]


def lane_slot(shape):
    return lax.broadcasted_iota(jnp.int32, shape, len(shape) - 1) // 32


def pack_kernel(core_ref, filters_ref, cot_ref, sent_ref, held, cot_held, staged, arrived, left):
    taps, half, _ = held.shape
    groups = slot_plan()
    start = pl.multiple_of(core_ref[0] * half, half)
    fetch_filters = pltpu.make_async_copy(filters_ref.at[:, pl.ds(start, half), :], held, arrived.at[0])
    fetch_cot = pltpu.make_async_copy(cot_ref, cot_held, arrived.at[1])
    fetch_cot.start()
    fetch_filters.start()
    slots = lane_slot((half, 128))
    shards = staged.shape[0]
    rows = len(groups) * half
    outs = cot_held.shape[1]
    cells = cot_held.shape[0]

    def send(index, first, count):
        part = pl.ds(first, count)
        return pltpu.make_async_copy(staged.at[:, part, :], sent_ref.at[:, part, :], left.at[index])

    fetch_cot.wait()
    turned_cot = cot_held[...].astype(wide).T.astype(low)
    for d in range(shards):
        for b in range(cells // 128):
            staged[d, pl.ds(rows + b * outs, outs), :] = turned_cot[:, b * 128 : (b + 1) * 128]
    copies = [send(0, rows, cells // 128 * outs)]
    copies[0].start()
    fetch_filters.wait()
    for g, group in enumerate(groups):
        for tile in range(shards // 4):
            turned = []
            for tap in group:
                if tap is None:
                    turned.append([jnp.zeros((half, 128), wide)] * 4)
                    continue
                block = held[tap_index(tap), :, pl.ds(tile * 128, 128)].astype(wide)
                turned.append([block] + [pltpu.roll(block, 32 * r, 1) for r in range(1, 4)])
            for m in range(4):
                joined = turned[0][(0 - m) % 4]
                for k in range(1, 4):
                    joined = jnp.where(slots == k, turned[k][(k - m) % 4], joined)
                staged[tile * 4 + m, pl.ds(g * half, half), :] = joined.astype(low)
        copies.append(send(g + 1, g * half, half))
        copies[-1].start()
    for copy in copies:
        copy.wait()


def pack(core, filters, cot, shards):
    taps, outs, middle = filters.shape
    groups = len(slot_plan())
    shape = (shards, groups * (outs // 2) + cot.shape[0] // 128 * outs, 128)
    return pl.pallas_call(
        pack_kernel,
        out_shape=pltpu.HBM(shape, low),
        in_specs=[scalar, anywhere, anywhere],
        out_specs=anywhere,
        scratch_shapes=[
            pltpu.VMEM((taps, outs // 2, middle), low),
            pltpu.VMEM(cot.shape, low),
            pltpu.VMEM(shape, low),
            pltpu.SemaphoreType.DMA((2,)),
            pltpu.SemaphoreType.DMA((groups + 1,)),
        ],
        compiler_params=params,
        cost_estimate=pl.CostEstimate(flops=10**6, bytes_accessed=3 * 10**6, transcendentals=0),
    )(core, pltpu.with_memory_space_constraint(filters, pltpu.HBM), pltpu.with_memory_space_constraint(cot, pltpu.HBM))


def sign_kernel(position_ref, volume_ref, own_ref):
    part = position_ref[0] % 4
    rows = own_ref.shape[0]
    slots = lane_slot((rows, 128))
    joined = None
    for depth_par in range(2):
        for row_par in range(2):
            slot = depth_par * 2 + row_par
            block = volume_ref[:, depth_par, :, row_par].astype(wide).reshape(rows, 128)
            block = pltpu.roll(block, (slot - part + 4) % 4 * 32, 1)
            joined = block if joined is None else jnp.where(slots == slot, block, joined)
    own_ref[...] = joined.astype(low)


def own_signs(position, volume):
    planes, rows, columns, channels = volume.shape
    split = volume.reshape(planes // 2, 2, rows // 2, 2, columns, channels)
    count = planes * rows * columns // 4
    return pl.pallas_call(
        sign_kernel,
        out_shape=jax.ShapeDtypeStruct((count, 128), low),
        grid_spec=pltpu.PrefetchScalarGridSpec(
            num_scalar_prefetch=1,
            grid=(1,),
            in_specs=[
                pl.BlockSpec(
                    (planes // 2, 2, rows // 2, 2, columns, 128),
                    lambda i, at: (0, 0, 0, 0, 0, at[0] // 4),
                )
            ],
            out_specs=pl.BlockSpec((count, 128), lambda i, at: (0, 0)),
        ),
        compiler_params=params,
        cost_estimate=pl.CostEstimate(flops=10**6, bytes_accessed=4 * 10**6, transcendentals=0),
    )(position, split)


def weight_kernel(got_ref, weight_ref):
    shards = got_ref.shape[0]
    groups = len(slot_plan())
    half = weight_ref.shape[0] // shards
    for c in range(shards):
        for g in range(groups):
            weight_ref[pl.ds(c * half, half), pl.ds(g * 128, 128)] = got_ref[c, pl.ds(g * half, half), :]


def weights(got, half):
    shards = got.shape[0]
    groups = len(slot_plan())
    return pl.pallas_call(
        weight_kernel,
        out_shape=jax.ShapeDtypeStruct((shards * half, groups * 128), low),
        grid=(1,),
        in_specs=[pl.BlockSpec((shards, groups * half, 128), lambda i: (0, 0, 0))],
        out_specs=whole,
        compiler_params=params,
        cost_estimate=pl.CostEstimate(flops=10**5, bytes_accessed=10**6, transcendentals=0),
    )(got)


def first_kernel(core_ref, got_ref, weight_ref, products_ref, later_ref, turned):
    shards = got_ref.shape[0]
    half = later_ref.shape[0] // shards
    groups = len(slot_plan())
    core = core_ref[0]
    for c in range(shards):
        span = pl.ds(c * half, half)
        for b in range(later_ref.shape[1] // 128):
            lanes = pl.ds(b * 128, 128)
            first = groups * half + b * 2 * half
            turned[span, lanes] = got_ref[c, pl.ds(pl.multiple_of(first + core * half, half), half), :]
            later_ref[span, lanes] = got_ref[c, pl.ds(pl.multiple_of(first + (1 - core) * half, half), half), :]
    products_ref[...] = lax.dot_general(
        turned[...], weight_ref[...], (((0,), (0,)), ((), ())), preferred_element_type=wide
    )


def spread_kernel(grid, first_ref, later_ref, other_ref, own_ref, sent_ref, products, joined):
    depth, height, width = grid
    cells = depth * height * width
    shards = sent_ref.shape[0]
    products[pl.ds(0, cells), :] = first_ref[...] + lax.dot_general(
        later_ref[...], other_ref[...], (((0,), (0,)), ((), ())), preferred_element_type=wide
    )
    products[pl.ds(cells, products.shape[0] - cells), :] = jnp.zeros(
        (products.shape[0] - cells, products.shape[1]), wide
    )
    chunk = cells // shards
    place = lax.broadcasted_iota(jnp.int32, (chunk, 128), 0)
    slots = lane_slot((chunk, 128))
    last_col = place % width == width - 1
    last_row = place // width % height == height - 1
    row_step, plane_step = width, width * height
    for n in range(shards):
        sums = [None, None]
        for col in range(3):

            def piece(group, offset):
                return products[pl.ds(n * chunk + offset, chunk), pl.ds(group * 128, 128)]

            part = piece(col, 0)
            part = part + jnp.where(slots >= 2, piece(3 + col, plane_step), 0.0)
            by_row = piece(3 + col, 0)
            moved = pltpu.roll(by_row, 96, 1)
            corner = piece(6, plane_step)
            if col > 0:
                corner = pltpu.roll(corner, 32 * col, 1)
            rows = jnp.where(slots == 1, by_row, jnp.where(slots == 3, moved + corner, 0.0))
            part = part + jnp.where(last_row, 0.0, pltpu.roll(rows, chunk - row_step, 0))
            if col == 0:
                part = jnp.where(last_col, 0.0, pltpu.roll(part, chunk - 1, 0))
            to = 0 if col == 1 else 1
            sums[to] = part if sums[to] is None else sums[to] + part
        joined[pl.ds(0, chunk, stride=2), :] = sums[0]
        joined[pl.ds(1, chunk, stride=2), :] = sums[1]
        span = pl.ds(n * 2 * chunk, 2 * chunk)
        slope = jnp.where(own_ref[span, :].astype(wide) > 0, 1.0, leak_slope)
        sent_ref[n] = (joined[...] * slope).astype(low)


def first_terms(core, got, weight, cells):
    rows, lanes = weight.shape
    return pl.pallas_call(
        first_kernel,
        out_shape=(jax.ShapeDtypeStruct((cells, lanes), wide), jax.ShapeDtypeStruct((rows, cells), low)),
        in_specs=[scalar, whole, whole],
        out_specs=(whole, whole),
        scratch_shapes=[pltpu.VMEM((rows, cells), low)],
        compiler_params=params,
        cost_estimate=pl.CostEstimate(flops=10**8, bytes_accessed=3 * 10**6, transcendentals=0),
    )(core, got, weight)


def spread(first, later, other, own, grid, shards):
    cells, lanes = first.shape
    return pl.pallas_call(
        functools.partial(spread_kernel, grid),
        out_shape=jax.ShapeDtypeStruct((shards, 2 * cells // shards, 128), low),
        in_specs=[whole, whole, whole, whole],
        out_specs=whole,
        scratch_shapes=[
            pltpu.VMEM((cells + 32, lanes), wide),
            pltpu.VMEM((2 * cells // shards, 128), wide),
        ],
        compiler_params=params,
        cost_estimate=pl.CostEstimate(flops=5 * 10**8, bytes_accessed=3 * 10**6, transcendentals=0),
    )(first, later, other, own)


def unpack_kernel(got_ref, wide_ref):
    shards, rows, _ = got_ref.shape
    planes, height, columns, _ = wide_ref.shape
    slots = lane_slot((rows, 128))
    for tile in range(shards // 4):
        turned = []
        for m in range(4):
            block = got_ref[tile * 4 + m].astype(wide)
            turned.append([block] + [pltpu.roll(block, 32 * r, 1) for r in range(1, 4)])
        for slot in range(4):
            joined = turned[0][(0 - slot) % 4]
            for m in range(1, 4):
                joined = jnp.where(slots == m, turned[m][(m - slot) % 4], joined)
            joined = joined.reshape(planes // 2, height // 2, columns, 128)
            lanes = pl.ds(tile * 128, 128)
            for z in range(planes // 2):
                for y in range(height // 2):
                    at = (2 * z + slot // 2, 2 * y + slot % 2)
                    wide_ref[at[0], at[1], :, lanes] = joined[z, y]


def unpack(got, grid):
    shape = (*grid, got.shape[0] * 32)
    return pl.pallas_call(
        unpack_kernel,
        out_shape=jax.ShapeDtypeStruct(shape, wide),
        in_specs=[whole],
        out_specs=whole,
        compiler_params=params,
        cost_estimate=pl.CostEstimate(flops=10**6, bytes_accessed=2 * 10**6, transcendentals=0),
    )(got)


def tap_cells(flat, planes, rows, columns):
    channels = flat.shape[1]
    half = columns // 2
    count = planes * rows * half
    first = lax.broadcasted_iota(jnp.int32, (count, channels), 0) % half == 0
    even = flat[pl.ds(0, count, stride=2), :]
    odd = flat[pl.ds(1, count, stride=2), :]
    before = jnp.where(first, 0.0, pltpu.roll(odd, 1, 0))
    cells = []
    for part in (before, even, odd):
        part = part.reshape(planes, rows // 2, 2, half, channels)
        on_even, on_odd = part[:, :, 0], part[:, :, 1]
        ahead = jnp.concatenate([jnp.zeros_like(on_odd[:, :1]), on_odd[:, :-1]], axis=1)
        for taken in (ahead, on_even, on_odd):
            cells.append(taken.reshape(planes, rows // 2 * half, channels).astype(low))
    return cells


def window_kernel(volume_ref, window_ref, done_ref, flat):
    done_ref[...] = jnp.zeros_like(done_ref)
    planes, rows, columns, _ = volume_ref.shape
    flat[...] = volume_ref[...].astype(wide).reshape(flat.shape)
    for n, taken in enumerate(tap_cells(flat, planes, rows, columns)):
        for plane in range(planes):
            window_ref[n, plane % 2, plane // 2] = taken[plane]


def windows(volume):
    planes, rows, columns, channels = volume.shape
    shape = (9, 2, planes // 2, rows * columns // 4, channels)
    return pl.pallas_call(
        window_kernel,
        out_shape=(jax.ShapeDtypeStruct(shape, low), jax.ShapeDtypeStruct((8, 128), wide)),
        in_specs=[whole],
        out_specs=(whole, whole),
        scratch_shapes=[pltpu.VMEM((planes * rows * columns, channels), wide)],
        compiler_params=params,
        cost_estimate=pl.CostEstimate(flops=10**6, bytes_accessed=4 * 10**6, transcendentals=0),
    )(volume)


def lanes_joined(blocks, slot, slots):
    joined = blocks[0][(0 - slot) % 4]
    for m in range(1, 4):
        joined = jnp.where(slots == m, blocks[m][(m - slot) % 4], joined)
    return joined


def cotangent_side(source_ref, cells):
    shards, rows, _ = source_ref.shape
    planes, height, columns, middle = cells.shape
    slots = lane_slot((rows, 128))
    for tile in range(shards // 4):
        turned = []
        for m in range(4):
            block = source_ref[tile * 4 + m].astype(wide)
            turned.append([block] + [pltpu.roll(block, 32 * r, 1) for r in range(1, 4)])
        for slot in range(4):
            joined = lanes_joined(turned, slot, slots).reshape(planes // 2, height // 2, columns, 128)
            for z in range(planes // 2):
                for y in range(height // 2):
                    cells[2 * z + slot // 2, 2 * y + slot % 2, :, pl.ds(tile * 128, 128)] = joined[z, y]
    return cells[...].reshape(planes * height * columns, middle).T.astype(low)


def rim_cells(rim_ref, flat, first_cells):
    _, rows, columns, _ = rim_ref.shape
    flat[...] = rim_ref[...].astype(wide).reshape(flat.shape)
    for n, taken in enumerate(tap_cells(flat, 1, rows, columns)):
        first_cells[n] = taken[0]


def tap_pair(window, first_cells, core, pair):
    planes = window.shape[2]
    both = []
    for n in (2 * pair, 2 * pair + 1):
        tap = core * 14 + n if n < 13 else 13
        depth, row, col = tap // 9, tap // 3 % 3, tap % 3
        which, parity = col * 3 + row, (depth + 1) % 2
        lowest = jnp.where(depth == 0, first_cells[which], window[which, parity, 0])
        below = jnp.where(depth == 0, 0, 1)
        rest = window[which, parity, pl.ds(below, planes - 1)]
        both.append(jnp.concatenate([lowest, rest.reshape(-1, window.shape[4])], axis=0))
    return jnp.concatenate(both, axis=1)


def lower_first_kernel(
    core_ref, got_ref, window, rim_ref, other_rim_ref, done_ref, total_ref, other_cells, cells, flat, first_cells
):
    del done_ref
    rim_cells(other_rim_ref, flat, other_cells)
    rim_cells(rim_ref, flat, first_cells)
    side = cotangent_side(got_ref, cells)
    for pair in range(total_ref.shape[0]):
        taps = tap_pair(window, first_cells, core_ref[0], pair)
        total_ref[pair] = jnp.dot(side, taps, preferred_element_type=wide)


def lower_scratch(grid, middle, window, rim):
    return [
        pltpu.VMEM((*grid, middle), wide),
        pltpu.VMEM((math.prod(rim.shape[:3]), rim.shape[3]), wide),
        pltpu.VMEM((9, *window.shape[3:]), low),
    ]


def lower_first(core, got, window, rim, other_rim, done, grid):
    middle = 32 * got.shape[0]
    return pl.pallas_call(
        lower_first_kernel,
        out_shape=(
            jax.ShapeDtypeStruct((7, middle, 2 * window.shape[4]), wide),
            jax.ShapeDtypeStruct((9, *window.shape[3:]), low),
        ),
        in_specs=[scalar, whole, whole, whole, whole, whole],
        out_specs=(whole, whole),
        scratch_shapes=lower_scratch(grid, middle, window, rim),
        compiler_params=params,
        cost_estimate=pl.CostEstimate(flops=5 * 10**8, bytes_accessed=5 * 10**6, transcendentals=0),
    )(core, got, window, rim, other_rim, done)


def lower_kernel(core_ref, total_ref, other_ref, window, first_cells, sent_ref, cells, staged, left):
    side = cotangent_side(other_ref, cells)
    shards = staged.shape[0]
    below = window.shape[4]
    share = below // shards
    copies = []
    for pair in range(total_ref.shape[0]):
        taps = tap_pair(window, first_cells, core_ref[0], pair)
        total = total_ref[pair] + jnp.dot(side, taps, preferred_element_type=wide)
        total = total.T.astype(low)
        count = 0
        for n in (2 * pair, 2 * pair + 1):
            rows = total[n % 2 * below : (n % 2 + 1) * below]
            halves = [rows[:, :128], rows[:, 128:]]
            if n == 13:
                halves = [jnp.where(core_ref[0] == 0, *halves)]
            for half in halves:
                start = 2 * pair * 2 * share + count * share
                for d in range(shards):
                    staged[d, pl.ds(start, share), :] = half[d * share : (d + 1) * share]
                count += 1
        part = pl.ds(4 * pair * share, count * share)
        copies.append(pltpu.make_async_copy(staged.at[:, part, :], sent_ref.at[:, part, :], left.at[pair]))
        copies[-1].start()
    for copy in copies:
        copy.wait()


def lower_terms(core, total, other, window, first_cells, grid):
    shards = other.shape[0]
    pairs, middle, _ = total.shape
    shape = (shards, 27 * window.shape[4] // shards, 128)
    return pl.pallas_call(
        lower_kernel,
        out_shape=pltpu.HBM(shape, low),
        in_specs=[scalar, whole, whole, whole, whole],
        out_specs=anywhere,
        scratch_shapes=[
            pltpu.VMEM((*grid, middle), wide),
            pltpu.VMEM(shape, low),
            pltpu.SemaphoreType.DMA((pairs,)),
        ],
        compiler_params=params,
        cost_estimate=pl.CostEstimate(flops=5 * 10**8, bytes_accessed=5 * 10**6, transcendentals=0),
    )(core, total, other, window, first_cells)


def total_kernel(shares_ref, total_ref, *, scale):
    share = total_ref.shape[1]
    for core in range(2):
        total = shares_ref[core].astype(wide)
        for by in range(2, shares_ref.shape[0], 2):
            total = total + shares_ref[core + by].astype(wide)
        total = total * scale
        for n in range(13):
            for half in range(2):
                start = (2 * n + half) * share
                total_ref[core * 14 + n, :, pl.ds(half * 128, 128)] = total[start : start + share]
        total_ref[13, :, pl.ds(core * 128, 128)] = total[26 * share : 27 * share]


def total_terms(shares, scale):
    return pl.pallas_call(
        functools.partial(total_kernel, scale=scale),
        out_shape=jax.ShapeDtypeStruct((27, shares.shape[1] // 27, 2 * shares.shape[2]), wide),
        in_specs=[whole],
        out_specs=whole,
        compiler_params=params,
        cost_estimate=pl.CostEstimate(flops=10**6, bytes_accessed=10**6, transcendentals=0),
    )(shares)


def upper_kernel(core_ref, volume_ref, cot_ref, mine_ref, theirs_ref, flat, cot_flat, lined, left):
    planes, rows, columns, channels = volume_ref.shape
    depth, height, width, outs = cot_ref.shape
    half = outs // 2
    tiles = channels // 128
    for tile in range(tiles):
        lanes = pl.ds(tile * 128, 128)
        flat[tile] = volume_ref[:, :, :, lanes].astype(wide).reshape(flat.shape[1:])
    cot_wide = cot_ref[...].astype(wide).reshape(cot_flat.shape[0], outs)
    cot_flat[...] = jnp.concatenate([cot_wide, jnp.zeros((cot_flat.shape[0], 128 - outs), wide)], axis=1)
    pieces = [cot_flat[pl.ds(n, depth, stride=height * width), :] for n in range(height * width)]
    left[...] = jnp.concatenate(pieces, axis=0).T[:outs].astype(low)
    core = core_ref[0]
    split = [left[pl.ds(pl.multiple_of(at * half, half), half), :] for at in (core, 1 - core)]
    side = jnp.concatenate(split, axis=0)
    first = lax.broadcasted_iota(jnp.int32, (depth, 128), 0) == 0
    stride = 2 * rows * columns
    for row in range(rows):
        for col in range(columns):
            for tile in range(tiles):
                even = flat[tile, pl.ds(row * columns + col, depth, stride=stride), :]
                odd = flat[tile, pl.ds(stride // 2 + row * columns + col, depth, stride=stride), :]
                before = jnp.where(first, 0.0, pltpu.roll(odd, 1, 0))
                for depth_tap, part in enumerate((before, even, odd)):
                    lined[depth_tap, row, col, :, pl.ds(tile * 128, 128)] = part.astype(low)
    nothing = jnp.zeros((depth, channels), low)
    for tap in range(27):
        depth_tap, row_tap, col_tap = tap // 9, tap // 3 % 3, tap % 3
        taken = []
        for y in range(height):
            for x in range(width):
                row, col = 2 * y + row_tap - 1, 2 * x + col_tap - 1
                taken.append(nothing if row < 0 or col < 0 else lined[depth_tap, row, col])
        term = jnp.dot(side, jnp.concatenate(taken, axis=0), preferred_element_type=wide)
        mine_ref[tap] = term[:half]
        theirs_ref[tap] = term[half:].astype(low)


def upper_terms(core, volume, cot):
    planes, rows, columns, channels = volume.shape
    depth, height, width, outs = cot.shape
    shape = (27, outs // 2, channels)
    return pl.pallas_call(
        upper_kernel,
        out_shape=(jax.ShapeDtypeStruct(shape, wide), jax.ShapeDtypeStruct(shape, low)),
        in_specs=[scalar, whole, whole],
        out_specs=(whole, whole),
        scratch_shapes=[
            pltpu.VMEM((channels // 128, planes * rows * columns, 128), wide),
            pltpu.VMEM((depth * height * width, 128), wide),
            pltpu.VMEM((3, rows, columns, depth, channels), low),
            pltpu.VMEM((outs, depth * height * width), low),
        ],
        compiler_params=params,
        cost_estimate=pl.CostEstimate(flops=5 * 10**8, bytes_accessed=6 * 10**6, transcendentals=0),
    )(core, volume, cot)


def partner(array, axis, by):
    size = lax.axis_size(axis)
    return lax.ppermute(array, axis, [(i, i ^ by) for i in range(size)])


def exchange(blocks, axis):
    return lax.all_to_all(blocks, axis, split_axis=0, concat_axis=0, tiled=True)


def filter_gradient(volume, cotangent, padding):
    return lax.conv_general_dilated(
        volume[None],
        cotangent[None],
        (1, 1, 1),
        padding,
        rhs_dilation=(2, 2, 2),
        dimension_numbers=("CDHWN", "IDHWO", "DHWNC"),
        preferred_element_type=jnp.float32,
    )


def input_gradient(cotangent, filters):
    return lax.conv_general_dilated(
        cotangent[None],
        filters[::-1, ::-1, ::-1],
        (1, 1, 1),
        ((1, 2), (1, 2), (1, 2)),
        lhs_dilation=(2, 2, 2),
        dimension_numbers=("NDHWC", "DHWOI", "NDHWC"),
        preferred_element_type=jnp.float32,
    )[0]


def plain_body(act_64, cot_32, filters_32, act_128):
    shards = lax.axis_size("chan")
    samples = lax.axis_size("sample")
    position = lax.axis_index("chan")
    core = lax.axis_index("sample") % 2
    volume_64 = act_64[0]
    cot_local = cot_32[0]
    depth, height, width, shard_out = cot_local.shape
    planes, rows, columns, middle = volume_64.shape
    below = act_128.shape[4]
    slab = planes // shards
    part = middle // shards

    rim = lax.ppermute(act_128[:, -1:], "chan", [(i, i + 1) for i in range(shards - 1)])

    taps = filters_32.reshape(27, shards, part, shard_out).transpose(1, 0, 3, 2)
    lanes = 128 if taps.size // shards % 256 == 0 else 64
    taps = taps.reshape(shards, 2, -1, lanes)
    own_half = lax.dynamic_index_in_dim(taps, core, 1, keepdims=False)
    cot_rows = jnp.broadcast_to(cot_local.reshape(1, -1, lanes), (shards, cot_local.size // lanes, lanes))
    sent = jnp.concatenate([own_half, cot_rows], axis=1)
    got = exchange(sent, "chan")
    cut = own_half.shape[1]
    got_half = got[:, :cut]
    other_half = partner(got_half, "sample", 1)
    first = jnp.where(core == 0, got_half, other_half)
    second = jnp.where(core == 0, other_half, got_half)
    part_filters = jnp.concatenate([first, second], axis=1)
    part_filters = part_filters.reshape(shards, 3, 3, 3, shard_out, part)
    part_filters = part_filters.transpose(1, 2, 3, 5, 0, 4).reshape(3, 3, 3, part, -1)
    cot_all = got[:, cut:].reshape(shards, depth, height, width, shard_out)
    cot_all = cot_all.transpose(1, 2, 3, 0, 4).reshape(depth, height, width, -1)

    grad_upper = filter_gradient(volume_64, cot_local, ((1, 0),) * 3)
    total_upper = lax.psum(grad_upper, "sample")

    grad_part = input_gradient(cot_all, part_filters)
    own_part = lax.dynamic_slice_in_dim(volume_64, position * part, part, 3)
    cot_part = (grad_part * jnp.where(own_part > 0, 1.0, leak_slope)).astype(low)
    cot_got = exchange(cot_part.reshape(shards, -1, 128), "chan")
    cot_low = cot_got.reshape(shards, slab, rows, columns, part)
    cot_low = cot_low.transpose(1, 2, 3, 0, 4).reshape(slab, rows, columns, middle)

    window = jnp.concatenate([rim, act_128], axis=1)[0]
    grad_lower = filter_gradient(window, cot_low, ((0, 0), (1, 0), (1, 0)))
    blocks = grad_lower.reshape(27, shards, 2, -1, middle).transpose(2, 1, 0, 3, 4)
    mine = lax.dynamic_index_in_dim(blocks, core, 0, keepdims=False)
    theirs = lax.dynamic_index_in_dim(blocks, 1 - core, 0, keepdims=False)
    mine = mine + partner(theirs.astype(low), "sample", 1).astype(jnp.float32)
    got_terms = exchange(mine.astype(low), "chan")
    share = jnp.sum(got_terms.astype(jnp.float32), axis=0)
    if samples > 2:
        pairs = [[2 * i + k for i in range(samples // 2)] for k in range(2)]
        share = lax.psum(share, "sample", axis_index_groups=pairs)
    share = lax.all_gather(
        share, "sample", axis=1, tiled=True, axis_index_groups=[[i, i + 1] for i in range(0, samples, 2)]
    )
    total_lower = share.reshape(3, 3, 3, below // shards, middle)
    return (
        total_upper / samples,
        total_lower / samples,
        cot_low.astype(jnp.float32)[None],
    )


def core_sum(mine, theirs):
    return (mine + partner(theirs, "sample", 1).astype(wide)).astype(low)


def sample_sum(mine, samples):
    core = lax.axis_index("sample") % 2
    total = mine.astype(wide)
    for by in range(2, samples, 2):
        pairs = [(i, (i + by) % samples) for i in range(samples)]
        total = total + lax.ppermute(mine, "sample", pairs).astype(wide)
    total = total * (1.0 / samples)
    other = partner(total, "sample", 1)
    first = jnp.where(core == 0, total, other)
    second = jnp.where(core == 0, other, total)
    return jnp.concatenate([first, second], axis=1)


def body(act_64, cot_32, filters_32, act_128):
    shards = lax.axis_size("chan")
    samples = lax.axis_size("sample")
    middle = act_64.shape[4]
    grid = cot_32.shape[1:4]
    shard_out = cot_32.shape[4]
    below = act_128.shape[4]
    if middle != 32 * shards or shards % 4 or samples != 4 or shard_out != 64 or (2 * grid[2]) != 8:
        return plain_body(act_64, cot_32, filters_32, act_128)
    core = lax.axis_index("sample") % 2
    cores = core[None].astype(jnp.int32)
    position = lax.axis_index("chan")[None].astype(jnp.int32)
    volume_64 = act_64[0]
    cot_local = cot_32[0]
    slab = volume_64.shape[0] // shards

    rim = lax.ppermute(act_128[:, -1:], "chan", [(i, i + 1) for i in range(shards - 1)])
    turned = filters_32.transpose(0, 1, 2, 4, 3).reshape(27, shard_out, middle)
    sent = pack(cores, turned, cot_local.reshape(-1, shard_out), shards)
    got = exchange(sent, "chan")

    own = own_signs(position, volume_64)
    other_act = partner(act_128, "sample", 1)
    halves = upper_terms(cores, volume_64, cot_local)
    window, done = windows(act_128[0])
    other_window, other_done = windows(other_act[0])
    done = done + other_done
    chip_upper = core_sum(*halves)
    beside = (got, own, rim, done, chip_upper)
    got, own, rim, done, chip_upper = lax.optimization_barrier(beside)
    weight = weights(got, shard_out // 2)
    other_weight = partner(weight, "sample", 1)
    first, later = first_terms(cores, got, weight, math.prod(grid))
    cot_sent = spread(first, later, other_weight, own, grid, shards)

    cot_sent, rim, chip_upper = lax.optimization_barrier((cot_sent, rim, chip_upper))
    cot_got = exchange(cot_sent, "chan")
    other_rim = partner(rim, "sample", 1)
    cot_got, other_rim = lax.optimization_barrier((cot_got, other_rim))
    total_upper = sample_sum(chip_upper, samples).reshape(3, 3, 3, shard_out, middle)
    total_upper = total_upper.transpose(0, 1, 2, 4, 3)

    other_cot = partner(cot_got, "sample", 1)
    slab_grid = (slab, *volume_64.shape[1:3])
    own_terms, below_other = lower_first(cores, cot_got, window, rim[0], other_rim[0], done, slab_grid)
    terms = lower_terms(cores, own_terms, other_cot, other_window, below_other, slab_grid)
    share = jnp.sum(exchange(terms, "chan").astype(wide), axis=0)
    cot_full = unpack(cot_got, slab_grid)
    shares = lax.all_gather(share.astype(low), "sample", axis=0)
    total_lower = total_terms(shares, 1.0 / samples).reshape(3, 3, 3, below // shards, middle)
    return (total_upper, total_lower, cot_full[None])


def solution(mesh):
    placed = (
        P("sample", None, None, None, None),
        P("sample", None, None, None, "chan"),
        P(None, None, None, None, "chan"),
        P("sample", "chan", None, None, None),
    )
    return jax.shard_map(
        body,
        mesh=mesh,
        in_specs=placed,
        out_specs=(
            P(None, None, None, None, "chan"),
            P(None, None, None, "chan", None),
            P("sample", "chan", None, None, None),
        ),
        check_vma=False,
    )
```

```python
import functools
import math

import jax
import jax.numpy as jnp
from jax import lax
from jax.experimental import pallas as pl
from jax.experimental.pallas import tpu as pltpu
from jax.sharding import PartitionSpec as P

leak_slope = 0.3
low = jnp.bfloat16
wide = jnp.float32
params = pltpu.CompilerParams(vmem_limit_bytes=20 * 2**20)
whole = pl.BlockSpec(memory_space=pltpu.VMEM)
scalar = pl.BlockSpec(memory_space=pltpu.SMEM)
anywhere = pl.BlockSpec(memory_space=pltpu.HBM)


def slot_plan():
    groups = []
    for col in range(3):
        groups.append([(1, 1, col), (1, 2, col), (2, 1, col), (2, 2, col)])
    for col in range(3):
        groups.append([(2, 0, col), (1, 0, col), (0, 1, col), (0, 2, col)])
    groups.append([None, (0, 0, 2), (0, 0, 1), (0, 0, 0)])
    return groups


def tap_index(tap):
    return (tap[0] * 3 + tap[1]) * 3 + tap[2]


def lane_slot(shape):
    return lax.broadcasted_iota(jnp.int32, shape, len(shape) - 1) // 32


def pack_kernel(core_ref, filters_ref, cot_ref, sent_ref, held, cot_held, staged, arrived, left):
    taps, half, _ = held.shape
    groups = slot_plan()
    start = pl.multiple_of(core_ref[0] * half, half)
    fetch_filters = pltpu.make_async_copy(filters_ref.at[:, pl.ds(start, half), :], held, arrived.at[0])
    fetch_cot = pltpu.make_async_copy(cot_ref, cot_held, arrived.at[1])
    fetch_cot.start()
    fetch_filters.start()
    slots = lane_slot((half, 128))
    shards = staged.shape[0]
    rows = len(groups) * half
    outs = cot_held.shape[1]
    cells = cot_held.shape[0]

    def send(index, first, count):
        part = pl.ds(first, count)
        return pltpu.make_async_copy(staged.at[:, part, :], sent_ref.at[:, part, :], left.at[index])

    fetch_cot.wait()
    turned_cot = cot_held[...].astype(wide).T.astype(low)
    for d in range(shards):
        for b in range(cells // 128):
            staged[d, pl.ds(rows + b * outs, outs), :] = turned_cot[:, b * 128 : (b + 1) * 128]
    copies = [send(0, rows, cells // 128 * outs)]
    copies[0].start()
    fetch_filters.wait()
    for g, group in enumerate(groups):
        for tile in range(shards // 4):
            turned = []
            for tap in group:
                if tap is None:
                    turned.append([jnp.zeros((half, 128), wide)] * 4)
                    continue
                block = held[tap_index(tap), :, pl.ds(tile * 128, 128)].astype(wide)
                turned.append([block] + [pltpu.roll(block, 32 * r, 1) for r in range(1, 4)])
            for m in range(4):
                joined = turned[0][(0 - m) % 4]
                for k in range(1, 4):
                    joined = jnp.where(slots == k, turned[k][(k - m) % 4], joined)
                staged[tile * 4 + m, pl.ds(g * half, half), :] = joined.astype(low)
        copies.append(send(g + 1, g * half, half))
        copies[-1].start()
    for copy in copies:
        copy.wait()


def pack(core, filters, cot, shards):
    taps, outs, middle = filters.shape
    groups = len(slot_plan())
    shape = (shards, groups * (outs // 2) + cot.shape[0] // 128 * outs, 128)
    return pl.pallas_call(
        pack_kernel,
        out_shape=pltpu.HBM(shape, low),
        in_specs=[scalar, anywhere, anywhere],
        out_specs=anywhere,
        scratch_shapes=[
            pltpu.VMEM((taps, outs // 2, middle), low),
            pltpu.VMEM(cot.shape, low),
            pltpu.VMEM(shape, low),
            pltpu.SemaphoreType.DMA((2,)),
            pltpu.SemaphoreType.DMA((groups + 1,)),
        ],
        compiler_params=params,
        cost_estimate=pl.CostEstimate(flops=10**6, bytes_accessed=3 * 10**6, transcendentals=0),
    )(core, pltpu.with_memory_space_constraint(filters, pltpu.HBM), pltpu.with_memory_space_constraint(cot, pltpu.HBM))


def sign_kernel(position_ref, volume_ref, own_ref):
    part = position_ref[0] % 4
    rows = own_ref.shape[0]
    slots = lane_slot((rows, 128))
    joined = None
    for depth_par in range(2):
        for row_par in range(2):
            slot = depth_par * 2 + row_par
            block = volume_ref[:, depth_par, :, row_par].astype(wide).reshape(rows, 128)
            block = pltpu.roll(block, (slot - part + 4) % 4 * 32, 1)
            joined = block if joined is None else jnp.where(slots == slot, block, joined)
    own_ref[...] = jnp.where(joined > 0, 1.0, leak_slope)


def own_signs(position, volume):
    planes, rows, columns, channels = volume.shape
    split = volume.reshape(planes // 2, 2, rows // 2, 2, columns, channels)
    count = planes * rows * columns // 4
    return pl.pallas_call(
        sign_kernel,
        out_shape=jax.ShapeDtypeStruct((count, 128), wide),
        grid_spec=pltpu.PrefetchScalarGridSpec(
            num_scalar_prefetch=1,
            grid=(1,),
            in_specs=[
                pl.BlockSpec(
                    (planes // 2, 2, rows // 2, 2, columns, 128),
                    lambda i, at: (0, 0, 0, 0, 0, at[0] // 4),
                )
            ],
            out_specs=pl.BlockSpec((count, 128), lambda i, at: (0, 0)),
        ),
        compiler_params=params,
        cost_estimate=pl.CostEstimate(flops=10**6, bytes_accessed=4 * 10**6, transcendentals=0),
    )(position, split)


def weight_kernel(got_ref, weight_ref):
    shards = got_ref.shape[0]
    groups = len(slot_plan())
    half = weight_ref.shape[0] // shards
    for c in range(shards):
        for g in range(groups):
            weight_ref[pl.ds(c * half, half), pl.ds(g * 128, 128)] = got_ref[c, pl.ds(g * half, half), :]


def weights(got, half):
    shards = got.shape[0]
    groups = len(slot_plan())
    return pl.pallas_call(
        weight_kernel,
        out_shape=jax.ShapeDtypeStruct((shards * half, groups * 128), low),
        grid=(1,),
        in_specs=[pl.BlockSpec((shards, groups * half, 128), lambda i: (0, 0, 0))],
        out_specs=whole,
        compiler_params=params,
        cost_estimate=pl.CostEstimate(flops=10**5, bytes_accessed=10**6, transcendentals=0),
    )(got)


def first_kernel(core_ref, got_ref, weight_ref, products_ref, later_ref, turned):
    shards = got_ref.shape[0]
    half = later_ref.shape[0] // shards
    groups = len(slot_plan())
    core = core_ref[0]
    for c in range(shards):
        span = pl.ds(c * half, half)
        for b in range(later_ref.shape[1] // 128):
            lanes = pl.ds(b * 128, 128)
            first = groups * half + b * 2 * half
            turned[span, lanes] = got_ref[c, pl.ds(pl.multiple_of(first + core * half, half), half), :]
            later_ref[span, lanes] = got_ref[c, pl.ds(pl.multiple_of(first + (1 - core) * half, half), half), :]
    products_ref[...] = lax.dot_general(
        turned[...], weight_ref[...], (((0,), (0,)), ((), ())), preferred_element_type=wide
    )


def spread_kernel(grid, first_ref, later_ref, other_ref, own_ref, sent_ref, products, joined):
    depth, height, width = grid
    cells = depth * height * width
    shards = sent_ref.shape[0]
    products[pl.ds(0, cells), :] = first_ref[...] + lax.dot_general(
        later_ref[...], other_ref[...], (((0,), (0,)), ((), ())), preferred_element_type=wide
    )
    products[pl.ds(cells, products.shape[0] - cells), :] = jnp.zeros(
        (products.shape[0] - cells, products.shape[1]), wide
    )
    chunk = cells // shards
    place = lax.broadcasted_iota(jnp.int32, (chunk, 128), 0)
    slots = lane_slot((chunk, 128))
    last_col = place % width == width - 1
    last_row = place // width % height == height - 1
    row_step, plane_step = width, width * height
    for n in range(shards):
        sums = [None, None]
        for col in range(3):

            def piece(group, offset):
                return products[pl.ds(n * chunk + offset, chunk), pl.ds(group * 128, 128)]

            part = piece(col, 0)
            part = part + jnp.where(slots >= 2, piece(3 + col, plane_step), 0.0)
            by_row = piece(3 + col, 0)
            moved = pltpu.roll(by_row, 96, 1)
            corner = piece(6, plane_step)
            if col > 0:
                corner = pltpu.roll(corner, 32 * col, 1)
            rows = jnp.where(slots == 1, by_row, jnp.where(slots == 3, moved + corner, 0.0))
            part = part + jnp.where(last_row, 0.0, pltpu.roll(rows, chunk - row_step, 0))
            if col == 0:
                part = jnp.where(last_col, 0.0, pltpu.roll(part, chunk - 1, 0))
            to = 0 if col == 1 else 1
            sums[to] = part if sums[to] is None else sums[to] + part
        joined[pl.ds(0, chunk, stride=2), :] = sums[0]
        joined[pl.ds(1, chunk, stride=2), :] = sums[1]
        span = pl.ds(n * 2 * chunk, 2 * chunk)
        slope = own_ref[span, :]
        sent_ref[n] = (joined[...] * slope).astype(low)


def first_terms(core, got, weight, cells):
    rows, lanes = weight.shape
    return pl.pallas_call(
        first_kernel,
        out_shape=(jax.ShapeDtypeStruct((cells, lanes), wide), jax.ShapeDtypeStruct((rows, cells), low)),
        in_specs=[scalar, whole, whole],
        out_specs=(whole, whole),
        scratch_shapes=[pltpu.VMEM((rows, cells), low)],
        compiler_params=params,
        cost_estimate=pl.CostEstimate(flops=10**8, bytes_accessed=3 * 10**6, transcendentals=0),
    )(core, got, weight)


def spread(first, later, other, own, grid, shards):
    cells, lanes = first.shape
    return pl.pallas_call(
        functools.partial(spread_kernel, grid),
        out_shape=jax.ShapeDtypeStruct((shards, 2 * cells // shards, 128), low),
        in_specs=[whole, whole, whole, whole],
        out_specs=whole,
        scratch_shapes=[
            pltpu.VMEM((cells + 32, lanes), wide),
            pltpu.VMEM((2 * cells // shards, 128), wide),
        ],
        compiler_params=params,
        cost_estimate=pl.CostEstimate(flops=5 * 10**8, bytes_accessed=3 * 10**6, transcendentals=0),
    )(first, later, other, own)


def unpack_kernel(got_ref, wide_ref):
    shards, rows, _ = got_ref.shape
    planes, height, columns, _ = wide_ref.shape
    slots = lane_slot((rows, 128))
    for tile in range(shards // 4):
        turned = []
        for m in range(4):
            block = got_ref[tile * 4 + m].astype(wide)
            turned.append([block] + [pltpu.roll(block, 32 * r, 1) for r in range(1, 4)])
        for slot in range(4):
            joined = turned[0][(0 - slot) % 4]
            for m in range(1, 4):
                joined = jnp.where(slots == m, turned[m][(m - slot) % 4], joined)
            joined = joined.reshape(planes // 2, height // 2, columns, 128)
            lanes = pl.ds(tile * 128, 128)
            for z in range(planes // 2):
                for y in range(height // 2):
                    at = (2 * z + slot // 2, 2 * y + slot % 2)
                    wide_ref[at[0], at[1], :, lanes] = joined[z, y]


def unpack(got, grid):
    shape = (*grid, got.shape[0] * 32)
    return pl.pallas_call(
        unpack_kernel,
        out_shape=jax.ShapeDtypeStruct(shape, wide),
        in_specs=[whole],
        out_specs=whole,
        compiler_params=params,
        cost_estimate=pl.CostEstimate(flops=10**6, bytes_accessed=2 * 10**6, transcendentals=0),
    )(got)


def tap_cells(flat, planes, rows, columns):
    channels = flat.shape[1]
    half = columns // 2
    count = planes * rows * half
    first = lax.broadcasted_iota(jnp.int32, (count, channels), 0) % half == 0
    even = flat[pl.ds(0, count, stride=2), :]
    odd = flat[pl.ds(1, count, stride=2), :]
    before = jnp.where(first, 0.0, pltpu.roll(odd, 1, 0))
    cells = []
    for part in (before, even, odd):
        part = part.reshape(planes, rows // 2, 2, half, channels)
        on_even, on_odd = part[:, :, 0], part[:, :, 1]
        ahead = jnp.concatenate([jnp.zeros_like(on_odd[:, :1]), on_odd[:, :-1]], axis=1)
        for taken in (ahead, on_even, on_odd):
            cells.append(taken.reshape(planes, rows // 2 * half, channels).astype(low))
    return cells


def window_kernel(volume_ref, window_ref, done_ref, flat):
    done_ref[...] = jnp.zeros_like(done_ref)
    planes, rows, columns, _ = volume_ref.shape
    flat[...] = volume_ref[...].astype(wide).reshape(flat.shape)
    for n, taken in enumerate(tap_cells(flat, planes, rows, columns)):
        for plane in range(planes):
            window_ref[n, plane % 2, plane // 2] = taken[plane]


def windows(volume):
    planes, rows, columns, channels = volume.shape
    shape = (9, 2, planes // 2, rows * columns // 4, channels)
    return pl.pallas_call(
        window_kernel,
        out_shape=(jax.ShapeDtypeStruct(shape, low), jax.ShapeDtypeStruct((8, 128), wide)),
        in_specs=[whole],
        out_specs=(whole, whole),
        scratch_shapes=[pltpu.VMEM((planes * rows * columns, channels), wide)],
        compiler_params=params,
        cost_estimate=pl.CostEstimate(flops=10**6, bytes_accessed=4 * 10**6, transcendentals=0),
    )(volume)


def lanes_joined(blocks, slot, slots):
    joined = blocks[0][(0 - slot) % 4]
    for m in range(1, 4):
        joined = jnp.where(slots == m, blocks[m][(m - slot) % 4], joined)
    return joined


def cotangent_side(source_ref, cells):
    shards, rows, _ = source_ref.shape
    planes, height, columns, middle = cells.shape
    slots = lane_slot((rows, 128))
    for tile in range(shards // 4):
        turned = []
        for m in range(4):
            block = source_ref[tile * 4 + m].astype(wide)
            turned.append([block] + [pltpu.roll(block, 32 * r, 1) for r in range(1, 4)])
        for slot in range(4):
            joined = lanes_joined(turned, slot, slots).reshape(planes // 2, height // 2, columns, 128)
            for z in range(planes // 2):
                for y in range(height // 2):
                    cells[2 * z + slot // 2, 2 * y + slot % 2, :, pl.ds(tile * 128, 128)] = joined[z, y]
    return cells[...].reshape(planes * height * columns, middle).astype(low).T


def rim_cells(rim_ref, flat, first_cells):
    _, rows, columns, _ = rim_ref.shape
    flat[...] = rim_ref[...].astype(wide).reshape(flat.shape)
    for n, taken in enumerate(tap_cells(flat, 1, rows, columns)):
        first_cells[n] = taken[0]


def tap_pair(window, first_cells, core, pair):
    planes = window.shape[2]
    both = []
    for n in (2 * pair, 2 * pair + 1):
        tap = core * 14 + n if n < 13 else 13
        depth, row, col = tap // 9, tap // 3 % 3, tap % 3
        which, parity = col * 3 + row, (depth + 1) % 2
        lowest = jnp.where(depth == 0, first_cells[which], window[which, parity, 0])
        below = jnp.where(depth == 0, 0, 1)
        rest = window[which, parity, pl.ds(below, planes - 1)]
        both.append(jnp.concatenate([lowest, rest.reshape(-1, window.shape[4])], axis=0))
    return jnp.concatenate(both, axis=1)


def lower_first_kernel(
    core_ref, got_ref, window, rim_ref, other_rim_ref, done_ref, total_ref, other_cells, cells, flat, first_cells
):
    del done_ref
    rim_cells(other_rim_ref, flat, other_cells)
    rim_cells(rim_ref, flat, first_cells)
    side = cotangent_side(got_ref, cells)
    for pair in range(total_ref.shape[0]):
        taps = tap_pair(window, first_cells, core_ref[0], pair)
        total_ref[pair] = jnp.dot(side, taps, preferred_element_type=wide)


def lower_scratch(grid, middle, window, rim):
    return [
        pltpu.VMEM((*grid, middle), wide),
        pltpu.VMEM((math.prod(rim.shape[:3]), rim.shape[3]), wide),
        pltpu.VMEM((9, *window.shape[3:]), low),
    ]


def lower_first(core, got, window, rim, other_rim, done, grid):
    middle = 32 * got.shape[0]
    return pl.pallas_call(
        lower_first_kernel,
        out_shape=(
            jax.ShapeDtypeStruct((7, middle, 2 * window.shape[4]), wide),
            jax.ShapeDtypeStruct((9, *window.shape[3:]), low),
        ),
        in_specs=[scalar, whole, whole, whole, whole, whole],
        out_specs=(whole, whole),
        scratch_shapes=lower_scratch(grid, middle, window, rim),
        compiler_params=params,
        cost_estimate=pl.CostEstimate(flops=5 * 10**8, bytes_accessed=5 * 10**6, transcendentals=0),
    )(core, got, window, rim, other_rim, done)


def lower_kernel(core_ref, total_ref, other_ref, window, first_cells, sent_ref, cells, staged, left):
    side = cotangent_side(other_ref, cells)
    shards = staged.shape[0]
    below = window.shape[4]
    share = below // shards
    copies = []
    for pair in range(total_ref.shape[0]):
        taps = tap_pair(window, first_cells, core_ref[0], pair)
        total = total_ref[pair] + jnp.dot(side, taps, preferred_element_type=wide)
        total = total.astype(low).T
        count = 0
        for n in (2 * pair, 2 * pair + 1):
            rows = total[n % 2 * below : (n % 2 + 1) * below]
            halves = [rows[:, :128], rows[:, 128:]]
            if n == 13:
                halves = [jnp.where(core_ref[0] == 0, *halves)]
            for half in halves:
                start = 2 * pair * 2 * share + count * share
                for d in range(shards):
                    staged[d, pl.ds(start, share), :] = half[d * share : (d + 1) * share]
                count += 1
        part = pl.ds(4 * pair * share, count * share)
        copies.append(pltpu.make_async_copy(staged.at[:, part, :], sent_ref.at[:, part, :], left.at[pair]))
        copies[-1].start()
    for copy in copies:
        copy.wait()


def lower_terms(core, total, other, window, first_cells, grid):
    shards = other.shape[0]
    pairs, middle, _ = total.shape
    shape = (shards, 27 * window.shape[4] // shards, 128)
    return pl.pallas_call(
        lower_kernel,
        out_shape=pltpu.HBM(shape, low),
        in_specs=[scalar, whole, whole, whole, whole],
        out_specs=anywhere,
        scratch_shapes=[
            pltpu.VMEM((*grid, middle), wide),
            pltpu.VMEM(shape, low),
            pltpu.SemaphoreType.DMA((pairs,)),
        ],
        compiler_params=params,
        cost_estimate=pl.CostEstimate(flops=5 * 10**8, bytes_accessed=5 * 10**6, transcendentals=0),
    )(core, total, other, window, first_cells)


def total_kernel(shares_ref, total_ref, *, scale):
    share = total_ref.shape[1]
    for core in range(2):
        total = shares_ref[core].astype(wide)
        for by in range(2, shares_ref.shape[0], 2):
            total = total + shares_ref[core + by].astype(wide)
        total = total * scale
        for n in range(13):
            for half in range(2):
                start = (2 * n + half) * share
                total_ref[core * 14 + n, :, pl.ds(half * 128, 128)] = total[start : start + share]
        total_ref[13, :, pl.ds(core * 128, 128)] = total[26 * share : 27 * share]


def total_terms(shares, scale):
    return pl.pallas_call(
        functools.partial(total_kernel, scale=scale),
        out_shape=jax.ShapeDtypeStruct((27, shares.shape[1] // 27, 2 * shares.shape[2]), wide),
        in_specs=[whole],
        out_specs=whole,
        compiler_params=params,
        cost_estimate=pl.CostEstimate(flops=10**6, bytes_accessed=10**6, transcendentals=0),
    )(shares)


def upper_kernel(core_ref, volume_ref, cot_ref, mine_ref, theirs_ref, flat, cot_flat, lined, left):
    planes, rows, columns, channels = volume_ref.shape
    depth, height, width, outs = cot_ref.shape
    half = outs // 2
    tiles = channels // 128
    for tile in range(tiles):
        lanes = pl.ds(tile * 128, 128)
        flat[tile] = volume_ref[:, :, :, lanes].astype(wide).reshape(flat.shape[1:])
    cot_wide = cot_ref[...].astype(wide).reshape(cot_flat.shape[0], outs)
    cot_flat[...] = jnp.concatenate([cot_wide, jnp.zeros((cot_flat.shape[0], 128 - outs), wide)], axis=1)
    pieces = [cot_flat[pl.ds(n, depth, stride=height * width), :] for n in range(height * width)]
    left[...] = jnp.concatenate(pieces, axis=0).T[:outs].astype(low)
    core = core_ref[0]
    split = [left[pl.ds(pl.multiple_of(at * half, half), half), :] for at in (core, 1 - core)]
    side = jnp.concatenate(split, axis=0)
    first = lax.broadcasted_iota(jnp.int32, (depth, 128), 0) == 0
    stride = 2 * rows * columns
    for row in range(rows):
        for col in range(columns):
            for tile in range(tiles):
                even = flat[tile, pl.ds(row * columns + col, depth, stride=stride), :]
                odd = flat[tile, pl.ds(stride // 2 + row * columns + col, depth, stride=stride), :]
                before = jnp.where(first, 0.0, pltpu.roll(odd, 1, 0))
                for depth_tap, part in enumerate((before, even, odd)):
                    lined[depth_tap, row, col, :, pl.ds(tile * 128, 128)] = part.astype(low)
    nothing = jnp.zeros((depth, channels), low)
    for tap in range(27):
        depth_tap, row_tap, col_tap = tap // 9, tap // 3 % 3, tap % 3
        taken = []
        for y in range(height):
            for x in range(width):
                row, col = 2 * y + row_tap - 1, 2 * x + col_tap - 1
                taken.append(nothing if row < 0 or col < 0 else lined[depth_tap, row, col])
        term = jnp.dot(side, jnp.concatenate(taken, axis=0), preferred_element_type=wide)
        mine_ref[tap] = term[:half]
        theirs_ref[tap] = term[half:].astype(low)


def upper_terms(core, volume, cot):
    planes, rows, columns, channels = volume.shape
    depth, height, width, outs = cot.shape
    shape = (27, outs // 2, channels)
    return pl.pallas_call(
        upper_kernel,
        out_shape=(jax.ShapeDtypeStruct(shape, wide), jax.ShapeDtypeStruct(shape, low)),
        in_specs=[scalar, whole, whole],
        out_specs=(whole, whole),
        scratch_shapes=[
            pltpu.VMEM((channels // 128, planes * rows * columns, 128), wide),
            pltpu.VMEM((depth * height * width, 128), wide),
            pltpu.VMEM((3, rows, columns, depth, channels), low),
            pltpu.VMEM((outs, depth * height * width), low),
        ],
        compiler_params=params,
        cost_estimate=pl.CostEstimate(flops=5 * 10**8, bytes_accessed=6 * 10**6, transcendentals=0),
    )(core, volume, cot)


def partner(array, axis, by):
    size = lax.axis_size(axis)
    return lax.ppermute(array, axis, [(i, i ^ by) for i in range(size)])


def exchange(blocks, axis):
    return lax.all_to_all(blocks, axis, split_axis=0, concat_axis=0, tiled=True)


def filter_gradient(volume, cotangent, padding):
    return lax.conv_general_dilated(
        volume[None],
        cotangent[None],
        (1, 1, 1),
        padding,
        rhs_dilation=(2, 2, 2),
        dimension_numbers=("CDHWN", "IDHWO", "DHWNC"),
        preferred_element_type=jnp.float32,
    )


def input_gradient(cotangent, filters):
    return lax.conv_general_dilated(
        cotangent[None],
        filters[::-1, ::-1, ::-1],
        (1, 1, 1),
        ((1, 2), (1, 2), (1, 2)),
        lhs_dilation=(2, 2, 2),
        dimension_numbers=("NDHWC", "DHWOI", "NDHWC"),
        preferred_element_type=jnp.float32,
    )[0]


def plain_body(act_64, cot_32, filters_32, act_128):
    shards = lax.axis_size("chan")
    samples = lax.axis_size("sample")
    position = lax.axis_index("chan")
    core = lax.axis_index("sample") % 2
    volume_64 = act_64[0]
    cot_local = cot_32[0]
    depth, height, width, shard_out = cot_local.shape
    planes, rows, columns, middle = volume_64.shape
    below = act_128.shape[4]
    slab = planes // shards
    part = middle // shards

    rim = lax.ppermute(act_128[:, -1:], "chan", [(i, i + 1) for i in range(shards - 1)])

    taps = filters_32.reshape(27, shards, part, shard_out).transpose(1, 0, 3, 2)
    lanes = 128 if taps.size // shards % 256 == 0 else 64
    taps = taps.reshape(shards, 2, -1, lanes)
    own_half = lax.dynamic_index_in_dim(taps, core, 1, keepdims=False)
    cot_rows = jnp.broadcast_to(cot_local.reshape(1, -1, lanes), (shards, cot_local.size // lanes, lanes))
    sent = jnp.concatenate([own_half, cot_rows], axis=1)
    got = exchange(sent, "chan")
    cut = own_half.shape[1]
    got_half = got[:, :cut]
    other_half = partner(got_half, "sample", 1)
    first = jnp.where(core == 0, got_half, other_half)
    second = jnp.where(core == 0, other_half, got_half)
    part_filters = jnp.concatenate([first, second], axis=1)
    part_filters = part_filters.reshape(shards, 3, 3, 3, shard_out, part)
    part_filters = part_filters.transpose(1, 2, 3, 5, 0, 4).reshape(3, 3, 3, part, -1)
    cot_all = got[:, cut:].reshape(shards, depth, height, width, shard_out)
    cot_all = cot_all.transpose(1, 2, 3, 0, 4).reshape(depth, height, width, -1)

    grad_upper = filter_gradient(volume_64, cot_local, ((1, 0),) * 3)
    total_upper = lax.psum(grad_upper, "sample")

    grad_part = input_gradient(cot_all, part_filters)
    own_part = lax.dynamic_slice_in_dim(volume_64, position * part, part, 3)
    cot_part = (grad_part * jnp.where(own_part > 0, 1.0, leak_slope)).astype(low)
    cot_got = exchange(cot_part.reshape(shards, -1, 128), "chan")
    cot_low = cot_got.reshape(shards, slab, rows, columns, part)
    cot_low = cot_low.transpose(1, 2, 3, 0, 4).reshape(slab, rows, columns, middle)

    window = jnp.concatenate([rim, act_128], axis=1)[0]
    grad_lower = filter_gradient(window, cot_low, ((0, 0), (1, 0), (1, 0)))
    blocks = grad_lower.reshape(27, shards, 2, -1, middle).transpose(2, 1, 0, 3, 4)
    mine = lax.dynamic_index_in_dim(blocks, core, 0, keepdims=False)
    theirs = lax.dynamic_index_in_dim(blocks, 1 - core, 0, keepdims=False)
    mine = mine + partner(theirs.astype(low), "sample", 1).astype(jnp.float32)
    got_terms = exchange(mine.astype(low), "chan")
    share = jnp.sum(got_terms.astype(jnp.float32), axis=0)
    if samples > 2:
        pairs = [[2 * i + k for i in range(samples // 2)] for k in range(2)]
        share = lax.psum(share, "sample", axis_index_groups=pairs)
    share = lax.all_gather(
        share, "sample", axis=1, tiled=True, axis_index_groups=[[i, i + 1] for i in range(0, samples, 2)]
    )
    total_lower = share.reshape(3, 3, 3, below // shards, middle)
    return (
        total_upper / samples,
        total_lower / samples,
        cot_low.astype(jnp.float32)[None],
    )


def core_sum(mine, theirs):
    return (mine + partner(theirs, "sample", 1).astype(wide)).astype(low)


def sample_sum(mine, samples):
    core = lax.axis_index("sample") % 2
    total = mine.astype(wide)
    for by in range(2, samples, 2):
        pairs = [(i, (i + by) % samples) for i in range(samples)]
        total = total + lax.ppermute(mine, "sample", pairs).astype(wide)
    total = total * (1.0 / samples)
    other = partner(total, "sample", 1)
    first = jnp.where(core == 0, total, other)
    second = jnp.where(core == 0, other, total)
    return jnp.concatenate([first, second], axis=1)


def body(act_64, cot_32, filters_32, act_128):
    shards = lax.axis_size("chan")
    samples = lax.axis_size("sample")
    middle = act_64.shape[4]
    grid = cot_32.shape[1:4]
    shard_out = cot_32.shape[4]
    below = act_128.shape[4]
    if middle != 32 * shards or shards % 4 or samples != 4 or shard_out != 64 or (2 * grid[2]) != 8:
        return plain_body(act_64, cot_32, filters_32, act_128)
    core = lax.axis_index("sample") % 2
    cores = core[None].astype(jnp.int32)
    position = lax.axis_index("chan")[None].astype(jnp.int32)
    volume_64 = act_64[0]
    cot_local = cot_32[0]
    slab = volume_64.shape[0] // shards

    rim = lax.ppermute(act_128[:, -1:], "chan", [(i, i + 1) for i in range(shards - 1)])
    turned = filters_32.transpose(0, 1, 2, 4, 3).reshape(27, shard_out, middle)
    sent = pack(cores, turned, cot_local.reshape(-1, shard_out), shards)
    got = exchange(sent, "chan")

    own = own_signs(position, volume_64)
    other_act = partner(act_128, "sample", 1)
    halves = upper_terms(cores, volume_64, cot_local)
    window, done = windows(act_128[0])
    other_window, other_done = windows(other_act[0])
    done = done + other_done
    chip_upper = core_sum(*halves)
    beside = (got, own, rim, done, chip_upper)
    got, own, rim, done, chip_upper = lax.optimization_barrier(beside)
    weight = weights(got, shard_out // 2)
    other_weight = partner(weight, "sample", 1)
    first, later = first_terms(cores, got, weight, math.prod(grid))
    cot_sent = spread(first, later, other_weight, own, grid, shards)

    cot_sent, rim, chip_upper = lax.optimization_barrier((cot_sent, rim, chip_upper))
    cot_got = exchange(cot_sent, "chan")
    other_rim = partner(rim, "sample", 1)
    cot_got, other_rim = lax.optimization_barrier((cot_got, other_rim))
    total_upper = sample_sum(chip_upper, samples).reshape(3, 3, 3, shard_out, middle)
    total_upper = total_upper.transpose(0, 1, 2, 4, 3)

    other_cot = partner(cot_got, "sample", 1)
    slab_grid = (slab, *volume_64.shape[1:3])
    own_terms, below_other = lower_first(cores, cot_got, window, rim[0], other_rim[0], done, slab_grid)
    terms = lower_terms(cores, own_terms, other_cot, other_window, below_other, slab_grid)
    share = jnp.sum(exchange(terms, "chan").astype(wide), axis=0)
    cot_full = unpack(cot_got, slab_grid)
    shares = lax.all_gather(share.astype(low), "sample", axis=0)
    total_lower = total_terms(shares, 1.0 / samples).reshape(3, 3, 3, below // shards, middle)
    return (total_upper, total_lower, cot_full[None])


def solution(mesh):
    placed = (
        P("sample", None, None, None, None),
        P("sample", None, None, None, "chan"),
        P(None, None, None, None, "chan"),
        P("sample", "chan", None, None, None),
    )
    return jax.shard_map(
        body,
        mesh=mesh,
        in_specs=placed,
        out_specs=(
            P(None, None, None, None, "chan"),
            P(None, None, None, "chan", None),
            P("sample", "chan", None, None, None),
        ),
        check_vma=False,
    )
```

```python
import functools
import math

import jax
import jax.numpy as jnp
from jax import lax
from jax.experimental import pallas as pl
from jax.experimental.pallas import tpu as pltpu
from jax.sharding import PartitionSpec as P

leak_slope = 0.3
low = jnp.bfloat16
wide = jnp.float32
params = pltpu.CompilerParams(vmem_limit_bytes=20 * 2**20)
whole = pl.BlockSpec(memory_space=pltpu.VMEM)
scalar = pl.BlockSpec(memory_space=pltpu.SMEM)
anywhere = pl.BlockSpec(memory_space=pltpu.HBM)


def slot_plan():
    groups = []
    for col in range(3):
        groups.append([(1, 1, col), (1, 2, col), (2, 1, col), (2, 2, col)])
    for col in range(3):
        groups.append([(2, 0, col), (1, 0, col), (0, 1, col), (0, 2, col)])
    groups.append([None, (0, 0, 2), (0, 0, 1), (0, 0, 0)])
    return groups


def tap_index(tap):
    return (tap[0] * 3 + tap[1]) * 3 + tap[2]


def lane_slot(shape):
    return lax.broadcasted_iota(jnp.int32, shape, len(shape) - 1) // 32


def pack_kernel(core_ref, filters_ref, cot_ref, sent_ref, held, cot_held, staged, arrived, left):
    taps, half, _ = held.shape
    groups = slot_plan()
    start = pl.multiple_of(core_ref[0] * half, half)
    fetch_filters = pltpu.make_async_copy(filters_ref.at[:, pl.ds(start, half), :], held, arrived.at[0])
    fetch_cot = pltpu.make_async_copy(cot_ref, cot_held, arrived.at[1])
    fetch_cot.start()
    fetch_filters.start()
    slots = lane_slot((half, 128))
    shards = staged.shape[0]
    rows = len(groups) * half
    outs = cot_held.shape[1]
    cells = cot_held.shape[0]

    def send(index, first, count):
        part = pl.ds(first, count)
        return pltpu.make_async_copy(staged.at[:, part, :], sent_ref.at[:, part, :], left.at[index])

    fetch_cot.wait()
    turned_cot = cot_held[...].astype(wide).T.astype(low)
    for d in range(shards):
        for b in range(cells // 128):
            staged[d, pl.ds(rows + b * outs, outs), :] = turned_cot[:, b * 128 : (b + 1) * 128]
    copies = [send(0, rows, cells // 128 * outs)]
    copies[0].start()
    fetch_filters.wait()
    for g, group in enumerate(groups):
        for tile in range(shards // 4):
            turned = []
            for tap in group:
                if tap is None:
                    turned.append([jnp.zeros((half, 128), wide)] * 4)
                    continue
                block = held[tap_index(tap), :, pl.ds(tile * 128, 128)].astype(wide)
                turned.append([block] + [pltpu.roll(block, 32 * r, 1) for r in range(1, 4)])
            for m in range(4):
                joined = turned[0][(0 - m) % 4]
                for k in range(1, 4):
                    joined = jnp.where(slots == k, turned[k][(k - m) % 4], joined)
                staged[tile * 4 + m, pl.ds(g * half, half), :] = joined.astype(low)
        copies.append(send(g + 1, g * half, half))
        copies[-1].start()
    for copy in copies:
        copy.wait()


def pack(core, filters, cot, shards):
    taps, outs, middle = filters.shape
    groups = len(slot_plan())
    shape = (shards, groups * (outs // 2) + cot.shape[0] // 128 * outs, 128)
    return pl.pallas_call(
        pack_kernel,
        out_shape=pltpu.HBM(shape, low),
        in_specs=[scalar, anywhere, anywhere],
        out_specs=anywhere,
        scratch_shapes=[
            pltpu.VMEM((taps, outs // 2, middle), low),
            pltpu.VMEM(cot.shape, low),
            pltpu.VMEM(shape, low),
            pltpu.SemaphoreType.DMA((2,)),
            pltpu.SemaphoreType.DMA((groups + 1,)),
        ],
        compiler_params=params,
        cost_estimate=pl.CostEstimate(flops=10**6, bytes_accessed=3 * 10**6, transcendentals=0),
    )(core, pltpu.with_memory_space_constraint(filters, pltpu.HBM), pltpu.with_memory_space_constraint(cot, pltpu.HBM))


def sign_kernel(position_ref, volume_ref, own_ref):
    part = position_ref[0] % 4
    rows = own_ref.shape[0]
    slots = lane_slot((rows, 128))
    joined = None
    for depth_par in range(2):
        for row_par in range(2):
            slot = depth_par * 2 + row_par
            block = volume_ref[:, depth_par, :, row_par].astype(wide).reshape(rows, 128)
            block = pltpu.roll(block, (slot - part + 4) % 4 * 32, 1)
            joined = block if joined is None else jnp.where(slots == slot, block, joined)
    own_ref[...] = jnp.where(joined > 0, 1.0, leak_slope)


def own_signs(position, volume):
    planes, rows, columns, channels = volume.shape
    split = volume.reshape(planes // 2, 2, rows // 2, 2, columns, channels)
    count = planes * rows * columns // 4
    return pl.pallas_call(
        sign_kernel,
        out_shape=jax.ShapeDtypeStruct((count, 128), wide),
        grid_spec=pltpu.PrefetchScalarGridSpec(
            num_scalar_prefetch=1,
            grid=(1,),
            in_specs=[
                pl.BlockSpec(
                    (planes // 2, 2, rows // 2, 2, columns, 128),
                    lambda i, at: (0, 0, 0, 0, 0, at[0] // 4),
                )
            ],
            out_specs=pl.BlockSpec((count, 128), lambda i, at: (0, 0)),
        ),
        compiler_params=params,
        cost_estimate=pl.CostEstimate(flops=10**6, bytes_accessed=4 * 10**6, transcendentals=0),
    )(position, split)


def weight_kernel(got_ref, weight_ref):
    shards = got_ref.shape[0]
    groups = len(slot_plan())
    half = weight_ref.shape[0] // shards
    for c in range(shards):
        for g in range(groups):
            weight_ref[pl.ds(c * half, half), pl.ds(g * 128, 128)] = got_ref[c, pl.ds(g * half, half), :]


def weights(got, half):
    shards = got.shape[0]
    groups = len(slot_plan())
    return pl.pallas_call(
        weight_kernel,
        out_shape=jax.ShapeDtypeStruct((shards * half, groups * 128), low),
        grid=(1,),
        in_specs=[pl.BlockSpec((shards, groups * half, 128), lambda i: (0, 0, 0))],
        out_specs=whole,
        compiler_params=params,
        cost_estimate=pl.CostEstimate(flops=10**5, bytes_accessed=10**6, transcendentals=0),
    )(got)


def first_kernel(core_ref, got_ref, weight_ref, products_ref, later_ref, turned):
    shards = got_ref.shape[0]
    half = later_ref.shape[0] // shards
    groups = len(slot_plan())
    core = core_ref[0]
    for c in range(shards):
        span = pl.ds(c * half, half)
        for b in range(later_ref.shape[1] // 128):
            lanes = pl.ds(b * 128, 128)
            first = groups * half + b * 2 * half
            turned[span, lanes] = got_ref[c, pl.ds(pl.multiple_of(first + core * half, half), half), :]
            later_ref[span, lanes] = got_ref[c, pl.ds(pl.multiple_of(first + (1 - core) * half, half), half), :]
    products_ref[...] = lax.dot_general(
        turned[...], weight_ref[...], (((0,), (0,)), ((), ())), preferred_element_type=wide
    )


def spread_kernel(grid, first_ref, later_ref, other_ref, own_ref, sent_ref, products, joined):
    depth, height, width = grid
    cells = depth * height * width
    shards = sent_ref.shape[0]
    products[pl.ds(0, cells), :] = first_ref[...] + lax.dot_general(
        later_ref[...], other_ref[...], (((0,), (0,)), ((), ())), preferred_element_type=wide
    )
    products[pl.ds(cells, products.shape[0] - cells), :] = jnp.zeros(
        (products.shape[0] - cells, products.shape[1]), wide
    )
    chunk = cells // shards
    place = lax.broadcasted_iota(jnp.int32, (chunk, 128), 0)
    slots = lane_slot((chunk, 128))
    last_col = place % width == width - 1
    last_row = place // width % height == height - 1
    row_step, plane_step = width, width * height
    for n in range(shards):
        sums = [None, None]
        for col in range(3):

            def piece(group, offset):
                return products[pl.ds(n * chunk + offset, chunk), pl.ds(group * 128, 128)]

            part = piece(col, 0)
            part = part + jnp.where(slots >= 2, piece(3 + col, plane_step), 0.0)
            by_row = piece(3 + col, 0)
            moved = pltpu.roll(by_row, 96, 1)
            corner = piece(6, plane_step)
            if col > 0:
                corner = pltpu.roll(corner, 32 * col, 1)
            rows = jnp.where(slots == 1, by_row, jnp.where(slots == 3, moved + corner, 0.0))
            part = part + jnp.where(last_row, 0.0, pltpu.roll(rows, chunk - row_step, 0))
            if col == 0:
                part = jnp.where(last_col, 0.0, pltpu.roll(part, chunk - 1, 0))
            to = 0 if col == 1 else 1
            sums[to] = part if sums[to] is None else sums[to] + part
        joined[pl.ds(0, chunk, stride=2), :] = sums[0]
        joined[pl.ds(1, chunk, stride=2), :] = sums[1]
        span = pl.ds(n * 2 * chunk, 2 * chunk)
        slope = own_ref[span, :]
        sent_ref[n] = (joined[...] * slope).astype(low)


def first_terms(core, got, weight, cells):
    rows, lanes = weight.shape
    return pl.pallas_call(
        first_kernel,
        out_shape=(jax.ShapeDtypeStruct((cells, lanes), wide), jax.ShapeDtypeStruct((rows, cells), low)),
        in_specs=[scalar, whole, whole],
        out_specs=(whole, whole),
        scratch_shapes=[pltpu.VMEM((rows, cells), low)],
        compiler_params=params,
        cost_estimate=pl.CostEstimate(flops=10**8, bytes_accessed=3 * 10**6, transcendentals=0),
    )(core, got, weight)


def spread(first, later, other, own, grid, shards):
    cells, lanes = first.shape
    return pl.pallas_call(
        functools.partial(spread_kernel, grid),
        out_shape=jax.ShapeDtypeStruct((shards, 2 * cells // shards, 128), low),
        in_specs=[whole, whole, whole, whole],
        out_specs=whole,
        scratch_shapes=[
            pltpu.VMEM((cells + grid[1] * grid[2], lanes), wide),
            pltpu.VMEM((2 * cells // shards, 128), wide),
        ],
        compiler_params=params,
        cost_estimate=pl.CostEstimate(flops=5 * 10**8, bytes_accessed=3 * 10**6, transcendentals=0),
    )(first, later, other, own)


def unpack_kernel(got_ref, wide_ref):
    shards, rows, _ = got_ref.shape
    planes, height, columns, _ = wide_ref.shape
    slots = lane_slot((rows, 128))
    for tile in range(shards // 4):
        turned = []
        for m in range(4):
            block = got_ref[tile * 4 + m].astype(wide)
            turned.append([block] + [pltpu.roll(block, 32 * r, 1) for r in range(1, 4)])
        for slot in range(4):
            joined = turned[0][(0 - slot) % 4]
            for m in range(1, 4):
                joined = jnp.where(slots == m, turned[m][(m - slot) % 4], joined)
            joined = joined.reshape(planes // 2, height // 2, columns, 128)
            lanes = pl.ds(tile * 128, 128)
            for z in range(planes // 2):
                for y in range(height // 2):
                    at = (2 * z + slot // 2, 2 * y + slot % 2)
                    wide_ref[at[0], at[1], :, lanes] = joined[z, y]


def unpack(got, grid):
    shape = (*grid, got.shape[0] * 32)
    return pl.pallas_call(
        unpack_kernel,
        out_shape=jax.ShapeDtypeStruct(shape, wide),
        in_specs=[whole],
        out_specs=whole,
        compiler_params=params,
        cost_estimate=pl.CostEstimate(flops=10**6, bytes_accessed=2 * 10**6, transcendentals=0),
    )(got)


def tap_cells(flat, planes, rows, columns):
    channels = flat.shape[1]
    half = columns // 2
    count = planes * rows * half
    first = lax.broadcasted_iota(jnp.int32, (count, channels), 0) % half == 0
    even = flat[pl.ds(0, count, stride=2), :]
    odd = flat[pl.ds(1, count, stride=2), :]
    before = jnp.where(first, 0.0, pltpu.roll(odd, 1, 0))
    cells = []
    for part in (before, even, odd):
        part = part.reshape(planes, rows // 2, 2, half, channels)
        on_even, on_odd = part[:, :, 0], part[:, :, 1]
        ahead = jnp.concatenate([jnp.zeros_like(on_odd[:, :1]), on_odd[:, :-1]], axis=1)
        for taken in (ahead, on_even, on_odd):
            cells.append(taken.reshape(planes, rows // 2 * half, channels).astype(low))
    return cells


def window_kernel(volume_ref, window_ref, done_ref, flat):
    done_ref[...] = jnp.zeros_like(done_ref)
    planes, rows, columns, _ = volume_ref.shape
    flat[...] = volume_ref[...].astype(wide).reshape(flat.shape)
    for n, taken in enumerate(tap_cells(flat, planes, rows, columns)):
        for plane in range(planes):
            window_ref[n, plane % 2, plane // 2] = taken[plane]


def windows(volume):
    planes, rows, columns, channels = volume.shape
    shape = (9, 2, planes // 2, rows * columns // 4, channels)
    return pl.pallas_call(
        window_kernel,
        out_shape=(jax.ShapeDtypeStruct(shape, low), jax.ShapeDtypeStruct((8, 128), wide)),
        in_specs=[whole],
        out_specs=(whole, whole),
        scratch_shapes=[pltpu.VMEM((planes * rows * columns, channels), wide)],
        compiler_params=params,
        cost_estimate=pl.CostEstimate(flops=10**6, bytes_accessed=4 * 10**6, transcendentals=0),
    )(volume)


def lanes_joined(blocks, slot, slots):
    joined = blocks[0][(0 - slot) % 4]
    for m in range(1, 4):
        joined = jnp.where(slots == m, blocks[m][(m - slot) % 4], joined)
    return joined


def cotangent_side(source_ref, cells):
    shards, rows, _ = source_ref.shape
    planes, height, columns, middle = cells.shape
    slots = lane_slot((rows, 128))
    for tile in range(shards // 4):
        turned = []
        for m in range(4):
            block = source_ref[tile * 4 + m].astype(wide)
            turned.append([block] + [pltpu.roll(block, 32 * r, 1) for r in range(1, 4)])
        for slot in range(4):
            joined = lanes_joined(turned, slot, slots).reshape(planes // 2, height // 2, columns, 128)
            for z in range(planes // 2):
                for y in range(height // 2):
                    cells[2 * z + slot // 2, 2 * y + slot % 2, :, pl.ds(tile * 128, 128)] = joined[z, y]
    return cells[...].reshape(planes * height * columns, middle).astype(low).T


def rim_cells(rim_ref, flat, first_cells):
    _, rows, columns, _ = rim_ref.shape
    flat[...] = rim_ref[...].astype(wide).reshape(flat.shape)
    for n, taken in enumerate(tap_cells(flat, 1, rows, columns)):
        first_cells[n] = taken[0]


def tap_pair(window, first_cells, core, pair):
    planes = window.shape[2]
    both = []
    for n in (2 * pair, 2 * pair + 1):
        tap = core * 14 + n if n < 13 else 13
        depth, row, col = tap // 9, tap // 3 % 3, tap % 3
        which, parity = col * 3 + row, (depth + 1) % 2
        lowest = jnp.where(depth == 0, first_cells[which], window[which, parity, 0])
        below = jnp.where(depth == 0, 0, 1)
        rest = window[which, parity, pl.ds(below, planes - 1)]
        both.append(jnp.concatenate([lowest, rest.reshape(-1, window.shape[4])], axis=0))
    return jnp.concatenate(both, axis=1)


def lower_first_kernel(
    core_ref, got_ref, window, rim_ref, other_rim_ref, done_ref, total_ref, other_cells, cells, flat, first_cells
):
    del done_ref
    rim_cells(other_rim_ref, flat, other_cells)
    rim_cells(rim_ref, flat, first_cells)
    side = cotangent_side(got_ref, cells)
    for pair in range(total_ref.shape[0]):
        taps = tap_pair(window, first_cells, core_ref[0], pair)
        total_ref[pair] = jnp.dot(side, taps, preferred_element_type=wide)


def lower_scratch(grid, middle, window, rim):
    return [
        pltpu.VMEM((*grid, middle), wide),
        pltpu.VMEM((math.prod(rim.shape[:3]), rim.shape[3]), wide),
        pltpu.VMEM((9, *window.shape[3:]), low),
    ]


def lower_first(core, got, window, rim, other_rim, done, grid):
    middle = 32 * got.shape[0]
    return pl.pallas_call(
        lower_first_kernel,
        out_shape=(
            jax.ShapeDtypeStruct((7, middle, 2 * window.shape[4]), wide),
            jax.ShapeDtypeStruct((9, *window.shape[3:]), low),
        ),
        in_specs=[scalar, whole, whole, whole, whole, whole],
        out_specs=(whole, whole),
        scratch_shapes=lower_scratch(grid, middle, window, rim),
        compiler_params=params,
        cost_estimate=pl.CostEstimate(flops=5 * 10**8, bytes_accessed=5 * 10**6, transcendentals=0),
    )(core, got, window, rim, other_rim, done)


def lower_kernel(core_ref, total_ref, other_ref, window, first_cells, sent_ref, cells, staged, left):
    side = cotangent_side(other_ref, cells)
    shards = staged.shape[0]
    below = window.shape[4]
    share = below // shards
    copies = []
    for pair in range(total_ref.shape[0]):
        taps = tap_pair(window, first_cells, core_ref[0], pair)
        total = total_ref[pair] + jnp.dot(side, taps, preferred_element_type=wide)
        total = total.astype(low).T
        count = 0
        for n in (2 * pair, 2 * pair + 1):
            rows = total[n % 2 * below : (n % 2 + 1) * below]
            halves = [rows[:, :128], rows[:, 128:]]
            if n == 13:
                halves = [jnp.where(core_ref[0] == 0, *halves)]
            for half in halves:
                start = 2 * pair * 2 * share + count * share
                for d in range(shards):
                    staged[d, pl.ds(start, share), :] = half[d * share : (d + 1) * share]
                count += 1
        part = pl.ds(4 * pair * share, count * share)
        copies.append(pltpu.make_async_copy(staged.at[:, part, :], sent_ref.at[:, part, :], left.at[pair]))
        copies[-1].start()
    for copy in copies:
        copy.wait()


def lower_terms(core, total, other, window, first_cells, grid):
    shards = other.shape[0]
    pairs, middle, _ = total.shape
    shape = (shards, 27 * window.shape[4] // shards, 128)
    return pl.pallas_call(
        lower_kernel,
        out_shape=pltpu.HBM(shape, low),
        in_specs=[scalar, whole, whole, whole, whole],
        out_specs=anywhere,
        scratch_shapes=[
            pltpu.VMEM((*grid, middle), wide),
            pltpu.VMEM(shape, low),
            pltpu.SemaphoreType.DMA((pairs,)),
        ],
        compiler_params=params,
        cost_estimate=pl.CostEstimate(flops=5 * 10**8, bytes_accessed=5 * 10**6, transcendentals=0),
    )(core, total, other, window, first_cells)


def total_kernel(shares_ref, total_ref, *, scale):
    share = total_ref.shape[1]
    for core in range(2):
        total = shares_ref[core].astype(wide)
        for by in range(2, shares_ref.shape[0], 2):
            total = total + shares_ref[core + by].astype(wide)
        total = total * scale
        for n in range(13):
            for half in range(2):
                start = (2 * n + half) * share
                total_ref[core * 14 + n, :, pl.ds(half * 128, 128)] = total[start : start + share]
        total_ref[13, :, pl.ds(core * 128, 128)] = total[26 * share : 27 * share]


def total_terms(shares, scale):
    return pl.pallas_call(
        functools.partial(total_kernel, scale=scale),
        out_shape=jax.ShapeDtypeStruct((27, shares.shape[1] // 27, 2 * shares.shape[2]), wide),
        in_specs=[whole],
        out_specs=whole,
        compiler_params=params,
        cost_estimate=pl.CostEstimate(flops=10**6, bytes_accessed=10**6, transcendentals=0),
    )(shares)


def upper_kernel(core_ref, volume_ref, cot_ref, mine_ref, theirs_ref, flat, cot_flat, lined, left):
    planes, rows, columns, channels = volume_ref.shape
    depth, height, width, outs = cot_ref.shape
    half = outs // 2
    tiles = channels // 128
    for tile in range(tiles):
        lanes = pl.ds(tile * 128, 128)
        flat[tile] = volume_ref[:, :, :, lanes].astype(wide).reshape(flat.shape[1:])
    cot_wide = cot_ref[...].astype(wide).reshape(cot_flat.shape[0], outs)
    cot_flat[...] = jnp.concatenate([cot_wide, jnp.zeros((cot_flat.shape[0], 128 - outs), wide)], axis=1)
    pieces = [cot_flat[pl.ds(n, depth, stride=height * width), :] for n in range(height * width)]
    left[...] = jnp.concatenate(pieces, axis=0).T[:outs].astype(low)
    core = core_ref[0]
    split = [left[pl.ds(pl.multiple_of(at * half, half), half), :] for at in (core, 1 - core)]
    side = jnp.concatenate(split, axis=0)
    first = lax.broadcasted_iota(jnp.int32, (depth, 128), 0) == 0
    stride = 2 * rows * columns
    for row in range(rows):
        for col in range(columns):
            for tile in range(tiles):
                even = flat[tile, pl.ds(row * columns + col, depth, stride=stride), :]
                odd = flat[tile, pl.ds(stride // 2 + row * columns + col, depth, stride=stride), :]
                before = jnp.where(first, 0.0, pltpu.roll(odd, 1, 0))
                for depth_tap, part in enumerate((before, even, odd)):
                    lined[depth_tap, row, col, :, pl.ds(tile * 128, 128)] = part.astype(low)
    nothing = jnp.zeros((depth, channels), low)
    for tap in range(27):
        depth_tap, row_tap, col_tap = tap // 9, tap // 3 % 3, tap % 3
        taken = []
        for y in range(height):
            for x in range(width):
                row, col = 2 * y + row_tap - 1, 2 * x + col_tap - 1
                taken.append(nothing if row < 0 or col < 0 else lined[depth_tap, row, col])
        term = jnp.dot(side, jnp.concatenate(taken, axis=0), preferred_element_type=wide)
        mine_ref[tap] = term[:half]
        theirs_ref[tap] = term[half:].astype(low)


def upper_terms(core, volume, cot):
    planes, rows, columns, channels = volume.shape
    depth, height, width, outs = cot.shape
    shape = (27, outs // 2, channels)
    return pl.pallas_call(
        upper_kernel,
        out_shape=(jax.ShapeDtypeStruct(shape, wide), jax.ShapeDtypeStruct(shape, low)),
        in_specs=[scalar, whole, whole],
        out_specs=(whole, whole),
        scratch_shapes=[
            pltpu.VMEM((channels // 128, planes * rows * columns, 128), wide),
            pltpu.VMEM((depth * height * width, 128), wide),
            pltpu.VMEM((3, rows, columns, depth, channels), low),
            pltpu.VMEM((outs, depth * height * width), low),
        ],
        compiler_params=params,
        cost_estimate=pl.CostEstimate(flops=5 * 10**8, bytes_accessed=6 * 10**6, transcendentals=0),
    )(core, volume, cot)


def partner(array, axis, by):
    size = lax.axis_size(axis)
    return lax.ppermute(array, axis, [(i, i ^ by) for i in range(size)])


def exchange(blocks, axis):
    return lax.all_to_all(blocks, axis, split_axis=0, concat_axis=0, tiled=True)


def filter_gradient(volume, cotangent, padding):
    return lax.conv_general_dilated(
        volume[None],
        cotangent[None],
        (1, 1, 1),
        padding,
        rhs_dilation=(2, 2, 2),
        dimension_numbers=("CDHWN", "IDHWO", "DHWNC"),
        preferred_element_type=jnp.float32,
    )


def input_gradient(cotangent, filters):
    return lax.conv_general_dilated(
        cotangent[None],
        filters[::-1, ::-1, ::-1],
        (1, 1, 1),
        ((1, 2), (1, 2), (1, 2)),
        lhs_dilation=(2, 2, 2),
        dimension_numbers=("NDHWC", "DHWOI", "NDHWC"),
        preferred_element_type=jnp.float32,
    )[0]


def plain_body(act_64, cot_32, filters_32, act_128):
    shards = lax.axis_size("chan")
    samples = lax.axis_size("sample")
    position = lax.axis_index("chan")
    core = lax.axis_index("sample") % 2
    volume_64 = act_64[0]
    cot_local = cot_32[0]
    depth, height, width, shard_out = cot_local.shape
    planes, rows, columns, middle = volume_64.shape
    below = act_128.shape[4]
    slab = planes // shards
    part = middle // shards

    rim = lax.ppermute(act_128[:, -1:], "chan", [(i, i + 1) for i in range(shards - 1)])

    taps = filters_32.reshape(27, shards, part, shard_out).transpose(1, 0, 3, 2)
    lanes = 128 if taps.size // shards % 256 == 0 else 64
    taps = taps.reshape(shards, 2, -1, lanes)
    own_half = lax.dynamic_index_in_dim(taps, core, 1, keepdims=False)
    cot_rows = jnp.broadcast_to(cot_local.reshape(1, -1, lanes), (shards, cot_local.size // lanes, lanes))
    sent = jnp.concatenate([own_half, cot_rows], axis=1)
    got = exchange(sent, "chan")
    cut = own_half.shape[1]
    got_half = got[:, :cut]
    other_half = partner(got_half, "sample", 1)
    first = jnp.where(core == 0, got_half, other_half)
    second = jnp.where(core == 0, other_half, got_half)
    part_filters = jnp.concatenate([first, second], axis=1)
    part_filters = part_filters.reshape(shards, 3, 3, 3, shard_out, part)
    part_filters = part_filters.transpose(1, 2, 3, 5, 0, 4).reshape(3, 3, 3, part, -1)
    cot_all = got[:, cut:].reshape(shards, depth, height, width, shard_out)
    cot_all = cot_all.transpose(1, 2, 3, 0, 4).reshape(depth, height, width, -1)

    grad_upper = filter_gradient(volume_64, cot_local, ((1, 0),) * 3)
    total_upper = lax.psum(grad_upper, "sample")

    grad_part = input_gradient(cot_all, part_filters)
    own_part = lax.dynamic_slice_in_dim(volume_64, position * part, part, 3)
    cot_part = (grad_part * jnp.where(own_part > 0, 1.0, leak_slope)).astype(low)
    cot_got = exchange(cot_part.reshape(shards, -1, 128), "chan")
    cot_low = cot_got.reshape(shards, slab, rows, columns, part)
    cot_low = cot_low.transpose(1, 2, 3, 0, 4).reshape(slab, rows, columns, middle)

    window = jnp.concatenate([rim, act_128], axis=1)[0]
    grad_lower = filter_gradient(window, cot_low, ((0, 0), (1, 0), (1, 0)))
    blocks = grad_lower.reshape(27, shards, 2, -1, middle).transpose(2, 1, 0, 3, 4)
    mine = lax.dynamic_index_in_dim(blocks, core, 0, keepdims=False)
    theirs = lax.dynamic_index_in_dim(blocks, 1 - core, 0, keepdims=False)
    mine = mine + partner(theirs.astype(low), "sample", 1).astype(jnp.float32)
    got_terms = exchange(mine.astype(low), "chan")
    share = jnp.sum(got_terms.astype(jnp.float32), axis=0)
    if samples > 2:
        pairs = [[2 * i + k for i in range(samples // 2)] for k in range(2)]
        share = lax.psum(share, "sample", axis_index_groups=pairs)
    share = lax.all_gather(
        share, "sample", axis=1, tiled=True, axis_index_groups=[[i, i + 1] for i in range(0, samples, 2)]
    )
    total_lower = share.reshape(3, 3, 3, below // shards, middle)
    return (
        total_upper / samples,
        total_lower / samples,
        cot_low.astype(jnp.float32)[None],
    )


def core_sum(mine, theirs):
    return (mine + partner(theirs, "sample", 1).astype(wide)).astype(low)


def sample_sum(mine, samples):
    core = lax.axis_index("sample") % 2
    total = mine.astype(wide)
    for by in range(2, samples, 2):
        pairs = [(i, (i + by) % samples) for i in range(samples)]
        total = total + lax.ppermute(mine, "sample", pairs).astype(wide)
    total = total * (1.0 / samples)
    other = partner(total, "sample", 1)
    first = jnp.where(core == 0, total, other)
    second = jnp.where(core == 0, other, total)
    return jnp.concatenate([first, second], axis=1)


def body(act_64, cot_32, filters_32, act_128):
    shards = lax.axis_size("chan")
    samples = lax.axis_size("sample")
    middle = act_64.shape[4]
    grid = cot_32.shape[1:4]
    shard_out = cot_32.shape[4]
    below = act_128.shape[4]
    if middle != 32 * shards or shards % 4 or samples != 4 or shard_out != 64 or (2 * grid[2]) != 8:
        return plain_body(act_64, cot_32, filters_32, act_128)
    core = lax.axis_index("sample") % 2
    cores = core[None].astype(jnp.int32)
    position = lax.axis_index("chan")[None].astype(jnp.int32)
    volume_64 = act_64[0]
    cot_local = cot_32[0]
    slab = volume_64.shape[0] // shards

    rim = lax.ppermute(act_128[:, -1:], "chan", [(i, i + 1) for i in range(shards - 1)])
    turned = filters_32.transpose(0, 1, 2, 4, 3).reshape(27, shard_out, middle)
    sent = pack(cores, turned, cot_local.reshape(-1, shard_out), shards)
    got = exchange(sent, "chan")

    own = own_signs(position, volume_64)
    other_act = partner(act_128, "sample", 1)
    halves = upper_terms(cores, volume_64, cot_local)
    window, done = windows(act_128[0])
    other_window, other_done = windows(other_act[0])
    done = done + other_done
    chip_upper = core_sum(*halves)
    beside = (got, own, rim, done, chip_upper)
    got, own, rim, done, chip_upper = lax.optimization_barrier(beside)
    weight = weights(got, shard_out // 2)
    other_weight = partner(weight, "sample", 1)
    first, later = first_terms(cores, got, weight, math.prod(grid))
    cot_sent = spread(first, later, other_weight, own, grid, shards)

    cot_sent, rim, chip_upper = lax.optimization_barrier((cot_sent, rim, chip_upper))
    cot_got = exchange(cot_sent, "chan")
    other_rim = partner(rim, "sample", 1)
    cot_got, other_rim = lax.optimization_barrier((cot_got, other_rim))
    total_upper = sample_sum(chip_upper, samples).reshape(3, 3, 3, shard_out, middle)
    total_upper = total_upper.transpose(0, 1, 2, 4, 3)

    other_cot = partner(cot_got, "sample", 1)
    slab_grid = (slab, *volume_64.shape[1:3])
    own_terms, below_other = lower_first(cores, cot_got, window, rim[0], other_rim[0], done, slab_grid)
    terms = lower_terms(cores, own_terms, other_cot, other_window, below_other, slab_grid)
    share = jnp.sum(exchange(terms, "chan").astype(wide), axis=0)
    cot_full = unpack(cot_got, slab_grid)
    shares = lax.all_gather(share.astype(low), "sample", axis=0)
    total_lower = total_terms(shares, 1.0 / samples).reshape(3, 3, 3, below // shards, middle)
    return (total_upper, total_lower, cot_full[None])


def solution(mesh):
    placed = (
        P("sample", None, None, None, None),
        P("sample", None, None, None, "chan"),
        P(None, None, None, None, "chan"),
        P("sample", "chan", None, None, None),
    )
    return jax.shard_map(
        body,
        mesh=mesh,
        in_specs=placed,
        out_specs=(
            P(None, None, None, None, "chan"),
            P(None, None, None, "chan", None),
            P("sample", "chan", None, None, None),
        ),
        check_vma=False,
    )
```
